256 devices in a mesh: dp: 16 (over x, y), feat: 16 (over z, core).
Axes of the slice: x: 4, y: 4, z: 8, core: 2. Of those that a mesh axis runs over, the one named last changes fastest.
Arguments:
- x_table: bfloat16 [1024, 131072], P('feat', 'dp'), may hold values from -6 to 6
- hub_feats: bfloat16 [1024, 2048], P('feat'), may hold values from -6 to 6
- send_rows: int32 [16, 16, 2048], P('dp'), may hold values from 0 to 8191
- self_slot: int32 [65536], P('dp'), may hold values from 0 to 34815
- nbr1: int32 [10, 65536], P(None, 'dp'), may hold values from 0 to 34815
- cnt1: int32 [65536], P('dp'), may hold values from 1 to 10
- h_saved: bfloat16 [65536, 512], P(('dp', 'feat')), as said below
- seed_self: int32 [65536], P(('dp', 'feat')), may hold values from 0 to 4095
- nbr2: int32 [65536, 25], P(('dp', 'feat')), may hold values from 0 to 4095
- cnt2: int32 [65536], P(('dp', 'feat')), may hold values from 1 to 25
- d_logits: bfloat16 [65536, 172], P(('dp', 'feat')), may hold values from -0.0234375 to 0.0234375
- w_self2: bfloat16 [512, 172], replicated, may hold values from -0.25 to 0.25
- w_nbr2: bfloat16 [512, 172], replicated, may hold values from -0.25 to 0.25
Outputs:
- grad_self1: float32 [1024, 512], P('feat')
- grad_nbr1: float32 [1024, 512], P('feat')
- grad_self2: float32 [512, 172], replicated
- grad_nbr2: float32 [512, 172], replicated
The draws below stay inside these ranges and needn't reach their ends.
Inputs may be any that keep to these rules, and one draw needn't show every extreme that they name: Entries nbr1[j, u] with j at or past cnt1[u] are padding and are not read. `nbr2`: entries of a row at positions at or past its count are padding and are not read. Every entry of h_saved is zero or positive.
All inputs are finite; a program needn't handle non-finite values.
Results may differ from the reference program's by a relative error of at most 0.0039.
Values may be sent and summed in bfloat16 or wider, within the bound.
A program may use at most 128 MiB of HBM per device.

```python
import jax
import jax.numpy as jnp
from jax import lax

F = 1024
H = 512
C = 172
K1 = 10
K2 = 25
SEED_DEV = 256
R1_DEV = 256
NODE_DEV = 8192
CAP = 2048
HUBS = 2048
NODES = 131072
HOP_ROWS = 65536
GROUP_ROWS = 4096
SEEDS = 65536
SLOTS = 34816
N_DP = 16
N_FEAT = 16


def draw_h_saved(key, part):
    key = jax.random.fold_in(key, 7)
    values = jax.random.normal(jax.random.fold_in(key, 1), (HOP_ROWS, H), jnp.float32)
    return jnp.maximum(values, 0.0).astype(jnp.bfloat16)


def place_ends(drawn, own_key, smallest, top_value):
    longest = drawn.shape.index(max(drawn.shape))
    spots = []
    for shift in (0, 1):
        where = [jax.random.randint(jax.random.fold_in(own_key, axis), (), 0, length) for axis, length in enumerate(drawn.shape)]
        where[longest] = (where[longest] + shift) % drawn.shape[longest]
        spots.append(tuple(where))
    return drawn.at[spots[0]].set(smallest).at[spots[1]].set(top_value)


def block_levels(key, shape, split, least, top_value):
    def one(axis_at, parts):
        draws = jax.random.uniform(jax.random.fold_in(jax.random.fold_in(key, 6), axis_at), (parts,), jnp.float32, least / len(split), top_value / len(split))
        return jnp.repeat(jnp.exp(draws), shape[axis_at] // parts).reshape((-1,) + (1,) * (len(shape) - axis_at - 1))

    loudness = one(*split[0])
    for cut in split[1:]:
        loudness = loudness * one(*cut)
    return loudness


def gaussian(rng, dims, width, reach, cuts=(), held_as=jnp.bfloat16):
    entries = jax.random.normal(rng, dims, jnp.float32) * width
    if len(cuts) > 0:
        entries = block_levels(rng, dims, cuts, -0.22, 0.18) * entries
    return jnp.clip(entries, min=-reach, max=reach).astype(held_as)


def setup_inputs(seed: int = 0) -> dict:
    keys = jax.random.split(jax.random.key(seed), 14)
    return {
        "x_table": gaussian(keys[0], (F, NODES), 1.0, 6.0, ((0, 16), (1, 16))),
        "hub_feats": gaussian(keys[1], (F, HUBS), 1.0, 6.0, ((0, 16),)),
        "send_rows": place_ends(jax.random.randint(keys[2], (N_DP, N_DP, CAP), 0, NODE_DEV), jax.random.fold_in(keys[2], 1), 0, NODE_DEV - 1).astype(jnp.int32),
        "self_slot": place_ends(jax.random.randint(keys[3], (HOP_ROWS,), 0, SLOTS), jax.random.fold_in(keys[3], 1), 0, SLOTS - 1).astype(jnp.int32),
        "nbr1": place_ends(jax.random.randint(keys[4], (K1, HOP_ROWS), 0, SLOTS), jax.random.fold_in(keys[4], 1), 0, SLOTS - 1).astype(jnp.int32),
        "cnt1": place_ends(jax.random.randint(keys[5], (HOP_ROWS,), 1, K1 + 1), jax.random.fold_in(keys[5], 1), 1, K1).astype(jnp.int32),
        "h_saved": draw_h_saved(jax.random.fold_in(keys[13], 71), 0),
        "seed_self": place_ends(jax.random.randint(keys[7], (SEEDS,), 0, GROUP_ROWS), jax.random.fold_in(keys[7], 1), 0, GROUP_ROWS - 1).astype(jnp.int32),
        "nbr2": place_ends(jax.random.randint(keys[8], (SEEDS, K2), 0, GROUP_ROWS), jax.random.fold_in(keys[8], 1), 0, GROUP_ROWS - 1).astype(jnp.int32),
        "cnt2": place_ends(jax.random.randint(keys[9], (SEEDS,), 1, K2 + 1), jax.random.fold_in(keys[9], 1), 1, K2).astype(jnp.int32),
        "d_logits": gaussian(keys[10], (SEEDS, C), (SEEDS ** -0.5), 0.0234375, ((0, 256),)),
        "w_self2": gaussian(keys[11], (H, C), H ** -0.5, 0.25),
        "w_nbr2": gaussian(keys[12], (H, C), H ** -0.5, 0.25),
    }


def reference(x_table, hub_feats, send_rows, self_slot, nbr1, cnt1, h_saved, seed_self, nbr2, cnt2, d_logits, w_self2, w_nbr2):
    group_rows = R1_DEV * N_FEAT
    group_seeds = SEED_DEV * N_FEAT
    owners = x_table.T.reshape(N_DP, NODE_DEV, F)
    hub_rows = hub_feats.T
    requests = jnp.transpose(send_rows, (1, 0, 2))
    highest = lax.Precision.HIGHEST
    w_nbr_f = w_nbr2.astype(jnp.float32)
    w_self_f = w_self2.astype(jnp.float32)

    def one_group(carry, inputs):
        picks, slots, neigh_one, count_one, hidden, seeds_own, neigh_two, count_two, grad_out = inputs
        fetched = jax.vmap(lambda table_part, row_ids: jnp.take(table_part, row_ids, axis=0))(owners, picks)
        lookup = jnp.concatenate([fetched.reshape(N_DP * CAP, F), hub_rows], axis=0)
        self_feats = jnp.take(lookup, slots, axis=0)
        total = jnp.zeros((group_rows, F), jnp.float32)
        for column in range(K1):
            rows_here = jnp.take(lookup, neigh_one[:, column], axis=0).astype(jnp.float32)
            total = total + jnp.where((column < count_one)[:, None], rows_here, jnp.float32(0.0))
        nbr_mean = (total / count_one[:, None].astype(jnp.float32)).astype(jnp.bfloat16)
        dz_mean = (grad_out.astype(jnp.float32) / count_two[:, None].astype(jnp.float32)).astype(jnp.bfloat16)
        dz_mean = lax.optimization_barrier(dz_mean).astype(jnp.float32)
        grad_nbr = jnp.zeros((group_rows, C), jnp.float32)
        for column in range(K2):
            valued = jnp.where((column < count_two)[:, None], dz_mean, jnp.float32(0.0))
            grad_nbr = grad_nbr.at[neigh_two[:, column]].add(valued)
        grad_self = jnp.zeros((group_rows, C), jnp.float32).at[seeds_own].add(grad_out.astype(jnp.float32))
        h_float = hidden.astype(jnp.float32)
        d_hidden = jnp.dot(grad_nbr, w_nbr_f.T, precision=highest) + jnp.dot(grad_self, w_self_f.T, precision=highest)
        d_pre = jnp.where(hidden > 0, d_hidden, jnp.float32(0.0)).astype(jnp.bfloat16)
        acc_self1 = carry[0] + jnp.dot(self_feats.T, d_pre, preferred_element_type=jnp.float32)
        acc_nbr1 = carry[1] + jnp.dot(nbr_mean.T, d_pre, preferred_element_type=jnp.float32)
        acc_self2 = carry[2] + jnp.dot(h_float.T, grad_self, precision=highest)
        acc_nbr2 = carry[3] + jnp.dot(h_float.T, grad_nbr, precision=highest)
        return (acc_self1, acc_nbr1, acc_self2, acc_nbr2), None

    inputs = (
        requests,
        self_slot.reshape(N_DP, group_rows),
        nbr1.T.reshape(N_DP, group_rows, K1),
        cnt1.reshape(N_DP, group_rows),
        h_saved.reshape(N_DP, group_rows, H),
        seed_self.reshape(N_DP, group_seeds),
        nbr2.reshape(N_DP, group_seeds, K2),
        cnt2.reshape(N_DP, group_seeds),
        d_logits.reshape(N_DP, group_seeds, C),
    )
    start = (jnp.zeros((F, H), jnp.float32), jnp.zeros((F, H), jnp.float32), jnp.zeros((H, C), jnp.float32), jnp.zeros((H, C), jnp.float32))
    result, unused = lax.scan(one_group, start, inputs)
    return result[0], result[1], result[2], result[3]
```

```python
import jax
import jax.numpy as jnp
from jax import lax
from jax.experimental import pallas as pl
from jax.experimental.pallas import tpu as pltpu
from jax.sharding import PartitionSpec as P

N_DP = 16
N_FEAT = 16
CAP = 2048
HALF = CAP // 2
HUBS = 2048
ROWS = 256
FAN1 = 10
FAN2 = 25
PICKS = 1 + FAN1
WIDE = 128
ZERO_ROW = N_DP * CAP + HUBS
MESH = pl.DeviceIdType.MESH
VMEM_LIMIT = 60 * 1024 * 1024


def vmem():
    return pl.BlockSpec(memory_space=pltpu.VMEM)


def smem():
    return pl.BlockSpec(memory_space=pltpu.SMEM)


def pick_kernel(idx_ref, table_ref, out_ref, rows_ref):
    step = 32

    def one_group(group, carry):
        def some_rows(block, inner):
            at = block * step
            first = group * HALF + at
            got = [table_ref[pl.ds(idx_ref[first + r], 1), :] for r in range(step)]
            for r in range(step):
                rows_ref[pl.ds(at + r, 1), :] = got[r]
            return inner

        lax.fori_loop(0, HALF // step, some_rows, 0)
        out_ref[group] = rows_ref[...].astype(jnp.bfloat16)
        return carry

    lax.fori_loop(0, N_DP, one_group, 0)


def pick(idx, table):
    return pl.pallas_call(
        pick_kernel,
        out_shape=jax.ShapeDtypeStruct((N_DP, HALF, WIDE), jnp.bfloat16),
        in_specs=[smem(), vmem()],
        out_specs=vmem(),
        scratch_shapes=[pltpu.VMEM((HALF, WIDE), jnp.float32)],
        compiler_params=pltpu.CompilerParams(vmem_limit_bytes=VMEM_LIMIT),
        name="pick",
    )(idx, table)


def fold_kernel(idx_ref, own_ref, other_ref, hub_ref, count_ref, out_ref, table_ref, self_ref, sum_ref):
    part = N_DP * HALF
    chunk = 1024

    def fill(block, carry):
        at = pl.multiple_of(block * chunk, chunk)
        table_ref[pl.ds(at, chunk), :] = own_ref[pl.ds(at, chunk), :].astype(jnp.float32)
        table_ref[pl.ds(part + at, chunk), :] = other_ref[pl.ds(at, chunk), :].astype(jnp.float32)
        return carry

    lax.fori_loop(0, part // chunk, fill, 0)
    table_ref[pl.ds(2 * part, HUBS), :] = hub_ref[...].astype(jnp.float32)
    table_ref[pl.ds(ZERO_ROW, 8), :] = jnp.zeros((8, WIDE), jnp.float32)
    step = 8

    def some_rows(block, carry):
        at = block * step
        for r in range(step):
            first = (at + r) * PICKS
            got = [table_ref[pl.ds(idx_ref[first + j], 1), :] for j in range(PICKS)]
            own = got[0]
            rest = got[1:]
            while len(rest) > 1:
                rest = [rest[k] + rest[k + 1] if k + 1 < len(rest) else rest[k] for k in range(0, len(rest), 2)]
            self_ref[pl.ds(at + r, 1), :] = own
            sum_ref[pl.ds(at + r, 1), :] = rest[0]
        return carry

    lax.fori_loop(0, 8 * ROWS // step, some_rows, 0)
    out_ref[:, :WIDE] = self_ref[...].astype(jnp.bfloat16)
    out_ref[:, WIDE:] = (sum_ref[...] / count_ref[...]).astype(jnp.bfloat16)


def fold(idx, own, other, hub, count):
    rows = 8 * ROWS
    return pl.pallas_call(
        fold_kernel,
        out_shape=jax.ShapeDtypeStruct((rows, 2 * WIDE), jnp.bfloat16),
        in_specs=[smem(), vmem(), vmem(), vmem(), vmem()],
        out_specs=vmem(),
        scratch_shapes=[
            pltpu.VMEM((ZERO_ROW + 8, WIDE), jnp.float32),
            pltpu.VMEM((rows, WIDE), jnp.float32),
            pltpu.VMEM((rows, WIDE), jnp.float32),
        ],
        compiler_params=pltpu.CompilerParams(vmem_limit_bytes=VMEM_LIMIT),
        name="fold",
    )(idx, own, other, hub, count)


def seeds_kernel(rel_ref, dl_ref, dz_ref, h_ref, ws_ref, wn_ref, dpre_ref, second_ref, tally_ref, hot_ref):
    seeds = rel_ref.shape[1]
    row_id = lax.broadcasted_iota(jnp.int32, (ROWS, 128), 0).astype(jnp.float32).astype(jnp.bfloat16)
    one = jnp.ones((ROWS, 128), jnp.bfloat16)
    none = jnp.zeros((ROWS, 128), jnp.bfloat16)

    def count(block, carry):
        cols = pl.ds(pl.multiple_of(block * 128, 128), 128)
        total = none
        for j in range(FAN2):
            line = jnp.broadcast_to(rel_ref[pl.ds(j, 1), cols].astype(jnp.bfloat16), (ROWS, 128))
            total = total + jnp.where(line == row_id, one, none)
        tally_ref[:, cols] = total
        line = jnp.broadcast_to(rel_ref[pl.ds(FAN2, 1), cols].astype(jnp.bfloat16), (ROWS, 128))
        hot_ref[:, cols] = jnp.where(line == row_id, one, none)
        return carry

    lax.fori_loop(0, seeds // 128, count, 0)
    chunk = 1024
    classes = dl_ref.shape[1]

    def gather(block, carry):
        at = pl.ds(pl.multiple_of(block * chunk, chunk), chunk)
        nbr = carry[0] + jnp.dot(tally_ref[:, at], dz_ref[at, :], preferred_element_type=jnp.float32)
        own = carry[1] + jnp.dot(hot_ref[:, at], dl_ref[at, :], preferred_element_type=jnp.float32)
        return nbr, own

    zero = jnp.zeros((ROWS, classes), jnp.float32)
    nbr, own = lax.fori_loop(0, seeds // chunk, gather, (zero, zero))
    highest = lax.Precision.HIGHEST
    last = (((1,), (1,)), ((), ()))
    h = h_ref[...].astype(jnp.float32)
    hidden = lax.dot_general(nbr, wn_ref[...].astype(jnp.float32), last, precision=highest, preferred_element_type=jnp.float32)
    hidden = hidden + lax.dot_general(own, ws_ref[...].astype(jnp.float32), last, precision=highest, preferred_element_type=jnp.float32)
    dpre_ref[...] = jnp.where(h > 0, hidden, 0.0).astype(jnp.bfloat16)
    ht = h.T
    second_ref[0] = jnp.dot(ht, own, precision=highest, preferred_element_type=jnp.float32)
    second_ref[1] = jnp.dot(ht, nbr, precision=highest, preferred_element_type=jnp.float32)


def seeds_step(rel, dl, dz, h, ws, wn):
    seeds = rel.shape[1]
    return pl.pallas_call(
        seeds_kernel,
        out_shape=(
            jax.ShapeDtypeStruct(h.shape, jnp.bfloat16),
            jax.ShapeDtypeStruct((2, h.shape[1], dl.shape[1]), jnp.float32),
        ),
        in_specs=[vmem()] * 6,
        out_specs=(vmem(), vmem()),
        scratch_shapes=[pltpu.VMEM((ROWS, seeds), jnp.bfloat16), pltpu.VMEM((ROWS, seeds), jnp.bfloat16)],
        compiler_params=pltpu.CompilerParams(vmem_limit_bytes=VMEM_LIMIT),
        name="seeds",
    )(rel, dl, dz, h, ws, wn)


def greet(peers):
    barrier = pltpu.get_barrier_semaphore()
    for peer in peers:
        pl.semaphore_signal(barrier, inc=1, device_id=peer, device_id_type=MESH)
    pl.semaphore_wait(barrier, len(peers))


def first_kernel(part_ref, out_ref, got_ref, done_ref, send_sem, recv_sem, send2_sem, recv2_sem):
    dp = lax.axis_index("dp")
    feat = lax.axis_index("feat")
    core = lax.rem(feat, 2)
    peers = []
    for flip in range(2):
        to_core = (1 - core) if flip else core
        to_feat = feat - core + to_core
        for shift in range(N_DP):
            if flip == 0 and shift == 0:
                continue
            to_dp = lax.rem(dp + shift, N_DP)
            peers.append((flip * N_DP + shift, to_dp, to_feat, to_core))
    greet([(d, f) for _, d, f, _ in peers])
    copies = []
    for slot, to_dp, to_feat, to_core in peers:
        copy = pltpu.make_async_remote_copy(
            src_ref=part_ref.at[to_core, pl.ds(pl.multiple_of(to_dp * 8, 8), 8), :],
            dst_ref=got_ref.at[slot],
            send_sem=send_sem.at[slot],
            recv_sem=recv_sem.at[slot],
            device_id=(to_dp, to_feat),
            device_id_type=MESH,
        )
        copy.start()
        copies.append(copy)
    mine = pl.ds(pl.multiple_of(dp * 8, 8), 8)
    total = part_ref[core, mine, :]
    for (slot, _, _, _), copy in zip(peers, copies):
        copy.wait_recv()
        total = total + got_ref[slot]
    done_ref[mine, :] = total
    spread = []
    for slot, to_dp, to_feat, _ in peers:
        if slot >= N_DP:
            continue
        copy = pltpu.make_async_remote_copy(
            src_ref=done_ref.at[mine, :],
            dst_ref=done_ref.at[mine, :],
            send_sem=send2_sem.at[slot],
            recv_sem=recv2_sem.at[slot],
            device_id=(to_dp, to_feat),
            device_id_type=MESH,
        )
        copy.start()
        spread.append(copy)
    for copy in copies:
        copy.wait_send()
    for copy in spread:
        copy.wait()
    out_ref[...] = done_ref[...]


def first_sum(part):
    width = part.shape[2]
    return pl.pallas_call(
        first_kernel,
        out_shape=jax.ShapeDtypeStruct((WIDE, width), jnp.float32),
        in_specs=[vmem()],
        out_specs=vmem(),
        scratch_shapes=[
            pltpu.VMEM((2 * N_DP, 8, width), jnp.float32),
            pltpu.VMEM((WIDE, width), jnp.float32),
            pltpu.SemaphoreType.DMA((2 * N_DP,)),
            pltpu.SemaphoreType.DMA((2 * N_DP,)),
            pltpu.SemaphoreType.DMA((N_DP,)),
            pltpu.SemaphoreType.DMA((N_DP,)),
        ],
        compiler_params=pltpu.CompilerParams(collective_id=1, has_side_effects=True, vmem_limit_bytes=VMEM_LIMIT),
        name="first_sum",
    )(part)


def second_kernel(part_ref, out_ref, got_ref, mid_ref, got2_ref, sems):
    dp = lax.axis_index("dp")
    feat = lax.axis_index("feat")
    along_feat = [(k, lax.rem(feat + k, N_FEAT)) for k in range(1, N_FEAT)]
    along_dp = [(k, lax.rem(dp + k, N_DP)) for k in range(1, N_DP)]
    greet([(dp, f) for _, f in along_feat] + [(d, feat) for _, d in along_dp])
    copies = []

    def push(src, dst, stage, slot, device):
        copy = pltpu.make_async_remote_copy(
            src_ref=src,
            dst_ref=dst,
            send_sem=sems.at[2 * stage, slot],
            recv_sem=sems.at[2 * stage + 1, slot],
            device_id=device,
            device_id_type=MESH,
        )
        copy.start()
        copies.append(copy)
        return copy

    scattered = [push(part_ref.at[f], got_ref.at[k], 0, k, (dp, f)) for k, f in along_feat]
    total = part_ref[feat]
    for (k, _), copy in zip(along_feat, scattered):
        copy.wait_recv()
        total = total + got_ref[k]
    mid_ref[...] = total
    summed = [push(mid_ref, got2_ref.at[k], 1, k, (d, feat)) for k, d in along_dp]
    for (k, _), copy in zip(along_dp, summed):
        copy.wait_recv()
        total = total + got2_ref[k]
    out_ref[feat] = total
    gathered = [push(out_ref.at[feat], out_ref.at[feat], 2, k, (dp, f)) for k, f in along_feat]
    for copy in gathered:
        copy.wait_recv()
    for copy in copies:
        copy.wait_send()


def second_sum(part):
    piece = part.shape[1:]
    return pl.pallas_call(
        second_kernel,
        out_shape=jax.ShapeDtypeStruct(part.shape, jnp.float32),
        in_specs=[vmem()],
        out_specs=vmem(),
        scratch_shapes=[
            pltpu.VMEM((N_FEAT,) + piece, jnp.float32),
            pltpu.VMEM(piece, jnp.float32),
            pltpu.VMEM((N_DP,) + piece, jnp.float32),
            pltpu.SemaphoreType.DMA((6, 16)),
        ],
        compiler_params=pltpu.CompilerParams(collective_id=2, has_side_effects=True, vmem_limit_bytes=VMEM_LIMIT),
        name="second_sum",
    )(part)


def body(
    x_table,
    hub_feats,
    send_rows,
    self_slot,
    nbr1,
    cnt1,
    h_saved,
    seed_self,
    nbr2,
    cnt2,
    d_logits,
    w_self2,
    w_nbr2,
):
    feat = lax.axis_index("feat")
    core = lax.rem(feat, 2)
    swap = [(i, i ^ 1) for i in range(N_FEAT)]

    mine = jnp.concatenate([x_table, hub_feats], axis=1)
    theirs = lax.ppermute(mine, "feat", swap)
    both = jnp.where(core == 0, jnp.concatenate([mine, theirs], axis=0), jnp.concatenate([theirs, mine], axis=0))
    nodes = x_table.shape[1]
    table = both[:, :nodes].T.astype(jnp.float32)
    hub = both[:, nodes:].T
    wanted = lax.dynamic_slice_in_dim(send_rows[0], core * HALF, HALF, axis=1).reshape(-1)
    outgoing = pick(wanted, table)
    own = lax.all_to_all(outgoing, "dp", split_axis=0, concat_axis=0, tiled=True)
    other = lax.ppermute(own, "feat", swap)

    kept = lax.iota(jnp.int32, FAN2)[:, None] < cnt2[None, :]
    ints = jnp.concatenate(
        [jnp.where(kept, nbr2.T, -1), seed_self[None], cnt2[None], jnp.zeros((32 - FAN2 - 2, ROWS), jnp.int32)], axis=0
    )
    ints = lax.all_gather(ints, "feat", axis=1, tiled=True)
    dl = lax.all_gather(d_logits, "feat", axis=0, tiled=True)
    dz = (dl.astype(jnp.float32) / ints[FAN2 + 1][:, None].astype(jnp.float32)).astype(jnp.bfloat16)
    rel = ints - feat * ROWS
    rel = jnp.where((rel >= 0) & (rel < ROWS), rel, -1).astype(jnp.float32)
    d_pre, second = seeds_step(rel, dl, dz, h_saved, w_self2, w_nbr2)
    lines = [[2 * z + c for z in range(N_FEAT // 2)] for c in range(2)]
    d_pre = lax.all_gather(d_pre, "feat", axis=0, tiled=True, axis_index_groups=lines)
    hidden, classes = second.shape[1:]
    second = second.reshape(2, N_FEAT, hidden // N_FEAT, classes).transpose(1, 0, 2, 3)
    second = second_sum(second).transpose(1, 0, 2, 3).reshape(2, hidden, classes)

    def half_rows(a):
        a = a.reshape(a.shape[:-1] + (N_FEAT // 2, 2, ROWS))
        return lax.dynamic_index_in_dim(a, core, axis=a.ndim - 2, keepdims=False).reshape(a.shape[:-3] + (-1,))

    count = half_rows(cnt1)
    slots = jnp.concatenate([half_rows(self_slot)[None], half_rows(nbr1)], axis=0)
    part = N_DP * HALF
    side = jnp.where(lax.rem(lax.div(slots, HALF), 2) == core, 0, part)
    place = jnp.where(slots < N_DP * CAP, side + lax.div(slots, CAP) * HALF + lax.rem(slots, HALF), slots)
    read = lax.iota(jnp.int32, PICKS)[:, None] <= count[None, :]
    place = jnp.where(read, place, ZERO_ROW).T.reshape(-1)
    rows = fold(
        place, own.reshape(part, WIDE), other.reshape(part, WIDE), hub, count[:, None].astype(jnp.float32)
    )
    summed = lax.dot_general(rows, d_pre, (((0,), (0,)), ((), ())), preferred_element_type=jnp.float32)
    width = h_saved.shape[1]
    summed = summed.reshape(2, 2, 64, width).transpose(1, 0, 2, 3).reshape(2, WIDE, width)
    first = first_sum(summed)
    return (first[:64], first[64:], second[0], second[1])


def solution(mesh):
    placed = (
        P("feat", "dp"),
        P("feat", None),
        P("dp", None, None),
        P("dp"),
        P(None, "dp"),
        P("dp"),
        P(("dp", "feat"), None),
        P(("dp", "feat")),
        P(("dp", "feat"), None),
        P(("dp", "feat")),
        P(("dp", "feat"), None),
        P(),
        P(),
    )
    return jax.shard_map(
        body,
        mesh=mesh,
        in_specs=placed,
        out_specs=(P("feat", None), P("feat", None), P(), P()),
        check_vma=False,
    )
```

```python
import jax
import jax.numpy as jnp
from jax import lax
from jax.experimental import pallas as pl
from jax.experimental.pallas import tpu as pltpu
from jax.sharding import PartitionSpec as P

N_DP = 16
N_FEAT = 16
CAP = 2048
HALF = CAP // 2
HUBS = 2048
ROWS = 256
FAN1 = 10
FAN2 = 25
PICKS = 1 + FAN1
WIDE = 128
ZERO_ROW = N_DP * CAP + HUBS
MESH = pl.DeviceIdType.MESH
VMEM_LIMIT = 60 * 1024 * 1024


def vmem():
    return pl.BlockSpec(memory_space=pltpu.VMEM)


def smem():
    return pl.BlockSpec(memory_space=pltpu.SMEM)


def remote(src, dst, sems, slot, device):
    return pltpu.make_async_remote_copy(
        src_ref=src,
        dst_ref=dst,
        send_sem=sems.at[0, slot],
        recv_sem=sems.at[1, slot],
        device_id=device,
        device_id_type=MESH,
    )


def greet(peers):
    barrier = pltpu.get_barrier_semaphore()
    for peer in peers:
        pl.semaphore_signal(barrier, inc=1, device_id=peer, device_id_type=MESH)
    pl.semaphore_wait(barrier, len(peers))


def main_kernel(
    send_ref, slot_ref, x_ref, hub_ref, count_ref, out_ref,
    feats_ref, nodes_ref, stage_ref, own_ref, other_ref, table_ref, rows_ref, self_ref, sum_ref,
    swap_sems, far_sems, near_sems,
):
    dp = lax.axis_index("dp")
    feat = lax.axis_index("feat")
    core = lax.rem(feat, 2)
    partner = (dp, feat + 1 - 2 * core)
    wide = [(k, lax.rem(dp + k, N_DP), lax.rem(dp + N_DP - k, N_DP)) for k in range(N_DP)]
    greet([partner] + [(to, feat) for _, to, _ in wide[1:]])

    nodes = x_ref.shape[1]
    lane = pl.ds(pl.multiple_of(core * 64, 64), 64)
    swaps = [
        remote(x_ref, feats_ref.at[lane, pl.ds(0, nodes)], swap_sems, 0, partner),
        remote(hub_ref, feats_ref.at[lane, pl.ds(nodes, HUBS)], swap_sems, 1, partner),
    ]
    for copy in swaps:
        copy.start()
    feats_ref[lane, pl.ds(0, nodes)] = x_ref[...]
    feats_ref[lane, pl.ds(nodes, HUBS)] = hub_ref[...]
    swaps[0].wait_recv()

    def turn(block, carry):
        at = pl.multiple_of(block * 128, 128)
        nodes_ref[pl.ds(at, 128), :] = feats_ref[:, pl.ds(at, 128)].astype(jnp.float32).T
        return carry

    lax.fori_loop(0, nodes // 128, turn, 0)

    step = 32
    far = []
    for k, to, _ in wide[1:] + wide[:1]:
        first = to * HALF

        def some_rows(block, carry, first=first):
            at = pl.multiple_of(block * step, step)
            got = [nodes_ref[pl.ds(send_ref[first + at + r], 1), :] for r in range(step)]
            for r in range(step):
                rows_ref[pl.ds(at + r, 1), :] = got[r]
            return carry

        lax.fori_loop(0, HALF // step, some_rows, 0)
        if k == 0:
            own_ref[dp] = rows_ref[...].astype(jnp.bfloat16)
        else:
            stage_ref[k] = rows_ref[...].astype(jnp.bfloat16)
            copy = remote(stage_ref.at[k], own_ref.at[dp], far_sems, k, (to, feat))
            copy.start()
            far.append(copy)

    part = N_DP * HALF
    near = []
    for k, _, source in wide:
        if k:
            far[k - 1].wait_recv()
        copy = remote(own_ref.at[source], other_ref.at[source], near_sems, k, partner)
        copy.start()
        near.append(copy)
        at = pl.multiple_of(source * HALF, HALF)
        table_ref[pl.ds(at, HALF), :] = own_ref[source].astype(jnp.float32)
    swaps[1].wait_recv()

    def turn_hub(block, carry):
        at = pl.multiple_of(block * 128, 128)
        table_ref[pl.ds(2 * part + at, 128), :] = feats_ref[:, pl.ds(nodes + at, 128)].astype(jnp.float32).T
        return carry

    lax.fori_loop(0, HUBS // 128, turn_hub, 0)
    table_ref[pl.ds(ZERO_ROW, 8), :] = jnp.zeros((8, WIDE), jnp.float32)
    for k, _, source in wide:
        near[k].wait_recv()
        at = pl.multiple_of(part + source * HALF, HALF)
        table_ref[pl.ds(at, HALF), :] = other_ref[source].astype(jnp.float32)

    unroll = 8

    def some_sums(block, carry):
        at = pl.multiple_of(block * unroll, unroll)
        for r in range(unroll):
            first = (at + r) * PICKS
            got = [table_ref[pl.ds(slot_ref[first + j], 1), :] for j in range(PICKS)]
            rest = got[1:]
            while len(rest) > 1:
                rest = [rest[i] + rest[i + 1] if i + 1 < len(rest) else rest[i] for i in range(0, len(rest), 2)]
            self_ref[pl.ds(at + r, 1), :] = got[0]
            sum_ref[pl.ds(at + r, 1), :] = rest[0]
        return carry

    lax.fori_loop(0, 8 * ROWS // unroll, some_sums, 0)
    out_ref[:, :WIDE] = self_ref[...].astype(jnp.bfloat16)
    out_ref[:, WIDE:] = (sum_ref[...] / count_ref[...]).astype(jnp.bfloat16)
    for copy in swaps + far + near:
        copy.wait_send()


def main_step(send, slots, x, hub, count):
    rows = 8 * ROWS
    nodes = x.shape[1]
    return pl.pallas_call(
        main_kernel,
        out_shape=jax.ShapeDtypeStruct((rows, 2 * WIDE), jnp.bfloat16),
        in_specs=[smem(), smem(), vmem(), vmem(), vmem()],
        out_specs=vmem(),
        scratch_shapes=[
            pltpu.VMEM((WIDE, nodes + HUBS), jnp.bfloat16),
            pltpu.VMEM((nodes, WIDE), jnp.float32),
            pltpu.VMEM((N_DP, HALF, WIDE), jnp.bfloat16),
            pltpu.VMEM((N_DP, HALF, WIDE), jnp.bfloat16),
            pltpu.VMEM((N_DP, HALF, WIDE), jnp.bfloat16),
            pltpu.VMEM((ZERO_ROW + 8, WIDE), jnp.float32),
            pltpu.VMEM((HALF, WIDE), jnp.float32),
            pltpu.VMEM((rows, WIDE), jnp.float32),
            pltpu.VMEM((rows, WIDE), jnp.float32),
            pltpu.SemaphoreType.DMA((2, 2)),
            pltpu.SemaphoreType.DMA((2, N_DP)),
            pltpu.SemaphoreType.DMA((2, N_DP)),
        ],
        compiler_params=pltpu.CompilerParams(collective_id=3, has_side_effects=True, vmem_limit_bytes=VMEM_LIMIT),
        name="main_step",
    )(send, slots, x, hub, count)


def seeds_kernel(rel_ref, dl_ref, dz_ref, h_ref, ws_ref, wn_ref, dpre_ref, second_ref, tally_ref, hot_ref):
    seeds = rel_ref.shape[1]
    row_id = lax.broadcasted_iota(jnp.int32, (ROWS, 128), 0).astype(jnp.float32).astype(jnp.bfloat16)
    one = jnp.ones((ROWS, 128), jnp.bfloat16)
    none = jnp.zeros((ROWS, 128), jnp.bfloat16)

    def count(block, carry):
        cols = pl.ds(pl.multiple_of(block * 128, 128), 128)
        total = none
        for j in range(FAN2):
            line = jnp.broadcast_to(rel_ref[pl.ds(j, 1), cols].astype(jnp.bfloat16), (ROWS, 128))
            total = total + jnp.where(line == row_id, one, none)
        tally_ref[:, cols] = total
        line = jnp.broadcast_to(rel_ref[pl.ds(FAN2, 1), cols].astype(jnp.bfloat16), (ROWS, 128))
        hot_ref[:, cols] = jnp.where(line == row_id, one, none)
        return carry

    lax.fori_loop(0, seeds // 128, count, 0)
    chunk = 1024
    classes = dl_ref.shape[1]

    def gather(block, carry):
        at = pl.ds(pl.multiple_of(block * chunk, chunk), chunk)
        nbr = carry[0] + jnp.dot(tally_ref[:, at], dz_ref[at, :], preferred_element_type=jnp.float32)
        own = carry[1] + jnp.dot(hot_ref[:, at], dl_ref[at, :], preferred_element_type=jnp.float32)
        return nbr, own

    zero = jnp.zeros((ROWS, classes), jnp.float32)
    nbr, own = lax.fori_loop(0, seeds // chunk, gather, (zero, zero))
    highest = lax.Precision.HIGHEST
    last = (((1,), (1,)), ((), ()))
    h = h_ref[...].astype(jnp.float32)
    hidden = lax.dot_general(nbr, wn_ref[...].astype(jnp.float32), last, precision=highest, preferred_element_type=jnp.float32)
    hidden = hidden + lax.dot_general(own, ws_ref[...].astype(jnp.float32), last, precision=highest, preferred_element_type=jnp.float32)
    dpre_ref[...] = jnp.where(h > 0, hidden, 0.0).astype(jnp.bfloat16)
    ht = h.T
    second_ref[0] = jnp.dot(ht, own, precision=highest, preferred_element_type=jnp.float32)
    second_ref[1] = jnp.dot(ht, nbr, precision=highest, preferred_element_type=jnp.float32)


def seeds_step(rel, dl, dz, h, ws, wn):
    seeds = rel.shape[1]
    return pl.pallas_call(
        seeds_kernel,
        out_shape=(
            jax.ShapeDtypeStruct(h.shape, jnp.bfloat16),
            jax.ShapeDtypeStruct((2, h.shape[1], dl.shape[1]), jnp.float32),
        ),
        in_specs=[vmem()] * 6,
        out_specs=(vmem(), vmem()),
        scratch_shapes=[pltpu.VMEM((ROWS, seeds), jnp.bfloat16), pltpu.VMEM((ROWS, seeds), jnp.bfloat16)],
        compiler_params=pltpu.CompilerParams(vmem_limit_bytes=VMEM_LIMIT),
        name="seeds",
    )(rel, dl, dz, h, ws, wn)


def first_kernel(part_ref, out_ref, got_ref, done_ref, send_sem, recv_sem, send2_sem, recv2_sem):
    dp = lax.axis_index("dp")
    feat = lax.axis_index("feat")
    core = lax.rem(feat, 2)
    peers = []
    for flip in range(2):
        to_core = (1 - core) if flip else core
        to_feat = feat - core + to_core
        for shift in range(N_DP):
            if flip == 0 and shift == 0:
                continue
            to_dp = lax.rem(dp + shift, N_DP)
            peers.append((flip * N_DP + shift, to_dp, to_feat, to_core))
    greet([(d, f) for _, d, f, _ in peers])
    copies = []
    for slot, to_dp, to_feat, to_core in peers:
        copy = pltpu.make_async_remote_copy(
            src_ref=part_ref.at[to_core, pl.ds(pl.multiple_of(to_dp * 8, 8), 8), :],
            dst_ref=got_ref.at[slot],
            send_sem=send_sem.at[slot],
            recv_sem=recv_sem.at[slot],
            device_id=(to_dp, to_feat),
            device_id_type=MESH,
        )
        copy.start()
        copies.append(copy)
    mine = pl.ds(pl.multiple_of(dp * 8, 8), 8)
    total = part_ref[core, mine, :]
    for (slot, _, _, _), copy in zip(peers, copies):
        copy.wait_recv()
        total = total + got_ref[slot]
    done_ref[mine, :] = total
    spread = []
    for slot, to_dp, to_feat, _ in peers:
        if slot >= N_DP:
            continue
        copy = pltpu.make_async_remote_copy(
            src_ref=done_ref.at[mine, :],
            dst_ref=done_ref.at[mine, :],
            send_sem=send2_sem.at[slot],
            recv_sem=recv2_sem.at[slot],
            device_id=(to_dp, to_feat),
            device_id_type=MESH,
        )
        copy.start()
        spread.append(copy)
    for copy in copies:
        copy.wait_send()
    for copy in spread:
        copy.wait()
    out_ref[...] = done_ref[...]


def first_sum(part):
    width = part.shape[2]
    return pl.pallas_call(
        first_kernel,
        out_shape=jax.ShapeDtypeStruct((WIDE, width), jnp.float32),
        in_specs=[vmem()],
        out_specs=vmem(),
        scratch_shapes=[
            pltpu.VMEM((2 * N_DP, 8, width), jnp.float32),
            pltpu.VMEM((WIDE, width), jnp.float32),
            pltpu.SemaphoreType.DMA((2 * N_DP,)),
            pltpu.SemaphoreType.DMA((2 * N_DP,)),
            pltpu.SemaphoreType.DMA((N_DP,)),
            pltpu.SemaphoreType.DMA((N_DP,)),
        ],
        compiler_params=pltpu.CompilerParams(collective_id=1, has_side_effects=True, vmem_limit_bytes=VMEM_LIMIT),
        name="first_sum",
    )(part)


def second_kernel(part_ref, out_ref, got_ref, mid_ref, got2_ref, sems):
    dp = lax.axis_index("dp")
    feat = lax.axis_index("feat")
    along_feat = [(k, lax.rem(feat + k, N_FEAT)) for k in range(1, N_FEAT)]
    along_dp = [(k, lax.rem(dp + k, N_DP)) for k in range(1, N_DP)]
    greet([(dp, f) for _, f in along_feat] + [(d, feat) for _, d in along_dp])
    copies = []

    def push(src, dst, stage, slot, device):
        copy = pltpu.make_async_remote_copy(
            src_ref=src,
            dst_ref=dst,
            send_sem=sems.at[2 * stage, slot],
            recv_sem=sems.at[2 * stage + 1, slot],
            device_id=device,
            device_id_type=MESH,
        )
        copy.start()
        copies.append(copy)
        return copy

    scattered = [push(part_ref.at[f], got_ref.at[k], 0, k, (dp, f)) for k, f in along_feat]
    total = part_ref[feat]
    for (k, _), copy in zip(along_feat, scattered):
        copy.wait_recv()
        total = total + got_ref[k]
    mid_ref[...] = total
    summed = [push(mid_ref, got2_ref.at[k], 1, k, (d, feat)) for k, d in along_dp]
    for (k, _), copy in zip(along_dp, summed):
        copy.wait_recv()
        total = total + got2_ref[k]
    out_ref[feat] = total
    gathered = [push(out_ref.at[feat], out_ref.at[feat], 2, k, (dp, f)) for k, f in along_feat]
    for copy in gathered:
        copy.wait_recv()
    for copy in copies:
        copy.wait_send()


def second_sum(part):
    piece = part.shape[1:]
    return pl.pallas_call(
        second_kernel,
        out_shape=jax.ShapeDtypeStruct(part.shape, jnp.float32),
        in_specs=[vmem()],
        out_specs=vmem(),
        scratch_shapes=[
            pltpu.VMEM((N_FEAT,) + piece, jnp.float32),
            pltpu.VMEM(piece, jnp.float32),
            pltpu.VMEM((N_DP,) + piece, jnp.float32),
            pltpu.SemaphoreType.DMA((6, 16)),
        ],
        compiler_params=pltpu.CompilerParams(collective_id=2, has_side_effects=True, vmem_limit_bytes=VMEM_LIMIT),
        name="second_sum",
    )(part)


def body(
    x_table,
    hub_feats,
    send_rows,
    self_slot,
    nbr1,
    cnt1,
    h_saved,
    seed_self,
    nbr2,
    cnt2,
    d_logits,
    w_self2,
    w_nbr2,
):
    feat = lax.axis_index("feat")
    core = lax.rem(feat, 2)
    wanted = lax.dynamic_slice_in_dim(send_rows[0], core * HALF, HALF, axis=1).reshape(-1)

    kept = lax.iota(jnp.int32, FAN2)[:, None] < cnt2[None, :]
    ints = jnp.concatenate(
        [jnp.where(kept, nbr2.T, -1), seed_self[None], cnt2[None], jnp.zeros((32 - FAN2 - 2, ROWS), jnp.int32)], axis=0
    )
    ints = lax.all_gather(ints, "feat", axis=1, tiled=True)
    dl = lax.all_gather(d_logits, "feat", axis=0, tiled=True)
    dz = (dl.astype(jnp.float32) / ints[FAN2 + 1][:, None].astype(jnp.float32)).astype(jnp.bfloat16)
    rel = ints - feat * ROWS
    rel = jnp.where((rel >= 0) & (rel < ROWS), rel, -1).astype(jnp.float32)
    d_pre, second = seeds_step(rel, dl, dz, h_saved, w_self2, w_nbr2)
    lines = [[2 * z + c for z in range(N_FEAT // 2)] for c in range(2)]
    d_pre = lax.all_gather(d_pre, "feat", axis=0, tiled=True, axis_index_groups=lines)
    hidden, classes = second.shape[1:]
    second = second.reshape(2, N_FEAT, hidden // N_FEAT, classes).transpose(1, 0, 2, 3)
    second = second_sum(second).transpose(1, 0, 2, 3).reshape(2, hidden, classes)

    def half_rows(a):
        a = a.reshape(a.shape[:-1] + (N_FEAT // 2, 2, ROWS))
        return lax.dynamic_index_in_dim(a, core, axis=a.ndim - 2, keepdims=False).reshape(a.shape[:-3] + (-1,))

    count = half_rows(cnt1)
    slots = jnp.concatenate([half_rows(self_slot)[None], half_rows(nbr1)], axis=0)
    part = N_DP * HALF
    side = jnp.where(lax.rem(lax.div(slots, HALF), 2) == core, 0, part)
    place = jnp.where(slots < N_DP * CAP, side + lax.div(slots, CAP) * HALF + lax.rem(slots, HALF), slots)
    read = lax.iota(jnp.int32, PICKS)[:, None] <= count[None, :]
    place = jnp.where(read, place, ZERO_ROW).T.reshape(-1)
    rows = main_step(wanted, place, x_table, hub_feats, count[:, None].astype(jnp.float32))
    summed = lax.dot_general(rows, d_pre, (((0,), (0,)), ((), ())), preferred_element_type=jnp.float32)
    width = h_saved.shape[1]
    summed = summed.reshape(2, 2, 64, width).transpose(1, 0, 2, 3).reshape(2, WIDE, width)
    first = first_sum(summed)
    return (first[:64], first[64:], second[0], second[1])


def solution(mesh):
    placed = (
        P("feat", "dp"),
        P("feat", None),
        P("dp", None, None),
        P("dp"),
        P(None, "dp"),
        P("dp"),
        P(("dp", "feat"), None),
        P(("dp", "feat")),
        P(("dp", "feat"), None),
        P(("dp", "feat")),
        P(("dp", "feat"), None),
        P(),
        P(),
    )
    return jax.shard_map(
        body,
        mesh=mesh,
        in_specs=placed,
        out_specs=(P("feat", None), P("feat", None), P(), P()),
        check_vma=False,
    )
```

```python
import jax
import jax.numpy as jnp
from jax import lax
from jax.experimental import pallas as pl
from jax.experimental.pallas import tpu as pltpu
from jax.sharding import PartitionSpec as P

N_DP = 16
SIDE = 4
N_FEAT = 16
N_Z = 8
CAP = 2048
HALF = CAP // 2
QUARTER = HALF // 2
HUBS = 2048
NODES = 8192
ROWS = 256
GROUP = N_Z * ROWS
HIDDEN = 512
CLASSES = 172
TALL = 176
FAN1 = 10
FAN2 = 25
PICKS = 1 + FAN1
WIDE = 128
PART = N_DP * HALF
ZERO_ROW = 2 * PART + HUBS
NOTE = TALL + 64
MESH = pl.DeviceIdType.MESH
F32 = jnp.float32
BF16 = jnp.bfloat16
HIGHEST = lax.Precision.HIGHEST

TWO = [(2, 2), (2, 0), (0, 2), (2, 1), (2, 3), (1, 2), (3, 2)]
DIAGONAL = [(1, 1), (3, 3), (1, 3), (3, 1)]
NEXT = [(1, 0), (3, 0), (0, 1), (0, 3)]


def through(shift, half):
    one = 3 if half else 1
    dx, dy = shift
    if dx == 2:
        return (one, one if dy == 2 else 0)
    return (dx, one)


STAGED = [(shift, half) for shift in TWO for half in range(2)]


def main_kernel(
    send_ref, slot_ref, x_ref, hub_ref, cnt1_ref, h_ref, seed_ref, nbr2_ref, cnt2_ref, dl_ref, ws_ref, wn_ref,
    self1_ref, nbr1_ref, self2_ref, nbr2o_ref,
    feats_ref, nodes_ref, stage_ref, mid_ref, own_ref, other_ref, table_ref, rows_ref,
    note_ref, gn_ref, gs_ref, gnt_ref, gst_ref, dpre_ref, second_ref, extra_ref, piece_ref, pieces_ref, column_ref, columns_ref, final_ref,
    self_ref, sum_ref, acc_ref, part_ref, theirs_ref, got_ref, done_ref,
    swap_sems, mid_sems, far_sems, near_sems, note_up, note_down, note_over,
    dpre_up, dpre_down, over_sems, z_sems, dp_sems, z2_sems, first_sems, first2_sems,
):
    dp = lax.axis_index("dp")
    feat = lax.axis_index("feat")
    core = lax.rem(feat, 2)
    z = lax.div(feat, 2)
    px = lax.div(dp, SIDE)
    py = lax.rem(dp, SIDE)
    partner = (dp, feat + 1 - 2 * core)
    pending = []

    def at_shift(dx, dy):
        return lax.rem(px + dx + SIDE, SIDE) * SIDE + lax.rem(py + dy + SIDE, SIDE)

    def z_feat(step):
        return lax.rem(z + step + N_Z, N_Z) * 2 + core

    def push(src, dst, sems, slot, device):
        copy = pltpu.make_async_remote_copy(
            src_ref=src,
            dst_ref=dst,
            send_sem=sems.at[0, slot],
            recv_sem=sems.at[1, slot],
            device_id=device,
            device_id_type=MESH,
        )
        copy.start()
        pending.append(copy)
        return copy

    barrier = pltpu.get_barrier_semaphore()
    peers = [partner]
    peers += [(at_shift(k // SIDE, k % SIDE), feat) for k in range(1, N_DP)]
    peers += [(dp, z_feat(k)) for k in range(1, N_Z)]
    for peer in peers:
        pl.semaphore_signal(barrier, inc=1, device_id=peer, device_id_type=MESH)
    pl.semaphore_wait(barrier, len(peers))

    lane = pl.ds(pl.multiple_of(core * 64, 64), 64)
    swap_x = push(x_ref, feats_ref.at[lane, pl.ds(0, NODES)], swap_sems, 0, partner)
    swap_hub = push(hub_ref, feats_ref.at[lane, pl.ds(NODES, HUBS)], swap_sems, 1, partner)

    cnt2 = cnt2_ref[...]
    kept = lax.broadcasted_iota(jnp.int32, (FAN2, ROWS), 0) < cnt2
    named = jnp.concatenate([jnp.where(kept, nbr2_ref[...], N_FEAT * ROWS), seed_ref[...]], axis=0)
    high = lax.div(named, ROWS)
    low = named - high * ROWS
    blank = jnp.zeros((32 - FAN2 - 1, ROWS), jnp.int32)
    fours = jnp.zeros((32 - FAN2 - 2, ROWS), jnp.int32)
    note_ref[feat, pl.ds(0, TALL), :] = jnp.concatenate(
        [dl_ref[...].astype(F32), jnp.zeros((TALL - CLASSES, ROWS), F32)], axis=0
    ).astype(BF16)
    note_ref[feat, pl.ds(TALL, 32), :] = jnp.concatenate([high, cnt2, fours], axis=0).astype(F32).astype(BF16)
    note_ref[feat, pl.ds(TALL + 32, 32), :] = jnp.concatenate([low, blank], axis=0).astype(F32).astype(BF16)

    class Ring:
        def __init__(self, view, up, down, over=None):
            self.view, self.up, self.down, self.over = view, up, down, over
            self.from_below, self.from_above, self.crossed = {}, {}, []

        def send_up(self, step):
            block = self.view(1 - step)
            self.from_below[step] = push(block, block, self.up, step - 1, (dp, z_feat(1)))

        def send_down(self, step):
            block = self.view(step - 1)
            self.from_above[step] = push(block, block, self.down, step - 1, (dp, z_feat(-1)))

        def cross(self, step):
            if self.over is not None:
                block = self.view(step)
                self.crossed.append(push(block, block, self.over, len(self.crossed), partner))

        def start(self):
            self.send_up(1)
            self.send_down(1)
            self.cross(0)

        def take(self, step):
            self.from_below[step].wait_recv()
            if step < 4:
                self.send_up(step + 1)
            self.cross(-step)
            if step < 4:
                self.from_above[step].wait_recv()
                if step < 3:
                    self.send_down(step + 1)
                self.cross(step)

    notes = Ring(lambda step: note_ref.at[z_feat(step)], note_up, note_down, note_over)
    notes.start()

    feats_ref[lane, pl.ds(0, NODES)] = x_ref[...]
    feats_ref[lane, pl.ds(NODES, HUBS)] = hub_ref[...]
    swap_x.wait_recv()
    nodes_flat = nodes_ref.reshape(NODES, WIDE)
    table_flat = table_ref.reshape(ZERO_ROW + 8, WIDE)
    rows_flat = rows_ref.reshape(QUARTER, WIDE)

    def turn(block, carry):
        at = pl.multiple_of(block * 128, 128)
        nodes_flat[pl.ds(at, 128), :] = feats_ref[:, pl.ds(at, 128)].astype(F32).T
        return carry

    lax.fori_loop(0, NODES // 128, turn, 0)

    far = {}
    staged = {}

    def pick(shift, half):
        to = at_shift(*shift)
        first = to * HALF + half * QUARTER
        unroll = 32

        def some_rows(block, carry):
            at = pl.multiple_of(block * unroll, unroll)
            got = [nodes_ref[send_ref[first + at + r]] for r in range(unroll)]
            for r in range(unroll):
                rows_ref[at + r] = got[r]
            return carry

        lax.fori_loop(0, QUARTER // unroll, some_rows, 0)
        slot = 2 * (shift[0] * SIDE + shift[1]) + half
        if shift == (0, 0):
            own_ref[dp, half] = rows_flat[...].astype(BF16)
            return
        stage_ref[slot] = rows_flat[...].astype(BF16)
        if (shift, half) in STAGED:
            s = STAGED.index((shift, half))
            staged[s] = push(stage_ref.at[slot], mid_ref.at[s], mid_sems, s, (at_shift(*through(shift, half)), feat))
        else:
            far[slot] = push(stage_ref.at[slot], own_ref.at[dp, half], far_sems, slot, (to, feat))

    def pass_on(s):
        shift, half = STAGED[s]
        mx, my = through(shift, half)
        slot = 2 * (shift[0] * SIDE + shift[1]) + half
        staged[s].wait_recv()
        source = at_shift(-mx, -my)
        to = at_shift(shift[0] - mx, shift[1] - my)
        far[slot] = push(mid_ref.at[s], own_ref.at[source, half], far_sems, slot, (to, feat))

    near = {}

    def arrive(shift, half):
        slot = 2 * (shift[0] * SIDE + shift[1]) + half
        source = at_shift(-shift[0], -shift[1])
        if slot in far:
            far[slot].wait_recv()
        near[slot] = push(own_ref.at[source, half], other_ref.at[source, half], near_sems, slot, partner)
        at = pl.multiple_of(source * HALF + half * QUARTER, QUARTER)
        table_flat[pl.ds(at, QUARTER), :] = own_ref[source, half].astype(F32)

    def cross(shift, half):
        slot = 2 * (shift[0] * SIDE + shift[1]) + half
        source = at_shift(-shift[0], -shift[1])
        near[slot].wait_recv()
        at = pl.multiple_of(PART + source * HALF + half * QUARTER, QUARTER)
        table_flat[pl.ds(at, QUARTER), :] = other_ref[source, half].astype(F32)

    for number, shift in enumerate(TWO):
        for half in range(2):
            pick(shift, half)
        if number in (2, 4, 6):
            notes.take(number // 2)
    for shift in DIAGONAL:
        for half in range(2):
            pick(shift, half)
    notes.take(4)
    for s in range(len(STAGED)):
        pass_on(s)
    for copy in notes.crossed:
        copy.wait_recv()

    row_id = lax.broadcasted_iota(jnp.int32, (ROWS, 128), 0).astype(F32).astype(BF16)
    one = jnp.ones((ROWS, 128), BF16)
    none = jnp.zeros((ROWS, 128), BF16)
    both_last = (((1,), (1,)), ((), ()))
    mine = jnp.full((32, ROWS), feat, jnp.int32).astype(F32)
    for ref in (gn_ref, gs_ref, gnt_ref, gst_ref):
        ref[...] = jnp.zeros_like(ref)

    def one_device(f, carry):
        high_here = note_ref[f, pl.ds(TALL, 32), :].astype(F32)
        low_here = note_ref[f, pl.ds(TALL + 32, 32), :].astype(F32)
        place = jnp.where(high_here == mine, low_here, -1.0)
        counts = high_here[FAN2 + 1 : FAN2 + 2, :]
        tallies, hots = [], []
        for side in range(ROWS // 128):
            total = none
            for j in range(FAN2 + 1):
                line = place[j : j + 1, side * 128 : side * 128 + 128].astype(BF16)
                match = jnp.where(jnp.broadcast_to(line, (ROWS, 128)) == row_id, one, none)
                if j < FAN2:
                    total = total + match
                else:
                    hots.append(match)
            tallies.append(total)
        tally = jnp.concatenate(tallies, axis=1)
        hot = jnp.concatenate(hots, axis=1)
        dl = note_ref[f, pl.ds(0, TALL), :]
        dz = (dl.astype(F32) / counts).astype(BF16)
        gn_ref[...] += lax.dot_general(tally, dz, both_last, preferred_element_type=F32)
        gs_ref[...] += lax.dot_general(hot, dl, both_last, preferred_element_type=F32)
        gnt_ref[...] += lax.dot_general(dz, tally, both_last, preferred_element_type=F32)
        gst_ref[...] += lax.dot_general(dl, hot, both_last, preferred_element_type=F32)
        return carry

    lax.fori_loop(0, N_FEAT, one_device, 0)
    h = h_ref[...].astype(F32)
    hidden = jnp.dot(gn_ref[:, :CLASSES], wn_ref[...].astype(F32), precision=HIGHEST, preferred_element_type=F32)
    hidden += jnp.dot(gs_ref[:, :CLASSES], ws_ref[...].astype(F32), precision=HIGHEST, preferred_element_type=F32)
    dpre_ref[z] = jnp.where(h > 0, hidden, 0.0).T.astype(BF16)
    second_ref[0] = jnp.dot(gst_ref[...], h, precision=HIGHEST, preferred_element_type=F32)
    second_ref[1] = jnp.dot(gnt_ref[...], h, precision=HIGHEST, preferred_element_type=F32)
    rows_ring = Ring(lambda step: dpre_ref.at[lax.rem(z + step + N_Z, N_Z)], dpre_up, dpre_down)
    rows_ring.start()
    second_over = push(second_ref.at[1 - core], extra_ref, over_sems, 0, partner)

    for shift in NEXT:
        for half in range(2):
            pick(shift, half)
    rows_ring.take(1)
    for half in range(2):
        pick((0, 0), half)
    second_over.wait_recv()
    column_ref[...] = second_ref[core] + extra_ref[...]

    def piece(step):
        to = lax.rem(z + step + N_Z, N_Z)
        tall = pl.ds(pl.multiple_of(lax.div(to, 4) * (TALL // 2), 8), TALL // 2)
        return tall, pl.ds(pl.multiple_of(lax.rem(to, 4) * 128, 128), 128)

    scattered = [push(column_ref.at[piece(k)], pieces_ref.at[k], z_sems, k, (dp, z_feat(k))) for k in range(1, N_Z)]

    swap_hub.wait_recv()

    def turn_hub(block, carry):
        at = pl.multiple_of(block * 128, 128)
        table_flat[pl.ds(2 * PART + at, 128), :] = feats_ref[:, pl.ds(NODES + at, 128)].astype(F32).T
        return carry

    lax.fori_loop(0, HUBS // 128, turn_hub, 0)
    table_flat[pl.ds(ZERO_ROW, 8), :] = jnp.zeros((8, WIDE), F32)

    order = [(shift, half) for shift in [(0, 0)] + DIAGONAL + TWO + NEXT for half in range(2)]
    for number, (shift, half) in enumerate(order):
        arrive(shift, half)
        if number == 16:
            rows_ring.take(2)
    total = column_ref[piece(0)]
    for k, copy in enumerate(scattered):
        copy.wait_recv()
        total = total + pieces_ref[k + 1]
    piece_ref[...] = total
    for shift, half in order:
        cross(shift, half)
    summed = [
        push(piece_ref, columns_ref.at[k], dp_sems, k, (at_shift(k // SIDE, k % SIDE), feat)) for k in range(1, N_DP)
    ]
    rows_ring.take(3)

    self_flat = self_ref.reshape(ROWS, WIDE)
    sum_flat = sum_ref.reshape(ROWS, WIDE)
    unroll = 8

    def fold(step):
        of = lax.rem(z + step + N_Z, N_Z)
        base = of * ROWS

        def some_sums(block, carry):
            at = pl.multiple_of(block * unroll, unroll)
            for r in range(unroll):
                got = [table_ref[slot_ref[j * GROUP + base + at + r]] for j in range(PICKS)]
                rest = got[1:]
                while len(rest) > 1:
                    rest = [rest[i] + rest[i + 1] if i + 1 < len(rest) else rest[i] for i in range(0, len(rest), 2)]
                self_ref[at + r] = got[0]
                sum_ref[at + r] = rest[0]
            return carry

        lax.fori_loop(0, ROWS // unroll, some_sums, 0)
        count = jnp.broadcast_to(cnt1_ref[of].astype(F32), (WIDE, ROWS)).T
        own = self_flat[...].astype(BF16)
        mean = (sum_flat[...] / count).astype(BF16)
        both = jnp.concatenate([own, mean], axis=1)
        product = jnp.dot(dpre_ref[of], both, preferred_element_type=F32)
        if step == 0:
            acc_ref[...] = product
        else:
            acc_ref[...] += product

    gathered = []
    for number, step in enumerate((0, -1, 1, -2, 2, -3, 3, -4)):
        fold(step)
        if number == 3:
            rows_ring.take(4)
            total = piece_ref[...]
            for k, copy in enumerate(summed):
                copy.wait_recv()
                total = total + columns_ref[k + 1]
            mine_tall, mine_lanes = piece(0)
            block = final_ref.at[core, mine_tall, mine_lanes]
            final_ref[core, mine_tall, mine_lanes] = total
            for k in range(1, N_Z):
                gathered.append(push(block, block, z2_sems, k, (dp, z_feat(k))))
        if number == 6:
            for copy in gathered:
                copy.wait_recv()
            second_back = push(final_ref.at[core], final_ref.at[core], over_sems, 1, partner)

    part_ref[...] = acc_ref[...].T
    first_over = [
        push(
            part_ref.at[pl.ds(pl.multiple_of(64 * (2 * i + 1 - core), 64), 64), :],
            theirs_ref.at[i],
            over_sems,
            2 + i,
            partner,
        )
        for i in range(2)
    ]
    second_back.wait_recv()
    self2_ref[...] = final_ref[0, :CLASSES, :]
    nbr2o_ref[...] = final_ref[1, :CLASSES, :]
    for i in range(2):
        first_over[i].wait_recv()
        mine_here = part_ref[pl.ds(pl.multiple_of(64 * (2 * i + core), 64), 64), :] + theirs_ref[i]
        part_ref[pl.ds(pl.multiple_of(64 * (2 * i + core), 64), 64), :] = mine_here

    def eight(to):
        return pl.ds(pl.multiple_of(lax.div(to, 8) * 128 + core * 64 + lax.rem(to, 8) * 8, 8), 8)

    spread = []
    for k in range(1, N_DP):
        to = at_shift(k // SIDE, k % SIDE)
        spread.append(push(part_ref.at[eight(to), :], got_ref.at[k], first_sems, k, (to, feat)))
    total = part_ref[eight(dp), :]
    for k, copy in enumerate(spread):
        copy.wait_recv()
        total = total + got_ref[k + 1]
    done_ref[dp] = total
    last = []
    for k in range(1, N_DP):
        to = at_shift(k // SIDE, k % SIDE)
        last.append(push(done_ref.at[dp], done_ref.at[dp], first2_sems, k, (to, feat)))
    for copy in last:
        copy.wait_recv()
    for k in range(8):
        self1_ref[pl.ds(8 * k, 8), :] = done_ref[k]
        nbr1_ref[pl.ds(8 * k, 8), :] = done_ref[8 + k]
    for copy in pending:
        copy.wait_send()


def main_step(send, slots, x, hub, cnt1, h, seed, nbr2, cnt2, dl, ws, wn):
    smem = pl.BlockSpec(memory_space=pltpu.SMEM)
    vmem = pl.BlockSpec(memory_space=pltpu.VMEM)
    dma = pltpu.SemaphoreType.DMA
    return pl.pallas_call(
        main_kernel,
        out_shape=(
            jax.ShapeDtypeStruct((64, HIDDEN), F32),
            jax.ShapeDtypeStruct((64, HIDDEN), F32),
            jax.ShapeDtypeStruct((CLASSES, HIDDEN), F32),
            jax.ShapeDtypeStruct((CLASSES, HIDDEN), F32),
        ),
        in_specs=[smem, smem] + [vmem] * 10,
        out_specs=(vmem,) * 4,
        scratch_shapes=[
            pltpu.VMEM((WIDE, NODES + HUBS), BF16),
            pltpu.VMEM((NODES, 1, WIDE), F32),
            pltpu.VMEM((2 * N_DP, QUARTER, WIDE), BF16),
            pltpu.VMEM((len(STAGED), QUARTER, WIDE), BF16),
            pltpu.VMEM((N_DP, 2, QUARTER, WIDE), BF16),
            pltpu.VMEM((N_DP, 2, QUARTER, WIDE), BF16),
            pltpu.VMEM((ZERO_ROW + 8, 1, WIDE), F32),
            pltpu.VMEM((QUARTER, 1, WIDE), F32),
            pltpu.VMEM((N_FEAT, NOTE, ROWS), BF16),
            pltpu.VMEM((ROWS, TALL), F32),
            pltpu.VMEM((ROWS, TALL), F32),
            pltpu.VMEM((TALL, ROWS), F32),
            pltpu.VMEM((TALL, ROWS), F32),
            pltpu.VMEM((N_Z, HIDDEN, ROWS), BF16),
            pltpu.VMEM((2, TALL, HIDDEN), F32),
            pltpu.VMEM((TALL, HIDDEN), F32),
            pltpu.VMEM((TALL // 2, 128), F32),
            pltpu.VMEM((N_Z, TALL // 2, 128), F32),
            pltpu.VMEM((TALL, HIDDEN), F32),
            pltpu.VMEM((N_DP, TALL // 2, 128), F32),
            pltpu.VMEM((2, TALL, HIDDEN), F32),
            pltpu.VMEM((ROWS, 1, WIDE), F32),
            pltpu.VMEM((ROWS, 1, WIDE), F32),
            pltpu.VMEM((HIDDEN, 2 * WIDE), F32),
            pltpu.VMEM((2 * WIDE, HIDDEN), F32),
            pltpu.VMEM((2, 64, HIDDEN), F32),
            pltpu.VMEM((N_DP, 8, HIDDEN), F32),
            pltpu.VMEM((N_DP, 8, HIDDEN), F32),
            dma((2, 2)),
            dma((2, len(STAGED))),
            dma((2, 2 * N_DP)),
            dma((2, 2 * N_DP)),
            dma((2, 4)),
            dma((2, 4)),
            dma((2, N_Z)),
            dma((2, 4)),
            dma((2, 4)),
            dma((2, 4)),
            dma((2, N_Z)),
            dma((2, N_DP)),
            dma((2, N_Z)),
            dma((2, N_DP)),
            dma((2, N_DP)),
        ],
        compiler_params=pltpu.CompilerParams(
            collective_id=1, has_side_effects=True, vmem_limit_bytes=60 * 1024 * 1024
        ),
        name="main_step",
    )(send, slots, x, hub, cnt1, h, seed, nbr2, cnt2, dl, ws, wn)


def body(
    x_table,
    hub_feats,
    send_rows,
    self_slot,
    nbr1,
    cnt1,
    h_saved,
    seed_self,
    nbr2,
    cnt2,
    d_logits,
    w_self2,
    w_nbr2,
):
    core = lax.rem(lax.axis_index("feat"), 2)
    send = lax.dynamic_slice_in_dim(send_rows[0], core * HALF, HALF, axis=1).reshape(-1)

    def half_rows(a):
        a = a.reshape(a.shape[:-1] + (N_Z, 2, ROWS))
        return lax.dynamic_index_in_dim(a, core, axis=a.ndim - 2, keepdims=False).reshape(a.shape[:-3] + (-1,))

    count = half_rows(cnt1)
    slots = jnp.concatenate([half_rows(self_slot)[None], half_rows(nbr1)], axis=0)
    side = jnp.where(lax.rem(lax.div(slots, HALF), 2) == core, 0, PART)
    place = jnp.where(slots < N_DP * CAP, side + lax.div(slots, CAP) * HALF + lax.rem(slots, HALF), slots)
    read = lax.iota(jnp.int32, PICKS)[:, None] <= count[None, :]
    place = jnp.where(read, place, ZERO_ROW).reshape(-1)
    self1, nbr1_out, self2, nbr2_out = main_step(
        send,
        place,
        x_table,
        hub_feats,
        count.reshape(N_Z, 1, ROWS),
        h_saved,
        seed_self[None],
        nbr2.T,
        cnt2[None],
        d_logits.T,
        w_self2.T,
        w_nbr2.T,
    )
    return (self1, nbr1_out, self2.T, nbr2_out.T)


def solution(mesh):
    placed = (
        P("feat", "dp"),
        P("feat", None),
        P("dp", None, None),
        P("dp"),
        P(None, "dp"),
        P("dp"),
        P(("dp", "feat"), None),
        P(("dp", "feat")),
        P(("dp", "feat"), None),
        P(("dp", "feat")),
        P(("dp", "feat"), None),
        P(),
        P(),
    )
    return jax.shard_map(
        body,
        mesh=mesh,
        in_specs=placed,
        out_specs=(P("feat", None), P("feat", None), P(), P()),
        check_vma=False,
    )
```

```python
import jax
import jax.numpy as jnp
from jax import lax
from jax.experimental import pallas as pl
from jax.experimental.pallas import tpu as pltpu
from jax.sharding import PartitionSpec as P

N_DP = 16
SIDE = 4
N_FEAT = 16
N_Z = 8
CAP = 2048
HALF = CAP // 2
QUARTER = HALF // 2
HUBS = 2048
NODES = 8192
ROWS = 256
GROUP = N_Z * ROWS
HIDDEN = 512
CLASSES = 172
TALL = 176
FAN1 = 10
FAN2 = 25
PICKS = 1 + FAN1
WIDE = 128
PART = N_DP * HALF
ZERO_ROW = 2 * PART + HUBS
NOTE = TALL + 32
NAMES = FAN2 + 1
MESH = pl.DeviceIdType.MESH
F32 = jnp.float32
BF16 = jnp.bfloat16
HIGHEST = lax.Precision.HIGHEST

TWO = [(2, 2), (2, 0), (0, 2), (2, 1), (2, 3), (1, 2), (3, 2)]
DIAGONAL = [(1, 1), (3, 3), (1, 3), (3, 1)]
NEXT = [(1, 0), (3, 0), (0, 1), (0, 3)]


def through(shift, half):
    one = 3 if half else 1
    dx, dy = shift
    if dx == 2:
        return (one, one if dy == 2 else 0)
    return (dx, one)


STAGED = [(shift, half) for shift in TWO for half in range(2)]


def main_kernel(
    send_rows_ref, self_slot_ref, slots_ref, x_ref, hub_ref, cnt1_ref, h_ref, seed_ref, nbr2_ref, cnt2_ref, dl_ref, ws_ref, wn_ref,
    self1_ref, nbr1_ref, self2_ref, nbr2o_ref,
    feats_ref, nodes_ref, stage_ref, mid_ref, own_ref, other_ref, table_ref, rows_ref,
    send_ref, place_ref, slot_ref, code_ref, note_ref, gnt_ref, gst_ref, dpre_ref, second_ref, extra_ref, piece_ref, pieces_ref, column_ref, columns_ref, final_ref,
    self_ref, sum_ref, acc_ref, part_ref, theirs_ref, got_ref, done_ref,
    index_sems, swap_sems, mid_sems, far_sems, near_sems, note_up, note_down, note_over,
    dpre_up, dpre_down, over_sems, z_sems, dp_sems, z2_sems, first_sems, first2_sems,
):
    dp = lax.axis_index("dp")
    feat = lax.axis_index("feat")
    core = lax.rem(feat, 2)
    z = lax.div(feat, 2)
    px = lax.div(dp, SIDE)
    py = lax.rem(dp, SIDE)
    partner = (dp, feat + 1 - 2 * core)
    pending = []

    def at_shift(dx, dy):
        return lax.rem(px + dx + SIDE, SIDE) * SIDE + lax.rem(py + dy + SIDE, SIDE)

    def z_feat(step):
        return lax.rem(z + step + N_Z, N_Z) * 2 + core

    def push(src, dst, sems, slot, device):
        copy = pltpu.make_async_remote_copy(
            src_ref=src,
            dst_ref=dst,
            send_sem=sems.at[0, slot],
            recv_sem=sems.at[1, slot],
            device_id=device,
            device_id_type=MESH,
        )
        copy.start()
        pending.append(copy)
        return copy

    wanted = pltpu.make_async_copy(
        send_rows_ref.at[0, :, pl.ds(pl.multiple_of(core * HALF, HALF), HALF)], send_ref, index_sems.at[0]
    )
    wanted.start()

    barrier = pltpu.get_barrier_semaphore()
    peers = [partner]
    peers += [(at_shift(k // SIDE, k % SIDE), feat) for k in range(1, N_DP)]
    peers += [(dp, z_feat(k)) for k in range(1, N_Z)]
    for peer in peers:
        pl.semaphore_signal(barrier, inc=1, device_id=peer, device_id_type=MESH)
    pl.semaphore_wait(barrier, len(peers))

    lane = pl.ds(pl.multiple_of(core * 64, 64), 64)
    swap_x = push(x_ref, feats_ref.at[lane, pl.ds(0, NODES)], swap_sems, 0, partner)
    swap_hub = push(hub_ref, feats_ref.at[lane, pl.ds(NODES, HUBS)], swap_sems, 1, partner)

    def code(row):
        power = jnp.where((row & 128) != 0, 2.0, 1.0)
        for bit in range(1, 5):
            power = power * jnp.where((row & (128 << bit)) != 0, 2.0 ** (2**bit), 1.0)
        return power * (128 + (row & 127)).astype(F32)

    cnt2 = cnt2_ref[...]
    kept = lax.broadcasted_iota(jnp.int32, (FAN2, ROWS), 0) < cnt2
    names = jnp.concatenate([jnp.where(kept, code(nbr2_ref[...]), 0.0), code(seed_ref[...]), cnt2.astype(F32)], axis=0)
    note_ref[feat, pl.ds(0, TALL), :] = jnp.concatenate(
        [dl_ref[...].astype(F32), jnp.zeros((TALL - CLASSES, ROWS), F32)], axis=0
    ).astype(BF16)
    note_ref[feat, pl.ds(TALL, 32), :] = jnp.concatenate(
        [names, jnp.zeros((32 - NAMES - 1, ROWS), F32)], axis=0
    ).astype(BF16)

    class Ring:
        def __init__(self, view, up, down, over=None):
            self.view, self.up, self.down, self.over = view, up, down, over
            self.from_below, self.from_above, self.crossed = {}, {}, []

        def send_up(self, step):
            block = self.view(1 - step)
            self.from_below[step] = push(block, block, self.up, step - 1, (dp, z_feat(1)))

        def send_down(self, step):
            block = self.view(step - 1)
            self.from_above[step] = push(block, block, self.down, step - 1, (dp, z_feat(-1)))

        def cross(self, step):
            if self.over is not None:
                block = self.view(step)
                self.crossed.append(push(block, block, self.over, len(self.crossed), partner))

        def start(self):
            self.send_up(1)
            self.send_down(1)
            self.cross(0)

        def take(self, step):
            self.from_below[step].wait_recv()
            if step < 4:
                self.send_up(step + 1)
            self.cross(-step)
            if step < 4:
                self.from_above[step].wait_recv()
                if step < 3:
                    self.send_down(step + 1)
                self.cross(step)

    notes = Ring(lambda step: note_ref.at[z_feat(step)], note_up, note_down, note_over)
    notes.start()

    feats_ref[lane, pl.ds(0, NODES)] = x_ref[...]
    feats_ref[lane, pl.ds(NODES, HUBS)] = hub_ref[...]

    def places(slots):
        mine_first = jnp.where(((slots >> 10) & 1) == core, 0, PART)
        return jnp.where(slots < N_DP * CAP, mine_first + (slots >> 11) * HALF + (slots & (HALF - 1)), slots)

    used = lax.broadcasted_iota(jnp.int32, (FAN1, N_FEAT * ROWS), 0) < cnt1_ref[...]
    place_ref[pl.ds(0, FAN1), :] = jnp.where(used, places(slots_ref[...]), ZERO_ROW)
    place_ref[pl.ds(FAN1, 1), :] = places(self_slot_ref[...])
    located = pltpu.make_async_copy(place_ref, slot_ref, index_sems.at[1])
    located.start()
    swap_x.wait_recv()
    nodes_flat = nodes_ref.reshape(NODES, WIDE)
    table_flat = table_ref.reshape(ZERO_ROW + 8, WIDE)
    rows_flat = rows_ref.reshape(QUARTER, WIDE)

    def turn(block, carry):
        at = pl.multiple_of(block * 1024, 1024)
        nodes_flat[pl.ds(at, 1024), :] = feats_ref[:, pl.ds(at, 1024)].astype(F32).T
        return carry

    lax.fori_loop(0, NODES // 1024, turn, 0)
    wanted.wait()

    far = {}
    staged = {}

    def pick(shift, half):
        to = at_shift(*shift)
        first = half * QUARTER
        unroll = 32

        def some_rows(block, carry):
            at = pl.multiple_of(block * unroll, unroll)
            got = [nodes_ref[send_ref[to, first + at + r]] for r in range(unroll)]
            for r in range(unroll):
                rows_ref[at + r] = got[r]
            return carry

        lax.fori_loop(0, QUARTER // unroll, some_rows, 0)
        slot = 2 * (shift[0] * SIDE + shift[1]) + half
        if shift == (0, 0):
            own_ref[dp, half] = rows_flat[...].astype(BF16)
            return
        stage_ref[slot] = rows_flat[...].astype(BF16)
        if (shift, half) in STAGED:
            s = STAGED.index((shift, half))
            staged[s] = push(stage_ref.at[slot], mid_ref.at[s], mid_sems, s, (at_shift(*through(shift, half)), feat))
        else:
            far[slot] = push(stage_ref.at[slot], own_ref.at[dp, half], far_sems, slot, (to, feat))

    def pass_on(s):
        shift, half = STAGED[s]
        mx, my = through(shift, half)
        slot = 2 * (shift[0] * SIDE + shift[1]) + half
        staged[s].wait_recv()
        source = at_shift(-mx, -my)
        to = at_shift(shift[0] - mx, shift[1] - my)
        far[slot] = push(mid_ref.at[s], own_ref.at[source, half], far_sems, slot, (to, feat))

    near = {}

    def arrive(shift, half):
        slot = 2 * (shift[0] * SIDE + shift[1]) + half
        source = at_shift(-shift[0], -shift[1])
        if slot in far:
            far[slot].wait_recv()
        near[slot] = push(own_ref.at[source, half], other_ref.at[source, half], near_sems, slot, partner)
        at = pl.multiple_of(source * HALF + half * QUARTER, QUARTER)
        table_flat[pl.ds(at, QUARTER), :] = own_ref[source, half].astype(F32)

    def cross(shift, half):
        slot = 2 * (shift[0] * SIDE + shift[1]) + half
        source = at_shift(-shift[0], -shift[1])
        near[slot].wait_recv()
        at = pl.multiple_of(PART + source * HALF + half * QUARTER, QUARTER)
        table_flat[pl.ds(at, QUARTER), :] = other_ref[source, half].astype(F32)

    for number, shift in enumerate(TWO):
        for half in range(2):
            pick(shift, half)
        if number in (1, 3, 5):
            notes.take((number + 1) // 2)
    for number, shift in enumerate(DIAGONAL):
        for half in range(2):
            pick(shift, half)
        if number == 0:
            notes.take(4)
        for s in range(4 * number, min(4 * number + 4, len(STAGED))):
            pass_on(s)
    for shift in NEXT:
        for half in range(2):
            pick(shift, half)
    for copy in notes.crossed:
        copy.wait_recv()

    code_ref[...] = code(feat * ROWS + lax.broadcasted_iota(jnp.int32, (ROWS, 128), 0)).astype(BF16)
    one = jnp.ones((ROWS, 128), BF16)
    none = jnp.zeros((ROWS, 128), BF16)
    both_last = (((1,), (1,)), ((), ()))
    for ref in (gnt_ref, gst_ref):
        ref[...] = jnp.zeros_like(ref)

    def one_device(f, carry):
        names_here = note_ref[f, pl.ds(TALL, 32), :].astype(F32)
        tallies, hots = [], []
        for side in range(ROWS // 128):
            total = none
            for j in range(NAMES):
                line = names_here[j : j + 1, side * 128 : side * 128 + 128].astype(BF16)
                match = jnp.where(jnp.broadcast_to(line, (ROWS, 128)) == code_ref[...], one, none)
                if j < FAN2:
                    total = total + match
                else:
                    hots.append(match)
            tallies.append(total)
        tally = jnp.concatenate(tallies, axis=1)
        hot = jnp.concatenate(hots, axis=1)
        dl = note_ref[f, pl.ds(0, TALL), :]
        dz = (dl.astype(F32) / names_here[NAMES : NAMES + 1, :]).astype(BF16)
        gnt_ref[...] += lax.dot_general(dz, tally, both_last, preferred_element_type=F32)
        gst_ref[...] += lax.dot_general(dl, hot, both_last, preferred_element_type=F32)
        return carry

    lax.fori_loop(0, N_FEAT, one_device, 0)

    def twice(value, other, left):
        top = value.astype(BF16)
        rest = (value - top.astype(F32)).astype(BF16)
        if left:
            return jnp.dot(top, other, preferred_element_type=F32) + jnp.dot(rest, other, preferred_element_type=F32)
        return jnp.dot(other, top, preferred_element_type=F32) + jnp.dot(other, rest, preferred_element_type=F32)

    def upright(w_ref):
        return jnp.concatenate([w_ref[...].astype(F32), jnp.zeros((256 - CLASSES, HIDDEN), F32)], axis=0).T.astype(BF16)

    below = jnp.zeros((256 - TALL, ROWS), F32)
    gnt = gnt_ref[...]
    gst = gst_ref[...]
    hidden = twice(jnp.concatenate([gnt, below], axis=0), upright(wn_ref), False)
    hidden += twice(jnp.concatenate([gst, below], axis=0), upright(ws_ref), False)
    dpre_ref[z] = jnp.where(h_ref[...].astype(F32).T > 0, hidden, 0.0).astype(BF16)
    rows_ring = Ring(lambda step: dpre_ref.at[lax.rem(z + step + N_Z, N_Z)], dpre_up, dpre_down)
    rows_ring.start()
    second_ref[0] = twice(gst, h_ref[...], True)
    second_ref[1] = twice(gnt, h_ref[...], True)
    second_over = push(second_ref.at[1 - core], extra_ref, over_sems, 0, partner)

    for half in range(2):
        pick((0, 0), half)
    swap_hub.wait_recv()

    def turn_hub(block, carry):
        at = pl.multiple_of(block * 1024, 1024)
        table_flat[pl.ds(2 * PART + at, 1024), :] = feats_ref[:, pl.ds(NODES + at, 1024)].astype(F32).T
        return carry

    lax.fori_loop(0, HUBS // 1024, turn_hub, 0)
    table_flat[pl.ds(ZERO_ROW, 8), :] = jnp.zeros((8, WIDE), F32)

    order = [(shift, half) for shift in [(0, 0)] + DIAGONAL + TWO + NEXT for half in range(2)]
    for number, (shift, half) in enumerate(order):
        arrive(shift, half)
        if number == 9:
            rows_ring.take(1)
        if number == 23:
            rows_ring.take(2)
    second_over.wait_recv()
    column_ref[...] = second_ref[core] + extra_ref[...]

    def piece(step):
        to = lax.rem(z + step + N_Z, N_Z)
        tall = pl.ds(pl.multiple_of(lax.div(to, 4) * (TALL // 2), 8), TALL // 2)
        return tall, pl.ds(pl.multiple_of(lax.rem(to, 4) * 128, 128), 128)

    scattered = [push(column_ref.at[piece(k)], pieces_ref.at[k], z_sems, k, (dp, z_feat(k))) for k in range(1, N_Z)]

    for shift, half in order:
        cross(shift, half)
    located.wait()

    self_flat = self_ref.reshape(ROWS, WIDE)
    sum_flat = sum_ref.reshape(ROWS, WIDE)
    unroll = 8

    def fold(step):
        of = lax.rem(z + step + N_Z, N_Z)
        base = (2 * of + core) * ROWS

        def some_sums(block, carry):
            at = pl.multiple_of(block * unroll, unroll)
            for r in range(unroll):
                got = [table_ref[slot_ref[j, base + at + r]] for j in range(PICKS)]
                rest = got[:FAN1]
                while len(rest) > 1:
                    rest = [rest[i] + rest[i + 1] if i + 1 < len(rest) else rest[i] for i in range(0, len(rest), 2)]
                self_ref[at + r] = got[FAN1]
                sum_ref[at + r] = rest[0]
            return carry

        lax.fori_loop(0, ROWS // unroll, some_sums, 0)
        here = pl.ds(pl.multiple_of(base, ROWS), ROWS)
        count = jnp.broadcast_to(cnt1_ref[:, here].astype(F32), (WIDE, ROWS)).T
        own = self_flat[...].astype(BF16)
        mean = (sum_flat[...] / count).astype(BF16)
        both = jnp.concatenate([own, mean], axis=1)
        product = jnp.dot(dpre_ref[of], both, preferred_element_type=F32)
        if step == 0:
            acc_ref[...] = product
        else:
            acc_ref[...] += product

    gathered = []
    for number, step in enumerate((0, -1, 1, -2, 2, -3, 3, -4)):
        fold(step)
        if number == 0:
            rows_ring.take(3)
            total = column_ref[piece(0)]
            for k, copy in enumerate(scattered):
                copy.wait_recv()
                total = total + pieces_ref[k + 1]
            piece_ref[...] = total
            summed = [
                push(piece_ref, columns_ref.at[k], dp_sems, k, (at_shift(k // SIDE, k % SIDE), feat))
                for k in range(1, N_DP)
            ]
        if number == 3:
            rows_ring.take(4)
            total = piece_ref[...]
            for k, copy in enumerate(summed):
                copy.wait_recv()
                total = total + columns_ref[k + 1]
            mine_tall, mine_lanes = piece(0)
            block = final_ref.at[core, mine_tall, mine_lanes]
            final_ref[core, mine_tall, mine_lanes] = total
            for k in range(1, N_Z):
                gathered.append(push(block, block, z2_sems, k, (dp, z_feat(k))))
        if number == 6:
            for copy in gathered:
                copy.wait_recv()
            second_back = push(final_ref.at[core], final_ref.at[core], over_sems, 1, partner)

    part_ref[...] = acc_ref[...].T
    first_over = [
        push(
            part_ref.at[pl.ds(pl.multiple_of(64 * (2 * i + 1 - core), 64), 64), :],
            theirs_ref.at[i],
            over_sems,
            2 + i,
            partner,
        )
        for i in range(2)
    ]
    second_back.wait_recv()
    self2_ref[...] = final_ref[0, :CLASSES, :]
    nbr2o_ref[...] = final_ref[1, :CLASSES, :]
    for i in range(2):
        first_over[i].wait_recv()
        mine_here = part_ref[pl.ds(pl.multiple_of(64 * (2 * i + core), 64), 64), :] + theirs_ref[i]
        part_ref[pl.ds(pl.multiple_of(64 * (2 * i + core), 64), 64), :] = mine_here

    def eight(to):
        return pl.ds(pl.multiple_of(lax.div(to, 8) * 128 + core * 64 + lax.rem(to, 8) * 8, 8), 8)

    spread = []
    for k in range(1, N_DP):
        to = at_shift(k // SIDE, k % SIDE)
        spread.append(push(part_ref.at[eight(to), :], got_ref.at[k], first_sems, k, (to, feat)))
    total = part_ref[eight(dp), :]
    for k, copy in enumerate(spread):
        copy.wait_recv()
        total = total + got_ref[k + 1]
    done_ref[dp] = total
    last = []
    for k in range(1, N_DP):
        to = at_shift(k // SIDE, k % SIDE)
        last.append(push(done_ref.at[dp], done_ref.at[dp], first2_sems, k, (to, feat)))
    for copy in last:
        copy.wait_recv()
    for k in range(8):
        self1_ref[pl.ds(8 * k, 8), :] = done_ref[k]
        nbr1_ref[pl.ds(8 * k, 8), :] = done_ref[8 + k]
    for copy in pending:
        copy.wait_send()


def main_step(*operands):
    vmem = pl.BlockSpec(memory_space=pltpu.VMEM)
    dma = pltpu.SemaphoreType.DMA
    return pl.pallas_call(
        main_kernel,
        out_shape=(
            jax.ShapeDtypeStruct((64, HIDDEN), F32),
            jax.ShapeDtypeStruct((64, HIDDEN), F32),
            jax.ShapeDtypeStruct((CLASSES, HIDDEN), F32),
            jax.ShapeDtypeStruct((CLASSES, HIDDEN), F32),
        ),
        in_specs=[vmem] * len(operands),
        out_specs=(vmem,) * 4,
        scratch_shapes=[
            pltpu.VMEM((WIDE, NODES + HUBS), BF16),
            pltpu.VMEM((NODES, 1, WIDE), F32),
            pltpu.VMEM((2 * N_DP, QUARTER, WIDE), BF16),
            pltpu.VMEM((len(STAGED), QUARTER, WIDE), BF16),
            pltpu.VMEM((N_DP, 2, QUARTER, WIDE), BF16),
            pltpu.VMEM((N_DP, 2, QUARTER, WIDE), BF16),
            pltpu.VMEM((ZERO_ROW + 8, 1, WIDE), F32),
            pltpu.VMEM((QUARTER, 1, WIDE), F32),
            pltpu.SMEM((N_DP, HALF), jnp.int32),
            pltpu.VMEM((PICKS, N_FEAT * ROWS), jnp.int32),
            pltpu.SMEM((PICKS, N_FEAT * ROWS), jnp.int32),
            pltpu.VMEM((ROWS, 128), BF16),
            pltpu.VMEM((N_FEAT, NOTE, ROWS), BF16),
            pltpu.VMEM((TALL, ROWS), F32),
            pltpu.VMEM((TALL, ROWS), F32),
            pltpu.VMEM((N_Z, HIDDEN, ROWS), BF16),
            pltpu.VMEM((2, TALL, HIDDEN), F32),
            pltpu.VMEM((TALL, HIDDEN), F32),
            pltpu.VMEM((TALL // 2, 128), F32),
            pltpu.VMEM((N_Z, TALL // 2, 128), F32),
            pltpu.VMEM((TALL, HIDDEN), F32),
            pltpu.VMEM((N_DP, TALL // 2, 128), F32),
            pltpu.VMEM((2, TALL, HIDDEN), F32),
            pltpu.VMEM((ROWS, 1, WIDE), F32),
            pltpu.VMEM((ROWS, 1, WIDE), F32),
            pltpu.VMEM((HIDDEN, 2 * WIDE), F32),
            pltpu.VMEM((2 * WIDE, HIDDEN), F32),
            pltpu.VMEM((2, 64, HIDDEN), F32),
            pltpu.VMEM((N_DP, 8, HIDDEN), F32),
            pltpu.VMEM((N_DP, 8, HIDDEN), F32),
            dma((2,)),
            dma((2, 2)),
            dma((2, len(STAGED))),
            dma((2, 2 * N_DP)),
            dma((2, 2 * N_DP)),
            dma((2, 4)),
            dma((2, 4)),
            dma((2, N_Z)),
            dma((2, 4)),
            dma((2, 4)),
            dma((2, 4)),
            dma((2, N_Z)),
            dma((2, N_DP)),
            dma((2, N_Z)),
            dma((2, N_DP)),
            dma((2, N_DP)),
        ],
        compiler_params=pltpu.CompilerParams(
            collective_id=1, has_side_effects=True, vmem_limit_bytes=60 * 1024 * 1024
        ),
        name="main_step",
    )(*operands)


def hand_kernel(*refs):
    sources, results, sems = refs[:4], refs[4:8], refs[8]
    copies = [pltpu.make_async_copy(src, dst, sems.at[i]) for i, (src, dst) in enumerate(zip(sources, results))]
    for copy in copies:
        copy.start()
    for copy in copies:
        copy.wait()


def hand_out(arrays):
    anywhere = pl.BlockSpec(memory_space=pl.ANY)
    return pl.pallas_call(
        hand_kernel,
        out_shape=tuple(jax.ShapeDtypeStruct(a.shape, a.dtype) for a in arrays),
        in_specs=[anywhere] * 4,
        out_specs=(anywhere,) * 4,
        scratch_shapes=[pltpu.SemaphoreType.DMA((4,))],
        compiler_params=pltpu.CompilerParams(vmem_limit_bytes=60 * 1024 * 1024),
        name="hand_out",
    )(*arrays)


def body(
    x_table,
    hub_feats,
    send_rows,
    self_slot,
    nbr1,
    cnt1,
    h_saved,
    seed_self,
    nbr2,
    cnt2,
    d_logits,
    w_self2,
    w_nbr2,
):
    sums = main_step(
        send_rows,
        self_slot[None],
        nbr1,
        x_table,
        hub_feats,
        cnt1[None],
        h_saved,
        seed_self[None],
        nbr2.T,
        cnt2[None],
        d_logits.T,
        w_self2.T,
        w_nbr2.T,
    )
    self1, nbr1_out, self2, nbr2_out = hand_out(sums)
    return (self1, nbr1_out, self2.T, nbr2_out.T)


def solution(mesh):
    placed = (
        P("feat", "dp"),
        P("feat", None),
        P("dp", None, None),
        P("dp"),
        P(None, "dp"),
        P("dp"),
        P(("dp", "feat"), None),
        P(("dp", "feat")),
        P(("dp", "feat"), None),
        P(("dp", "feat")),
        P(("dp", "feat"), None),
        P(),
        P(),
    )
    return jax.shard_map(
        body,
        mesh=mesh,
        in_specs=placed,
        out_specs=(P("feat", None), P("feat", None), P(), P()),
        check_vma=False,
    )
```

```python
import jax
import jax.numpy as jnp
from jax import lax
from jax.experimental import pallas as pl
from jax.experimental.pallas import tpu as pltpu
from jax.sharding import PartitionSpec as P

N_DP = 16
SIDE = 4
N_FEAT = 16
N_Z = 8
CAP = 2048
HALF = CAP // 2
QUARTER = HALF // 2
HUBS = 2048
NODES = 8192
ROWS = 256
GROUP = N_Z * ROWS
HIDDEN = 512
CLASSES = 172
TALL = 176
FAN1 = 10
FAN2 = 25
PICKS = 1 + FAN1
WIDE = 128
PART = N_DP * HALF
ZERO_ROW = 2 * PART + HUBS
NOTE = TALL + 32
NAMES = FAN2 + 1
MESH = pl.DeviceIdType.MESH
F32 = jnp.float32
BF16 = jnp.bfloat16
HIGHEST = lax.Precision.HIGHEST

TWO = [(2, 2), (2, 0), (0, 2), (2, 1), (2, 3), (1, 2), (3, 2)]
DIAGONAL = [(1, 1), (3, 3), (1, 3), (3, 1)]
NEXT = [(1, 0), (3, 0), (0, 1), (0, 3)]


def through(shift, half):
    one = 3 if half else 1
    dx, dy = shift
    if dx == 2:
        return (one, one if dy == 2 else 0)
    return (dx, one)


STAGED = [(shift, half) for shift in TWO for half in range(2)]


def main_kernel(
    send_rows_ref, self_slot_ref, slots_ref, x_ref, hub_ref, cnt1_ref, h_ref, seed_ref, nbr2_ref, cnt2_ref, dl_ref, ws_ref, wn_ref,
    self1_ref, nbr1_ref, self2_ref, nbr2o_ref,
    feats_ref, nodes_ref, stage_ref, mid_ref, own_ref, other_ref, table_ref, rows_ref,
    send_ref, place_ref, slot_ref, code_ref, note_ref, gnt_ref, gst_ref, dpre_ref, second_ref, extra_ref, piece_ref, pieces_ref, column_ref, columns_ref, final_ref,
    self_ref, sum_ref, acc_ref, part_ref, theirs_ref, got_ref, done_ref,
    index_sems, swap_sems, mid_sems, far_sems, near_sems, note_up, note_down, note_over,
    dpre_up, dpre_down, over_sems, z_sems, dp_sems, z2_sems, first_sems, first2_sems,
):
    dp = lax.axis_index("dp")
    feat = lax.axis_index("feat")
    core = lax.rem(feat, 2)
    z = lax.div(feat, 2)
    px = lax.div(dp, SIDE)
    py = lax.rem(dp, SIDE)
    partner = (dp, feat + 1 - 2 * core)
    pending = []

    def at_shift(dx, dy):
        return lax.rem(px + dx + SIDE, SIDE) * SIDE + lax.rem(py + dy + SIDE, SIDE)

    def z_feat(step):
        return lax.rem(z + step + N_Z, N_Z) * 2 + core

    def push(src, dst, sems, slot, device):
        copy = pltpu.make_async_remote_copy(
            src_ref=src,
            dst_ref=dst,
            send_sem=sems.at[0, slot],
            recv_sem=sems.at[1, slot],
            device_id=device,
            device_id_type=MESH,
        )
        copy.start()
        pending.append(copy)
        return copy

    wanted = pltpu.make_async_copy(
        send_rows_ref.at[0, :, pl.ds(pl.multiple_of(core * HALF, HALF), HALF)], send_ref, index_sems.at[0]
    )
    wanted.start()

    barrier = pltpu.get_barrier_semaphore()
    peers = [partner]
    peers += [(at_shift(k // SIDE, k % SIDE), feat) for k in range(1, N_DP)]
    peers += [(dp, z_feat(k)) for k in range(1, N_Z)]
    for peer in peers:
        pl.semaphore_signal(barrier, inc=1, device_id=peer, device_id_type=MESH)
    pl.semaphore_wait(barrier, len(peers))

    lane = pl.ds(pl.multiple_of(core * 64, 64), 64)
    swap_x = push(x_ref, feats_ref.at[lane, pl.ds(0, NODES)], swap_sems, 0, partner)
    swap_hub = push(hub_ref, feats_ref.at[lane, pl.ds(NODES, HUBS)], swap_sems, 1, partner)

    def code(row):
        power = jnp.where((row & 128) != 0, 2.0, 1.0)
        for bit in range(1, 5):
            power = power * jnp.where((row & (128 << bit)) != 0, 2.0 ** (2**bit), 1.0)
        return power * (128 + (row & 127)).astype(F32)

    cnt2 = cnt2_ref[...]
    kept = lax.broadcasted_iota(jnp.int32, (FAN2, ROWS), 0) < cnt2
    names = jnp.concatenate([jnp.where(kept, code(nbr2_ref[...]), 0.0), code(seed_ref[...]), cnt2.astype(F32)], axis=0)
    note_ref[feat, pl.ds(0, TALL), :] = jnp.concatenate(
        [dl_ref[...].astype(F32), jnp.zeros((TALL - CLASSES, ROWS), F32)], axis=0
    ).astype(BF16)
    note_ref[feat, pl.ds(TALL, 32), :] = jnp.concatenate(
        [names, jnp.zeros((32 - NAMES - 1, ROWS), F32)], axis=0
    ).astype(BF16)

    class Ring:
        def __init__(self, view, up, down, over=None):
            self.view, self.up, self.down, self.over = view, up, down, over
            self.from_below, self.from_above, self.crossed = {}, {}, []

        def send_up(self, step):
            block = self.view(1 - step)
            self.from_below[step] = push(block, block, self.up, step - 1, (dp, z_feat(1)))

        def send_down(self, step):
            block = self.view(step - 1)
            self.from_above[step] = push(block, block, self.down, step - 1, (dp, z_feat(-1)))

        def cross(self, step):
            if self.over is not None:
                block = self.view(step)
                self.crossed.append(push(block, block, self.over, len(self.crossed), partner))

        def start(self):
            self.send_up(1)
            self.send_down(1)
            self.cross(0)

        def take(self, step):
            self.from_below[step].wait_recv()
            if step < 4:
                self.send_up(step + 1)
            self.cross(-step)
            if step < 4:
                self.from_above[step].wait_recv()
                if step < 3:
                    self.send_down(step + 1)
                self.cross(step)

    notes = Ring(lambda step: note_ref.at[z_feat(step)], note_up, note_down, note_over)
    notes.start()

    feats_ref[lane, pl.ds(0, NODES)] = x_ref[...]
    feats_ref[lane, pl.ds(NODES, HUBS)] = hub_ref[...]

    def places(slots):
        mine_first = jnp.where(((slots >> 10) & 1) == core, 0, PART)
        return jnp.where(slots < N_DP * CAP, mine_first + (slots >> 11) * HALF + (slots & (HALF - 1)), slots)

    used = lax.broadcasted_iota(jnp.int32, (FAN1, N_FEAT * ROWS), 0) < cnt1_ref[...]
    place_ref[pl.ds(0, FAN1), :] = jnp.where(used, places(slots_ref[...]), ZERO_ROW)
    place_ref[pl.ds(FAN1, 1), :] = places(self_slot_ref[...])
    located = pltpu.make_async_copy(place_ref, slot_ref, index_sems.at[1])
    located.start()
    swap_x.wait_recv()

    def turn(block, carry):
        at = pl.multiple_of(block * 1024, 1024)
        nodes_ref[pl.ds(at, 1024), :] = feats_ref[:, pl.ds(at, 1024)].astype(F32).T
        return carry

    lax.fori_loop(0, NODES // 1024, turn, 0)
    wanted.wait()

    far = {}
    staged = {}

    def pick(shift, half):
        to = at_shift(*shift)
        first = half * QUARTER
        unroll = 32

        def some_rows(block, carry):
            at = pl.multiple_of(block * unroll, unroll)
            got = [nodes_ref[pl.ds(send_ref[to, first + at + r], 1), :] for r in range(unroll)]
            for r in range(unroll):
                rows_ref[pl.ds(at + r, 1), :] = got[r]
            return carry

        lax.fori_loop(0, QUARTER // unroll, some_rows, 0)
        slot = 2 * (shift[0] * SIDE + shift[1]) + half
        if shift == (0, 0):
            own_ref[dp, half] = rows_ref[...].astype(BF16)
            return
        stage_ref[slot] = rows_ref[...].astype(BF16)
        if (shift, half) in STAGED:
            s = STAGED.index((shift, half))
            staged[s] = push(stage_ref.at[slot], mid_ref.at[s], mid_sems, s, (at_shift(*through(shift, half)), feat))
        else:
            far[slot] = push(stage_ref.at[slot], own_ref.at[dp, half], far_sems, slot, (to, feat))

    def pass_on(s):
        shift, half = STAGED[s]
        mx, my = through(shift, half)
        slot = 2 * (shift[0] * SIDE + shift[1]) + half
        staged[s].wait_recv()
        source = at_shift(-mx, -my)
        to = at_shift(shift[0] - mx, shift[1] - my)
        far[slot] = push(mid_ref.at[s], own_ref.at[source, half], far_sems, slot, (to, feat))

    near = {}

    def arrive(shift, half):
        slot = 2 * (shift[0] * SIDE + shift[1]) + half
        source = at_shift(-shift[0], -shift[1])
        if slot in far:
            far[slot].wait_recv()
        near[slot] = push(own_ref.at[source, half], other_ref.at[source, half], near_sems, slot, partner)
        at = pl.multiple_of(source * HALF + half * QUARTER, QUARTER)
        table_ref[pl.ds(at, QUARTER), :] = own_ref[source, half].astype(F32)

    def cross(shift, half):
        slot = 2 * (shift[0] * SIDE + shift[1]) + half
        source = at_shift(-shift[0], -shift[1])
        near[slot].wait_recv()
        at = pl.multiple_of(PART + source * HALF + half * QUARTER, QUARTER)
        table_ref[pl.ds(at, QUARTER), :] = other_ref[source, half].astype(F32)

    for number, shift in enumerate(TWO):
        for half in range(2):
            pick(shift, half)
        if number in (1, 3, 5):
            notes.take((number + 1) // 2)
    for number, shift in enumerate(DIAGONAL):
        for half in range(2):
            pick(shift, half)
        if number == 0:
            notes.take(4)
        for s in range(4 * number, min(4 * number + 4, len(STAGED))):
            pass_on(s)
    for shift in NEXT:
        for half in range(2):
            pick(shift, half)
    for copy in notes.crossed:
        copy.wait_recv()

    code_ref[...] = code(feat * ROWS + lax.broadcasted_iota(jnp.int32, (ROWS, 128), 0)).astype(BF16)
    one = jnp.ones((ROWS, 128), BF16)
    none = jnp.zeros((ROWS, 128), BF16)
    both_last = (((1,), (1,)), ((), ()))
    for ref in (gnt_ref, gst_ref):
        ref[...] = jnp.zeros_like(ref)

    def one_device(f, carry):
        names_here = note_ref[f, pl.ds(TALL, 32), :].astype(F32)
        tallies, hots = [], []
        for side in range(ROWS // 128):
            total = none
            for j in range(NAMES):
                line = names_here[j : j + 1, side * 128 : side * 128 + 128].astype(BF16)
                match = jnp.where(jnp.broadcast_to(line, (ROWS, 128)) == code_ref[...], one, none)
                if j < FAN2:
                    total = total + match
                else:
                    hots.append(match)
            tallies.append(total)
        tally = jnp.concatenate(tallies, axis=1)
        hot = jnp.concatenate(hots, axis=1)
        dl = note_ref[f, pl.ds(0, TALL), :]
        dz = (dl.astype(F32) / names_here[NAMES : NAMES + 1, :]).astype(BF16)
        gnt_ref[...] += lax.dot_general(dz, tally, both_last, preferred_element_type=F32)
        gst_ref[...] += lax.dot_general(dl, hot, both_last, preferred_element_type=F32)
        return carry

    lax.fori_loop(0, N_FEAT, one_device, 0)

    def twice(value, other, left):
        top = value.astype(BF16)
        rest = (value - top.astype(F32)).astype(BF16)
        if left:
            return jnp.dot(top, other, preferred_element_type=F32) + jnp.dot(rest, other, preferred_element_type=F32)
        return jnp.dot(other, top, preferred_element_type=F32) + jnp.dot(other, rest, preferred_element_type=F32)

    def upright(w_ref):
        return jnp.concatenate([w_ref[...].astype(F32), jnp.zeros((256 - CLASSES, HIDDEN), F32)], axis=0).T.astype(BF16)

    below = jnp.zeros((256 - TALL, ROWS), F32)
    gnt = gnt_ref[...]
    gst = gst_ref[...]
    hidden = twice(jnp.concatenate([gnt, below], axis=0), upright(wn_ref), False)
    hidden += twice(jnp.concatenate([gst, below], axis=0), upright(ws_ref), False)
    dpre_ref[z] = jnp.where(h_ref[...].astype(F32).T > 0, hidden, 0.0).astype(BF16)
    rows_ring = Ring(lambda step: dpre_ref.at[lax.rem(z + step + N_Z, N_Z)], dpre_up, dpre_down)
    rows_ring.start()
    second_ref[0] = twice(gst, h_ref[...], True)
    second_ref[1] = twice(gnt, h_ref[...], True)
    second_over = push(second_ref.at[1 - core], extra_ref, over_sems, 0, partner)

    for half in range(2):
        pick((0, 0), half)
    swap_hub.wait_recv()

    def turn_hub(block, carry):
        at = pl.multiple_of(block * 1024, 1024)
        table_ref[pl.ds(2 * PART + at, 1024), :] = feats_ref[:, pl.ds(NODES + at, 1024)].astype(F32).T
        return carry

    lax.fori_loop(0, HUBS // 1024, turn_hub, 0)
    table_ref[pl.ds(ZERO_ROW, 8), :] = jnp.zeros((8, WIDE), F32)

    order = [(shift, half) for shift in [(0, 0)] + DIAGONAL + TWO + NEXT for half in range(2)]
    for number, (shift, half) in enumerate(order):
        arrive(shift, half)
        if number == 9:
            rows_ring.take(1)
        if number == 23:
            rows_ring.take(2)
    second_over.wait_recv()
    column_ref[...] = second_ref[core] + extra_ref[...]

    def piece(step):
        to = lax.rem(z + step + N_Z, N_Z)
        tall = pl.ds(pl.multiple_of(lax.div(to, 4) * (TALL // 2), 8), TALL // 2)
        return tall, pl.ds(pl.multiple_of(lax.rem(to, 4) * 128, 128), 128)

    scattered = [push(column_ref.at[piece(k)], pieces_ref.at[k], z_sems, k, (dp, z_feat(k))) for k in range(1, N_Z)]

    for shift, half in order:
        cross(shift, half)
    located.wait()

    unroll = 8

    def fold(step):
        of = lax.rem(z + step + N_Z, N_Z)
        base = (2 * of + core) * ROWS

        def some_sums(block, carry):
            at = pl.multiple_of(block * unroll, unroll)
            for r in range(unroll):
                got = [table_ref[pl.ds(slot_ref[j, base + at + r], 1), :] for j in range(PICKS)]
                rest = got[:FAN1]
                while len(rest) > 1:
                    rest = [rest[i] + rest[i + 1] if i + 1 < len(rest) else rest[i] for i in range(0, len(rest), 2)]
                self_ref[pl.ds(at + r, 1), :] = got[FAN1]
                sum_ref[pl.ds(at + r, 1), :] = rest[0]
            return carry

        lax.fori_loop(0, ROWS // unroll, some_sums, 0)
        here = pl.ds(pl.multiple_of(base, ROWS), ROWS)
        count = jnp.broadcast_to(cnt1_ref[:, here].astype(F32), (WIDE, ROWS)).T
        own = self_ref[...].astype(BF16)
        mean = (sum_ref[...] / count).astype(BF16)
        both = jnp.concatenate([own, mean], axis=1)
        product = jnp.dot(dpre_ref[of], both, preferred_element_type=F32)
        if step == 0:
            acc_ref[...] = product
        else:
            acc_ref[...] += product

    gathered = []
    for number, step in enumerate((0, -1, 1, -2, 2, -3, 3, -4)):
        fold(step)
        if number == 0:
            rows_ring.take(3)
            total = column_ref[piece(0)]
            for k, copy in enumerate(scattered):
                copy.wait_recv()
                total = total + pieces_ref[k + 1]
            piece_ref[...] = total
            summed = [
                push(piece_ref, columns_ref.at[k], dp_sems, k, (at_shift(k // SIDE, k % SIDE), feat))
                for k in range(1, N_DP)
            ]
        if number == 3:
            rows_ring.take(4)
            total = piece_ref[...]
            for k, copy in enumerate(summed):
                copy.wait_recv()
                total = total + columns_ref[k + 1]
            mine_tall, mine_lanes = piece(0)
            block = final_ref.at[core, mine_tall, mine_lanes]
            final_ref[core, mine_tall, mine_lanes] = total
            for k in range(1, N_Z):
                gathered.append(push(block, block, z2_sems, k, (dp, z_feat(k))))
        if number == 6:
            for copy in gathered:
                copy.wait_recv()
            second_back = push(final_ref.at[core], final_ref.at[core], over_sems, 1, partner)

    part_ref[...] = acc_ref[...].T
    first_over = [
        push(
            part_ref.at[pl.ds(pl.multiple_of(64 * (2 * i + 1 - core), 64), 64), :],
            theirs_ref.at[i],
            over_sems,
            2 + i,
            partner,
        )
        for i in range(2)
    ]
    second_back.wait_recv()
    self2_ref[...] = final_ref[0, :CLASSES, :]
    nbr2o_ref[...] = final_ref[1, :CLASSES, :]
    for i in range(2):
        first_over[i].wait_recv()
        mine_here = part_ref[pl.ds(pl.multiple_of(64 * (2 * i + core), 64), 64), :] + theirs_ref[i]
        part_ref[pl.ds(pl.multiple_of(64 * (2 * i + core), 64), 64), :] = mine_here

    def eight(to):
        return pl.ds(pl.multiple_of(lax.div(to, 8) * 128 + core * 64 + lax.rem(to, 8) * 8, 8), 8)

    spread = []
    for k in range(1, N_DP):
        to = at_shift(k // SIDE, k % SIDE)
        spread.append(push(part_ref.at[eight(to), :], got_ref.at[k], first_sems, k, (to, feat)))
    total = part_ref[eight(dp), :]
    for k, copy in enumerate(spread):
        copy.wait_recv()
        total = total + got_ref[k + 1]
    done_ref[dp] = total
    last = []
    for k in range(1, N_DP):
        to = at_shift(k // SIDE, k % SIDE)
        last.append(push(done_ref.at[dp], done_ref.at[dp], first2_sems, k, (to, feat)))
    for copy in last:
        copy.wait_recv()
    for k in range(8):
        self1_ref[pl.ds(8 * k, 8), :] = done_ref[k]
        nbr1_ref[pl.ds(8 * k, 8), :] = done_ref[8 + k]
    for copy in pending:
        copy.wait_send()


def main_step(*operands):
    vmem = pl.BlockSpec(memory_space=pltpu.VMEM)
    dma = pltpu.SemaphoreType.DMA
    return pl.pallas_call(
        main_kernel,
        out_shape=(
            jax.ShapeDtypeStruct((64, HIDDEN), F32),
            jax.ShapeDtypeStruct((64, HIDDEN), F32),
            jax.ShapeDtypeStruct((CLASSES, HIDDEN), F32),
            jax.ShapeDtypeStruct((CLASSES, HIDDEN), F32),
        ),
        in_specs=[vmem] * len(operands),
        out_specs=(vmem,) * 4,
        scratch_shapes=[
            pltpu.VMEM((WIDE, NODES + HUBS), BF16),
            pltpu.VMEM((NODES, WIDE), F32),
            pltpu.VMEM((2 * N_DP, QUARTER, WIDE), BF16),
            pltpu.VMEM((len(STAGED), QUARTER, WIDE), BF16),
            pltpu.VMEM((N_DP, 2, QUARTER, WIDE), BF16),
            pltpu.VMEM((N_DP, 2, QUARTER, WIDE), BF16),
            pltpu.VMEM((ZERO_ROW + 8, WIDE), F32),
            pltpu.VMEM((QUARTER, WIDE), F32),
            pltpu.SMEM((N_DP, HALF), jnp.int32),
            pltpu.VMEM((PICKS, N_FEAT * ROWS), jnp.int32),
            pltpu.SMEM((PICKS, N_FEAT * ROWS), jnp.int32),
            pltpu.VMEM((ROWS, 128), BF16),
            pltpu.VMEM((N_FEAT, NOTE, ROWS), BF16),
            pltpu.VMEM((TALL, ROWS), F32),
            pltpu.VMEM((TALL, ROWS), F32),
            pltpu.VMEM((N_Z, HIDDEN, ROWS), BF16),
            pltpu.VMEM((2, TALL, HIDDEN), F32),
            pltpu.VMEM((TALL, HIDDEN), F32),
            pltpu.VMEM((TALL // 2, 128), F32),
            pltpu.VMEM((N_Z, TALL // 2, 128), F32),
            pltpu.VMEM((TALL, HIDDEN), F32),
            pltpu.VMEM((N_DP, TALL // 2, 128), F32),
            pltpu.VMEM((2, TALL, HIDDEN), F32),
            pltpu.VMEM((ROWS, WIDE), F32),
            pltpu.VMEM((ROWS, WIDE), F32),
            pltpu.VMEM((HIDDEN, 2 * WIDE), F32),
            pltpu.VMEM((2 * WIDE, HIDDEN), F32),
            pltpu.VMEM((2, 64, HIDDEN), F32),
            pltpu.VMEM((N_DP, 8, HIDDEN), F32),
            pltpu.VMEM((N_DP, 8, HIDDEN), F32),
            dma((2,)),
            dma((2, 2)),
            dma((2, len(STAGED))),
            dma((2, 2 * N_DP)),
            dma((2, 2 * N_DP)),
            dma((2, 4)),
            dma((2, 4)),
            dma((2, N_Z)),
            dma((2, 4)),
            dma((2, 4)),
            dma((2, 4)),
            dma((2, N_Z)),
            dma((2, N_DP)),
            dma((2, N_Z)),
            dma((2, N_DP)),
            dma((2, N_DP)),
        ],
        compiler_params=pltpu.CompilerParams(
            collective_id=1, has_side_effects=True, vmem_limit_bytes=60 * 1024 * 1024
        ),
        name="main_step",
    )(*operands)


def hand_kernel(*refs):
    for source, result in zip(refs[:4], refs[4:]):
        result[...] = source[...]


def hand_out(arrays):
    vmem = pl.BlockSpec(memory_space=pltpu.VMEM)
    return pl.pallas_call(
        hand_kernel,
        out_shape=tuple(jax.ShapeDtypeStruct(a.shape, a.dtype) for a in arrays),
        in_specs=[vmem] * 4,
        out_specs=(vmem,) * 4,
        compiler_params=pltpu.CompilerParams(vmem_limit_bytes=60 * 1024 * 1024),
        name="hand_out",
    )(*arrays)


def body(
    x_table,
    hub_feats,
    send_rows,
    self_slot,
    nbr1,
    cnt1,
    h_saved,
    seed_self,
    nbr2,
    cnt2,
    d_logits,
    w_self2,
    w_nbr2,
):
    sums = main_step(
        send_rows,
        self_slot[None],
        nbr1,
        x_table,
        hub_feats,
        cnt1[None],
        h_saved,
        seed_self[None],
        nbr2.T,
        cnt2[None],
        d_logits.T,
        w_self2.T,
        w_nbr2.T,
    )
    self1, nbr1_out, self2, nbr2_out = hand_out(sums)
    return (self1, nbr1_out, self2.T, nbr2_out.T)


def solution(mesh):
    placed = (
        P("feat", "dp"),
        P("feat", None),
        P("dp", None, None),
        P("dp"),
        P(None, "dp"),
        P("dp"),
        P(("dp", "feat"), None),
        P(("dp", "feat")),
        P(("dp", "feat"), None),
        P(("dp", "feat")),
        P(("dp", "feat"), None),
        P(),
        P(),
    )
    return jax.shard_map(
        body,
        mesh=mesh,
        in_specs=placed,
        out_specs=(P("feat", None), P("feat", None), P(), P()),
        check_vma=False,
    )
```

```python
import jax
import jax.numpy as jnp
from jax import lax
from jax.experimental import pallas as pl
from jax.experimental.pallas import tpu as pltpu
from jax.sharding import PartitionSpec as P

N_DP = 16
SIDE = 4
N_FEAT = 16
N_Z = 8
CAP = 2048
HALF = CAP // 2
QUARTER = HALF // 2
HUBS = 2048
NODES = 8192
ROWS = 256
GROUP = N_Z * ROWS
HIDDEN = 512
CLASSES = 172
TALL = 176
FAN1 = 10
FAN2 = 25
PICKS = 1 + FAN1
WIDE = 128
PART = N_DP * HALF
ZERO_ROW = 2 * PART + HUBS
NOTE = TALL + 32
NAMES = FAN2 + 1
MESH = pl.DeviceIdType.MESH
F32 = jnp.float32
BF16 = jnp.bfloat16
HIGHEST = lax.Precision.HIGHEST

TWO = [(2, 2), (2, 0), (0, 2), (2, 1), (2, 3), (1, 2), (3, 2)]
DIAGONAL = [(1, 1), (3, 3), (1, 3), (3, 1)]
NEXT = [(1, 0), (3, 0), (0, 1), (0, 3)]


def main_kernel(
    send_rows_ref, self_slot_ref, slots_ref, x_ref, hub_ref, cnt1_ref, h_ref, seed_ref, nbr2_ref, cnt2_ref, dl_ref, ws_ref, wn_ref,
    self1_ref, nbr1_ref, self2_ref, nbr2o_ref,
    feats_ref, nodes_ref, stage_ref, own_ref, other_ref, table_ref, rows_ref,
    send_ref, place_ref, slot_ref, code_ref, note_ref, gnt_ref, gst_ref, dpre_ref, second_ref, extra_ref, piece_ref, pieces_ref, column_ref, columns_ref, final_ref,
    self_ref, sum_ref, acc_ref, part_ref, theirs_ref, got_ref, done_ref,
    index_sems, swap_sems, far_sems, near_sems, note_sems, note_over,
    dpre_sems, over_sems, z_sems, dp_sems, z2_sems, first_sems, first2_sems,
):
    dp = lax.axis_index("dp")
    feat = lax.axis_index("feat")
    core = lax.rem(feat, 2)
    z = lax.div(feat, 2)
    px = lax.div(dp, SIDE)
    py = lax.rem(dp, SIDE)
    partner = (dp, feat + 1 - 2 * core)
    pending = []

    def at_shift(dx, dy):
        return lax.rem(px + dx + SIDE, SIDE) * SIDE + lax.rem(py + dy + SIDE, SIDE)

    def z_feat(step):
        return lax.rem(z + step + N_Z, N_Z) * 2 + core

    def push(src, dst, sems, slot, device):
        copy = pltpu.make_async_remote_copy(
            src_ref=src,
            dst_ref=dst,
            send_sem=sems.at[0, slot],
            recv_sem=sems.at[1, slot],
            device_id=device,
            device_id_type=MESH,
        )
        copy.start()
        pending.append(copy)
        return copy

    wanted = pltpu.make_async_copy(
        send_rows_ref.at[0, :, pl.ds(pl.multiple_of(core * HALF, HALF), HALF)], send_ref, index_sems.at[0]
    )
    wanted.start()

    barrier = pltpu.get_barrier_semaphore()
    peers = [partner]
    peers += [(at_shift(k // SIDE, k % SIDE), feat) for k in range(1, N_DP)]
    peers += [(dp, z_feat(k)) for k in range(1, N_Z)]
    for peer in peers:
        pl.semaphore_signal(barrier, inc=1, device_id=peer, device_id_type=MESH)
    pl.semaphore_wait(barrier, len(peers))

    lane = pl.ds(pl.multiple_of(core * 64, 64), 64)
    swap_x = push(x_ref, feats_ref.at[lane, pl.ds(0, NODES)], swap_sems, 0, partner)
    swap_hub = push(hub_ref, feats_ref.at[lane, pl.ds(NODES, HUBS)], swap_sems, 1, partner)

    def code(row):
        power = jnp.where((row & 128) != 0, 2.0, 1.0)
        for bit in range(1, 5):
            power = power * jnp.where((row & (128 << bit)) != 0, 2.0 ** (2**bit), 1.0)
        return power * (128 + (row & 127)).astype(F32)

    cnt2 = cnt2_ref[...]
    kept = lax.broadcasted_iota(jnp.int32, (FAN2, ROWS), 0) < cnt2
    names = jnp.concatenate([jnp.where(kept, code(nbr2_ref[...]), 0.0), code(seed_ref[...]), cnt2.astype(F32)], axis=0)
    note_ref[feat, pl.ds(0, TALL), :] = jnp.concatenate(
        [dl_ref[...].astype(F32), jnp.zeros((TALL - CLASSES, ROWS), F32)], axis=0
    ).astype(BF16)
    note_ref[feat, pl.ds(TALL, 32), :] = jnp.concatenate(
        [names, jnp.zeros((32 - NAMES - 1, ROWS), F32)], axis=0
    ).astype(BF16)

    around = (1, 7, 2, 6, 3, 5, 4)
    noted = {k: push(note_ref.at[feat], note_ref.at[feat], note_sems, k, (dp, z_feat(k))) for k in around}
    crossed = [push(note_ref.at[feat], note_ref.at[feat], note_over, 0, partner)]

    feats_ref[lane, pl.ds(0, NODES)] = x_ref[...]
    feats_ref[lane, pl.ds(NODES, HUBS)] = hub_ref[...]

    def places(slots):
        mine_first = jnp.where(((slots >> 10) & 1) == core, 0, PART)
        return jnp.where(slots < N_DP * CAP, mine_first + (slots >> 11) * HALF + (slots & (HALF - 1)), slots)

    used = lax.broadcasted_iota(jnp.int32, (FAN1, N_FEAT * ROWS), 0) < cnt1_ref[...]
    place_ref[pl.ds(0, FAN1), :] = jnp.where(used, places(slots_ref[...]), ZERO_ROW)
    place_ref[pl.ds(FAN1, 1), :] = places(self_slot_ref[...])
    located = pltpu.make_async_copy(place_ref, slot_ref, index_sems.at[1])
    located.start()
    swap_x.wait_recv()

    def turn(block, carry):
        at = pl.multiple_of(block * 1024, 1024)
        nodes_ref[pl.ds(at, 1024), :] = feats_ref[:, pl.ds(at, 1024)].astype(F32).T
        return carry

    lax.fori_loop(0, NODES // 1024, turn, 0)
    wanted.wait()

    far = {}

    def pick(shift, half):
        to = at_shift(*shift)
        first = half * QUARTER
        unroll = 32

        def some_rows(block, carry):
            at = pl.multiple_of(block * unroll, unroll)
            got = [nodes_ref[pl.ds(send_ref[to, first + at + r], 1), :] for r in range(unroll)]
            for r in range(unroll):
                rows_ref[pl.ds(at + r, 1), :] = got[r]
            return carry

        lax.fori_loop(0, QUARTER // unroll, some_rows, 0)
        if shift == (0, 0):
            own_ref[dp, half] = rows_ref[...].astype(BF16)
        else:
            stage_ref[2 * (shift[0] * SIDE + shift[1]) + half] = rows_ref[...].astype(BF16)

    def send(shift, half):
        slot = 2 * (shift[0] * SIDE + shift[1]) + half
        far[slot] = push(stage_ref.at[slot], own_ref.at[dp, half], far_sems, slot, (at_shift(*shift), feat))

    near = {}

    def arrive(shift, half):
        slot = 2 * (shift[0] * SIDE + shift[1]) + half
        source = at_shift(-shift[0], -shift[1])
        if slot in far:
            far[slot].wait_recv()
        near[slot] = push(own_ref.at[source, half], other_ref.at[source, half], near_sems, slot, partner)
        at = pl.multiple_of(source * HALF + half * QUARTER, QUARTER)
        table_ref[pl.ds(at, QUARTER), :] = own_ref[source, half].astype(F32)

    def cross(shift, half):
        slot = 2 * (shift[0] * SIDE + shift[1]) + half
        source = at_shift(-shift[0], -shift[1])
        near[slot].wait_recv()
        at = pl.multiple_of(PART + source * HALF + half * QUARTER, QUARTER)
        table_ref[pl.ds(at, QUARTER), :] = other_ref[source, half].astype(F32)

    away = [(shift, half) for shift in TWO + DIAGONAL + NEXT for half in range(2)]
    for number, block in enumerate(away):
        pick(*block)
        if number < 4:
            send(*block)
        if number == 11:
            for k in around:
                noted[k].wait_recv()
                landed = note_ref.at[z_feat(-k)]
                crossed.append(push(landed, landed, note_over, k, partner))
            for earlier in away[4:12]:
                send(*earlier)
        if number > 11:
            send(*block)
    for copy in crossed:
        copy.wait_recv()

    code_ref[...] = code(feat * ROWS + lax.broadcasted_iota(jnp.int32, (ROWS, 128), 0)).astype(BF16)
    one = jnp.ones((ROWS, 128), BF16)
    none = jnp.zeros((ROWS, 128), BF16)
    both_last = (((1,), (1,)), ((), ()))
    for ref in (gnt_ref, gst_ref):
        ref[...] = jnp.zeros_like(ref)

    def one_device(f, carry):
        names_here = note_ref[f, pl.ds(TALL, 32), :].astype(F32)
        tallies, hots = [], []
        for side in range(ROWS // 128):
            total = none
            for j in range(NAMES):
                line = names_here[j : j + 1, side * 128 : side * 128 + 128].astype(BF16)
                match = jnp.where(jnp.broadcast_to(line, (ROWS, 128)) == code_ref[...], one, none)
                if j < FAN2:
                    total = total + match
                else:
                    hots.append(match)
            tallies.append(total)
        tally = jnp.concatenate(tallies, axis=1)
        hot = jnp.concatenate(hots, axis=1)
        dl = note_ref[f, pl.ds(0, TALL), :]
        dz = (dl.astype(F32) / names_here[NAMES : NAMES + 1, :]).astype(BF16)
        gnt_ref[...] += lax.dot_general(dz, tally, both_last, preferred_element_type=F32)
        gst_ref[...] += lax.dot_general(dl, hot, both_last, preferred_element_type=F32)
        return carry

    lax.fori_loop(0, N_FEAT, one_device, 0)

    def twice(value, other, left):
        top = value.astype(BF16)
        rest = (value - top.astype(F32)).astype(BF16)
        if left:
            return jnp.dot(top, other, preferred_element_type=F32) + jnp.dot(rest, other, preferred_element_type=F32)
        return jnp.dot(other, top, preferred_element_type=F32) + jnp.dot(other, rest, preferred_element_type=F32)

    def upright(w_ref):
        return jnp.concatenate([w_ref[...].astype(F32), jnp.zeros((256 - CLASSES, HIDDEN), F32)], axis=0).T.astype(BF16)

    below = jnp.zeros((256 - TALL, ROWS), F32)
    gnt = gnt_ref[...]
    gst = gst_ref[...]
    hidden = twice(jnp.concatenate([gnt, below], axis=0), upright(wn_ref), False)
    hidden += twice(jnp.concatenate([gst, below], axis=0), upright(ws_ref), False)
    dpre_ref[z] = jnp.where(h_ref[...].astype(F32).T > 0, hidden, 0.0).astype(BF16)
    second_ref[0] = twice(gst, h_ref[...], True)
    second_ref[1] = twice(gnt, h_ref[...], True)
    second_over = push(second_ref.at[1 - core], extra_ref, over_sems, 0, partner)

    for half in range(2):
        pick((0, 0), half)
    swap_hub.wait_recv()

    def turn_hub(block, carry):
        at = pl.multiple_of(block * 1024, 1024)
        table_ref[pl.ds(2 * PART + at, 1024), :] = feats_ref[:, pl.ds(NODES + at, 1024)].astype(F32).T
        return carry

    lax.fori_loop(0, HUBS // 1024, turn_hub, 0)
    table_ref[pl.ds(ZERO_ROW, 8), :] = jnp.zeros((8, WIDE), F32)

    second_over.wait_recv()
    column_ref[...] = second_ref[core] + extra_ref[...]

    def piece(step):
        to = lax.rem(z + step + N_Z, N_Z)
        tall = pl.ds(pl.multiple_of(lax.div(to, 4) * (TALL // 2), 8), TALL // 2)
        return tall, pl.ds(pl.multiple_of(lax.rem(to, 4) * 128, 128), 128)

    scattered = {k: push(column_ref.at[piece(k)], pieces_ref.at[k], z_sems, k, (dp, z_feat(k))) for k in around}

    order = [((0, 0), half) for half in range(2)] + away
    shared = {}
    for number, block in enumerate(order):
        arrive(*block)
        if number % 4 == 3 and len(shared) < len(around):
            k = around[len(shared)]
            shared[k] = push(dpre_ref.at[z], dpre_ref.at[z], dpre_sems, k, (dp, z_feat(k)))
    total = column_ref[piece(0)]
    for k in around:
        scattered[k].wait_recv()
        total = total + pieces_ref[k]
    piece_ref[0] = total
    along_x = [push(piece_ref.at[0], columns_ref.at[k], dp_sems, k, (at_shift(k, 0), feat)) for k in range(1, SIDE)]
    for block in order:
        cross(*block)
    located.wait()

    unroll = 8

    def fold(step):
        of = lax.rem(z + step + N_Z, N_Z)
        base = (2 * of + core) * ROWS

        def some_sums(block, carry):
            at = pl.multiple_of(block * unroll, unroll)
            for r in range(unroll):
                got = [table_ref[pl.ds(slot_ref[j, base + at + r], 1), :] for j in range(PICKS)]
                rest = got[:FAN1]
                while len(rest) > 1:
                    rest = [rest[i] + rest[i + 1] if i + 1 < len(rest) else rest[i] for i in range(0, len(rest), 2)]
                self_ref[pl.ds(at + r, 1), :] = got[FAN1]
                sum_ref[pl.ds(at + r, 1), :] = rest[0]
            return carry

        lax.fori_loop(0, ROWS // unroll, some_sums, 0)
        here = pl.ds(pl.multiple_of(base, ROWS), ROWS)
        count = jnp.broadcast_to(cnt1_ref[:, here].astype(F32), (WIDE, ROWS)).T
        own = self_ref[...].astype(BF16)
        mean = (sum_ref[...] / count).astype(BF16)
        both = jnp.concatenate([own, mean], axis=1)
        product = jnp.dot(dpre_ref[of], both, preferred_element_type=F32)
        if step == 0:
            acc_ref[...] = product
        else:
            acc_ref[...] += product

    gathered = []
    for number, k in enumerate((0,) + around):
        if number:
            shared[k].wait_recv()
        fold(-k)
        if number == 1:
            total = piece_ref[0]
            for i, copy in enumerate(along_x):
                copy.wait_recv()
                total = total + columns_ref[i + 1]
            piece_ref[1] = total
            along_y = [
                push(piece_ref.at[1], columns_ref.at[SIDE + i], dp_sems, SIDE + i, (at_shift(0, i), feat))
                for i in range(1, SIDE)
            ]
        if number == 3:
            total = piece_ref[1]
            for i, copy in enumerate(along_y):
                copy.wait_recv()
                total = total + columns_ref[SIDE + i + 1]
            mine_tall, mine_lanes = piece(0)
            block = final_ref.at[core, mine_tall, mine_lanes]
            final_ref[core, mine_tall, mine_lanes] = total
            for i in around:
                gathered.append(push(block, block, z2_sems, i, (dp, z_feat(i))))
        if number == 6:
            for copy in gathered:
                copy.wait_recv()
            second_back = push(final_ref.at[core], final_ref.at[core], over_sems, 1, partner)

    part_ref[...] = acc_ref[...].T
    first_over = [
        push(
            part_ref.at[pl.ds(pl.multiple_of(64 * (2 * i + 1 - core), 64), 64), :],
            theirs_ref.at[i],
            over_sems,
            2 + i,
            partner,
        )
        for i in range(2)
    ]
    second_back.wait_recv()
    self2_ref[...] = final_ref[0, :CLASSES, :]
    nbr2o_ref[...] = final_ref[1, :CLASSES, :]
    for i in range(2):
        first_over[i].wait_recv()
        mine_here = part_ref[pl.ds(pl.multiple_of(64 * (2 * i + core), 64), 64), :] + theirs_ref[i]
        part_ref[pl.ds(pl.multiple_of(64 * (2 * i + core), 64), 64), :] = mine_here

    def eight(to):
        return pl.ds(pl.multiple_of(lax.div(to, 8) * 128 + core * 64 + lax.rem(to, 8) * 8, 8), 8)

    spread = []
    for k in range(1, N_DP):
        to = at_shift(k // SIDE, k % SIDE)
        spread.append(push(part_ref.at[eight(to), :], got_ref.at[k], first_sems, k, (to, feat)))
    total = part_ref[eight(dp), :]
    for k, copy in enumerate(spread):
        copy.wait_recv()
        total = total + got_ref[k + 1]
    done_ref[dp] = jnp.concatenate([total[:, : HIDDEN // 2], total[:, HIDDEN // 2 :]], axis=0).astype(BF16)
    last = []
    for k in range(1, N_DP):
        to = at_shift(k // SIDE, k % SIDE)
        last.append(push(done_ref.at[dp], done_ref.at[dp], first2_sems, k, (to, feat)))
    for copy in last:
        copy.wait_recv()
    for k in range(N_DP):
        result = (self1_ref, nbr1_ref)[k // 8]
        eight_rows = done_ref[k].astype(F32)
        result[pl.ds(8 * (k % 8), 8), pl.ds(0, HIDDEN // 2)] = eight_rows[:8]
        result[pl.ds(8 * (k % 8), 8), pl.ds(HIDDEN // 2, HIDDEN // 2)] = eight_rows[8:]
    for copy in pending:
        copy.wait_send()


def main_step(*operands):
    vmem = pl.BlockSpec(memory_space=pltpu.VMEM)
    dma = pltpu.SemaphoreType.DMA
    return pl.pallas_call(
        main_kernel,
        out_shape=(
            jax.ShapeDtypeStruct((64, HIDDEN), F32),
            jax.ShapeDtypeStruct((64, HIDDEN), F32),
            jax.ShapeDtypeStruct((CLASSES, HIDDEN), F32),
            jax.ShapeDtypeStruct((CLASSES, HIDDEN), F32),
        ),
        in_specs=[vmem] * len(operands),
        out_specs=(vmem,) * 4,
        scratch_shapes=[
            pltpu.VMEM((WIDE, NODES + HUBS), BF16),
            pltpu.VMEM((NODES, WIDE), F32),
            pltpu.VMEM((2 * N_DP, QUARTER, WIDE), BF16),
            pltpu.VMEM((N_DP, 2, QUARTER, WIDE), BF16),
            pltpu.VMEM((N_DP, 2, QUARTER, WIDE), BF16),
            pltpu.VMEM((ZERO_ROW + 8, WIDE), F32),
            pltpu.VMEM((QUARTER, WIDE), F32),
            pltpu.SMEM((N_DP, HALF), jnp.int32),
            pltpu.VMEM((PICKS, N_FEAT * ROWS), jnp.int32),
            pltpu.SMEM((PICKS, N_FEAT * ROWS), jnp.int32),
            pltpu.VMEM((ROWS, 128), BF16),
            pltpu.VMEM((N_FEAT, NOTE, ROWS), BF16),
            pltpu.VMEM((TALL, ROWS), F32),
            pltpu.VMEM((TALL, ROWS), F32),
            pltpu.VMEM((N_Z, HIDDEN, ROWS), BF16),
            pltpu.VMEM((2, TALL, HIDDEN), F32),
            pltpu.VMEM((TALL, HIDDEN), F32),
            pltpu.VMEM((2, TALL // 2, 128), F32),
            pltpu.VMEM((N_Z, TALL // 2, 128), F32),
            pltpu.VMEM((TALL, HIDDEN), F32),
            pltpu.VMEM((2 * SIDE, TALL // 2, 128), F32),
            pltpu.VMEM((2, TALL, HIDDEN), F32),
            pltpu.VMEM((ROWS, WIDE), F32),
            pltpu.VMEM((ROWS, WIDE), F32),
            pltpu.VMEM((HIDDEN, 2 * WIDE), F32),
            pltpu.VMEM((2 * WIDE, HIDDEN), F32),
            pltpu.VMEM((2, 64, HIDDEN), F32),
            pltpu.VMEM((N_DP, 8, HIDDEN), F32),
            pltpu.VMEM((N_DP, 16, HIDDEN // 2), BF16),
            dma((2,)),
            dma((2, 2)),
            dma((2, 2 * N_DP)),
            dma((2, 2 * N_DP)),
            dma((2, N_Z)),
            dma((2, N_Z)),
            dma((2, N_Z)),
            dma((2, 4)),
            dma((2, N_Z)),
            dma((2, N_DP)),
            dma((2, N_Z)),
            dma((2, N_DP)),
            dma((2, N_DP)),
        ],
        compiler_params=pltpu.CompilerParams(
            collective_id=1, has_side_effects=True, vmem_limit_bytes=60 * 1024 * 1024
        ),
        name="main_step",
    )(*operands)


def hand_kernel(*refs):
    for source, result in zip(refs[:4], refs[4:]):
        result[...] = source[...]


def hand_out(arrays):
    vmem = pl.BlockSpec(memory_space=pltpu.VMEM)
    return pl.pallas_call(
        hand_kernel,
        out_shape=tuple(jax.ShapeDtypeStruct(a.shape, a.dtype) for a in arrays),
        in_specs=[vmem] * 4,
        out_specs=(vmem,) * 4,
        compiler_params=pltpu.CompilerParams(vmem_limit_bytes=60 * 1024 * 1024),
        name="hand_out",
    )(*arrays)


def body(
    x_table,
    hub_feats,
    send_rows,
    self_slot,
    nbr1,
    cnt1,
    h_saved,
    seed_self,
    nbr2,
    cnt2,
    d_logits,
    w_self2,
    w_nbr2,
):
    sums = main_step(
        send_rows,
        self_slot[None],
        nbr1,
        x_table,
        hub_feats,
        cnt1[None],
        h_saved,
        seed_self[None],
        nbr2.T,
        cnt2[None],
        d_logits.T,
        w_self2.T,
        w_nbr2.T,
    )
    self1, nbr1_out, self2, nbr2_out = hand_out(sums)
    return (self1, nbr1_out, self2.T, nbr2_out.T)


def solution(mesh):
    placed = (
        P("feat", "dp"),
        P("feat", None),
        P("dp", None, None),
        P("dp"),
        P(None, "dp"),
        P("dp"),
        P(("dp", "feat"), None),
        P(("dp", "feat")),
        P(("dp", "feat"), None),
        P(("dp", "feat")),
        P(("dp", "feat"), None),
        P(),
        P(),
    )
    return jax.shard_map(
        body,
        mesh=mesh,
        in_specs=placed,
        out_specs=(P("feat", None), P("feat", None), P(), P()),
        check_vma=False,
    )
```

```python
import jax
import jax.numpy as jnp
from jax import lax
from jax.experimental import pallas as pl
from jax.experimental.pallas import tpu as pltpu
from jax.sharding import PartitionSpec as P

N_DP = 16
SIDE = 4
N_FEAT = 16
N_Z = 8
CAP = 2048
HALF = CAP // 2
QUARTER = HALF // 2
HUBS = 2048
NODES = 8192
ROWS = 256
GROUP = N_Z * ROWS
HIDDEN = 512
CLASSES = 172
TALL = 176
FAN1 = 10
FAN2 = 25
PICKS = 1 + FAN1
WIDE = 128
PART = N_DP * HALF
ZERO_ROW = 2 * PART + HUBS
NOTE = TALL + 32
NAMES = FAN2 + 1
MESH = pl.DeviceIdType.MESH
F32 = jnp.float32
BF16 = jnp.bfloat16
HIGHEST = lax.Precision.HIGHEST

TWO = [(2, 2), (2, 0), (0, 2), (2, 1), (2, 3), (1, 2), (3, 2)]
DIAGONAL = [(1, 1), (3, 3), (1, 3), (3, 1)]
NEXT = [(1, 0), (3, 0), (0, 1), (0, 3)]


def through(shift, half):
    one = 3 if half else 1
    dx, dy = shift
    if dx == 2:
        return (one, one if dy == 2 else 0)
    return (dx, one)


STAGED = [(shift, half) for shift in TWO for half in range(2)]


def main_kernel(
    send_rows_ref, self_slot_ref, slots_ref, x_ref, hub_ref, cnt1_ref, h_ref, seed_ref, nbr2_ref, cnt2_ref, dl_ref, ws_ref, wn_ref,
    self1_ref, nbr1_ref, self2_ref, nbr2o_ref,
    feats_ref, nodes_ref, stage_ref, mid_ref, own_ref, other_ref, table_ref, rows_ref,
    send_ref, place_ref, slot_ref, code_ref, note_ref, gnt_ref, gst_ref, dpre_ref, second_ref, extra_ref, piece_ref, pieces_ref, column_ref, columns_ref, final_ref,
    self_ref, sum_ref, acc_ref, part_ref, theirs_ref, got_ref, done_ref,
    index_sems, swap_sems, mid_sems, far_sems, near_sems, note_up, note_down, note_over,
    dpre_up, dpre_down, over_sems, z_sems, dp_sems, z2_sems, first_sems, first2_sems,
):
    dp = lax.axis_index("dp")
    feat = lax.axis_index("feat")
    core = lax.rem(feat, 2)
    z = lax.div(feat, 2)
    px = lax.div(dp, SIDE)
    py = lax.rem(dp, SIDE)
    partner = (dp, feat + 1 - 2 * core)
    pending = []

    def at_shift(dx, dy):
        return lax.rem(px + dx + SIDE, SIDE) * SIDE + lax.rem(py + dy + SIDE, SIDE)

    def z_feat(step):
        return lax.rem(z + step + N_Z, N_Z) * 2 + core

    def push(src, dst, sems, slot, device):
        copy = pltpu.make_async_remote_copy(
            src_ref=src,
            dst_ref=dst,
            send_sem=sems.at[0, slot],
            recv_sem=sems.at[1, slot],
            device_id=device,
            device_id_type=MESH,
        )
        copy.start()
        pending.append(copy)
        return copy

    wanted = pltpu.make_async_copy(
        send_rows_ref.at[0, :, pl.ds(pl.multiple_of(core * HALF, HALF), HALF)], send_ref, index_sems.at[0]
    )
    wanted.start()

    barrier = pltpu.get_barrier_semaphore()
    peers = [partner]
    peers += [(at_shift(k // SIDE, k % SIDE), feat) for k in range(1, N_DP)]
    peers += [(dp, z_feat(k)) for k in range(1, N_Z)]
    for peer in peers:
        pl.semaphore_signal(barrier, inc=1, device_id=peer, device_id_type=MESH)
    pl.semaphore_wait(barrier, len(peers))

    lane = pl.ds(pl.multiple_of(core * 64, 64), 64)
    swap_x = push(x_ref, feats_ref.at[lane, pl.ds(0, NODES)], swap_sems, 0, partner)
    swap_hub = push(hub_ref, feats_ref.at[lane, pl.ds(NODES, HUBS)], swap_sems, 1, partner)

    def code(row):
        power = jnp.where((row & 128) != 0, 2.0, 1.0)
        for bit in range(1, 5):
            power = power * jnp.where((row & (128 << bit)) != 0, 2.0 ** (2**bit), 1.0)
        return power * (128 + (row & 127)).astype(F32)

    cnt2 = cnt2_ref[...]
    kept = lax.broadcasted_iota(jnp.int32, (FAN2, ROWS), 0) < cnt2
    names = jnp.concatenate([jnp.where(kept, code(nbr2_ref[...]), 0.0), code(seed_ref[...]), cnt2.astype(F32)], axis=0)
    note_ref[feat, pl.ds(0, TALL), :] = jnp.concatenate(
        [dl_ref[...].astype(F32), jnp.zeros((TALL - CLASSES, ROWS), F32)], axis=0
    ).astype(BF16)
    note_ref[feat, pl.ds(TALL, 32), :] = jnp.concatenate(
        [names, jnp.zeros((32 - NAMES - 1, ROWS), F32)], axis=0
    ).astype(BF16)

    around = (1, 7, 2, 6, 3, 5, 4)

    class Ring:
        def __init__(self, view, up, down, over=None):
            self.view, self.up, self.down, self.over = view, up, down, over
            self.from_below, self.from_above, self.crossed = {}, {}, []

        def send_up(self, step):
            block = self.view(1 - step)
            self.from_below[step] = push(block, block, self.up, step - 1, (dp, z_feat(1)))

        def send_down(self, step):
            block = self.view(step - 1)
            self.from_above[step] = push(block, block, self.down, step - 1, (dp, z_feat(-1)))

        def cross(self, step):
            if self.over is not None:
                block = self.view(step)
                self.crossed.append(push(block, block, self.over, len(self.crossed), partner))

        def start(self):
            self.send_up(1)
            self.send_down(1)
            self.cross(0)

        def take(self, step):
            self.from_below[step].wait_recv()
            if step < 4:
                self.send_up(step + 1)
            self.cross(-step)
            if step < 4:
                self.from_above[step].wait_recv()
                if step < 3:
                    self.send_down(step + 1)
                self.cross(step)

    notes = Ring(lambda step: note_ref.at[z_feat(step)], note_up, note_down, note_over)
    notes.start()

    feats_ref[lane, pl.ds(0, NODES)] = x_ref[...]
    feats_ref[lane, pl.ds(NODES, HUBS)] = hub_ref[...]

    def places(slots):
        mine_first = jnp.where(((slots >> 10) & 1) == core, 0, PART)
        return jnp.where(slots < N_DP * CAP, mine_first + (slots >> 11) * HALF + (slots & (HALF - 1)), slots)

    used = lax.broadcasted_iota(jnp.int32, (FAN1, N_FEAT * ROWS), 0) < cnt1_ref[...]
    place_ref[pl.ds(0, FAN1), :] = jnp.where(used, places(slots_ref[...]), ZERO_ROW)
    place_ref[pl.ds(FAN1, 1), :] = places(self_slot_ref[...])
    located = pltpu.make_async_copy(place_ref, slot_ref, index_sems.at[1])
    located.start()
    swap_x.wait_recv()

    def turn(block, carry):
        at = pl.multiple_of(block * 1024, 1024)
        nodes_ref[pl.ds(at, 1024), :] = feats_ref[:, pl.ds(at, 1024)].astype(F32).T
        return carry

    lax.fori_loop(0, NODES // 1024, turn, 0)
    wanted.wait()

    far = {}
    staged = {}

    def pick(shift, half):
        to = at_shift(*shift)
        first = half * QUARTER
        unroll = 32

        def some_rows(block, carry):
            at = pl.multiple_of(block * unroll, unroll)
            got = [nodes_ref[pl.ds(send_ref[to, first + at + r], 1), :] for r in range(unroll)]
            for r in range(unroll):
                rows_ref[pl.ds(at + r, 1), :] = got[r]
            return carry

        lax.fori_loop(0, QUARTER // unroll, some_rows, 0)
        if shift == (0, 0):
            own_ref[dp, half] = rows_ref[...].astype(BF16)
        else:
            stage_ref[2 * (shift[0] * SIDE + shift[1]) + half] = rows_ref[...].astype(BF16)

    def send(shift, half):
        slot = 2 * (shift[0] * SIDE + shift[1]) + half
        if (shift, half) in STAGED:
            s = STAGED.index((shift, half))
            staged[s] = push(stage_ref.at[slot], mid_ref.at[s], mid_sems, s, (at_shift(*through(shift, half)), feat))
        else:
            far[slot] = push(stage_ref.at[slot], own_ref.at[dp, half], far_sems, slot, (at_shift(*shift), feat))

    def pass_on(s):
        shift, half = STAGED[s]
        mx, my = through(shift, half)
        slot = 2 * (shift[0] * SIDE + shift[1]) + half
        staged[s].wait_recv()
        source = at_shift(-mx, -my)
        to = at_shift(shift[0] - mx, shift[1] - my)
        far[slot] = push(mid_ref.at[s], own_ref.at[source, half], far_sems, slot, (to, feat))

    near = {}

    def arrive(shift, half):
        slot = 2 * (shift[0] * SIDE + shift[1]) + half
        source = at_shift(-shift[0], -shift[1])
        if slot in far:
            far[slot].wait_recv()
        near[slot] = push(own_ref.at[source, half], other_ref.at[source, half], near_sems, slot, partner)
        at = pl.multiple_of(source * HALF + half * QUARTER, QUARTER)
        table_ref[pl.ds(at, QUARTER), :] = own_ref[source, half].astype(F32)

    def cross(shift, half):
        slot = 2 * (shift[0] * SIDE + shift[1]) + half
        source = at_shift(-shift[0], -shift[1])
        near[slot].wait_recv()
        at = pl.multiple_of(PART + source * HALF + half * QUARTER, QUARTER)
        table_ref[pl.ds(at, QUARTER), :] = other_ref[source, half].astype(F32)

    diagonal = [(shift, half) for shift in DIAGONAL for half in range(2)]
    nearest = [(shift, half) for half in range(2) for shift in NEXT]
    away = STAGED + diagonal + nearest
    notes.take(1)
    for number, block in enumerate(STAGED + diagonal):
        pick(*block)
        if number < len(STAGED):
            send(*block)
        if number in (5, 11, 17):
            notes.take(number // 6 + 2)
    for copy in notes.crossed:
        copy.wait_recv()

    code_ref[...] = code(feat * ROWS + lax.broadcasted_iota(jnp.int32, (ROWS, 128), 0)).astype(BF16)
    one = jnp.ones((ROWS, 128), BF16)
    none = jnp.zeros((ROWS, 128), BF16)
    both_last = (((1,), (1,)), ((), ()))
    for ref in (gnt_ref, gst_ref):
        ref[...] = jnp.zeros_like(ref)

    def one_device(f, carry):
        names_here = note_ref[f, pl.ds(TALL, 32), :].astype(F32)
        tallies, hots = [], []
        for side in range(ROWS // 128):
            total = none
            for j in range(NAMES):
                line = names_here[j : j + 1, side * 128 : side * 128 + 128].astype(BF16)
                match = jnp.where(jnp.broadcast_to(line, (ROWS, 128)) == code_ref[...], one, none)
                if j < FAN2:
                    total = total + match
                else:
                    hots.append(match)
            tallies.append(total)
        tally = jnp.concatenate(tallies, axis=1)
        hot = jnp.concatenate(hots, axis=1)
        dl = note_ref[f, pl.ds(0, TALL), :]
        dz = (dl.astype(F32) / names_here[NAMES : NAMES + 1, :]).astype(BF16)
        gnt_ref[...] += lax.dot_general(dz, tally, both_last, preferred_element_type=F32)
        gst_ref[...] += lax.dot_general(dl, hot, both_last, preferred_element_type=F32)
        return carry

    for part in range(8):
        lax.fori_loop(2 * part, 2 * part + 2, one_device, 0)
        for s in range(2 * part, min(2 * part + 2, len(STAGED))):
            pass_on(s)

    def twice(value, other, left):
        top = value.astype(BF16)
        rest = (value - top.astype(F32)).astype(BF16)
        if left:
            return jnp.dot(top, other, preferred_element_type=F32) + jnp.dot(rest, other, preferred_element_type=F32)
        return jnp.dot(other, top, preferred_element_type=F32) + jnp.dot(other, rest, preferred_element_type=F32)

    def upright(w_ref):
        return jnp.concatenate([w_ref[...].astype(F32), jnp.zeros((256 - CLASSES, HIDDEN), F32)], axis=0).T.astype(BF16)

    below = jnp.zeros((256 - TALL, ROWS), F32)
    gnt = gnt_ref[...]
    gst = gst_ref[...]
    hidden = twice(jnp.concatenate([gnt, below], axis=0), upright(wn_ref), False)
    hidden += twice(jnp.concatenate([gst, below], axis=0), upright(ws_ref), False)
    dpre_ref[z] = jnp.where(h_ref[...].astype(F32).T > 0, hidden, 0.0).astype(BF16)
    rows_ring = Ring(lambda step: dpre_ref.at[lax.rem(z + step + N_Z, N_Z)], dpre_up, dpre_down)
    rows_ring.start()
    for number, block in enumerate(nearest):
        send(*diagonal[number])
        pick(*block)
        send(*block)
    second_ref[0] = twice(gst, h_ref[...], True)
    second_ref[1] = twice(gnt, h_ref[...], True)
    second_over = push(second_ref.at[1 - core], extra_ref, over_sems, 0, partner)

    for half in range(2):
        pick((0, 0), half)
    rows_ring.take(1)
    swap_hub.wait_recv()

    def turn_hub(block, carry):
        at = pl.multiple_of(block * 1024, 1024)
        table_ref[pl.ds(2 * PART + at, 1024), :] = feats_ref[:, pl.ds(NODES + at, 1024)].astype(F32).T
        return carry

    lax.fori_loop(0, HUBS // 1024, turn_hub, 0)
    table_ref[pl.ds(ZERO_ROW, 8), :] = jnp.zeros((8, WIDE), F32)

    order = [((0, 0), half) for half in range(2)] + away
    for number, block in enumerate(order):
        arrive(*block)
        if number == 15:
            rows_ring.take(2)
    rows_ring.take(3)
    second_over.wait_recv()
    column_ref[...] = second_ref[core] + extra_ref[...]

    def piece(step):
        to = lax.rem(z + step + N_Z, N_Z)
        tall = pl.ds(pl.multiple_of(lax.div(to, 4) * (TALL // 2), 8), TALL // 2)
        return tall, pl.ds(pl.multiple_of(lax.rem(to, 4) * 128, 128), 128)

    scattered = {k: push(column_ref.at[piece(k)], pieces_ref.at[k], z_sems, k, (dp, z_feat(k))) for k in around}
    for block in order:
        cross(*block)
    located.wait()

    unroll = 8

    def fold(step):
        of = lax.rem(z + step + N_Z, N_Z)
        base = (2 * of + core) * ROWS

        def some_sums(block, carry):
            at = pl.multiple_of(block * unroll, unroll)
            for r in range(unroll):
                got = [table_ref[pl.ds(slot_ref[j, base + at + r], 1), :] for j in range(PICKS)]
                rest = got[:FAN1]
                while len(rest) > 1:
                    rest = [rest[i] + rest[i + 1] if i + 1 < len(rest) else rest[i] for i in range(0, len(rest), 2)]
                self_ref[pl.ds(at + r, 1), :] = got[FAN1]
                sum_ref[pl.ds(at + r, 1), :] = rest[0]
            return carry

        lax.fori_loop(0, ROWS // unroll, some_sums, 0)
        here = pl.ds(pl.multiple_of(base, ROWS), ROWS)
        count = jnp.broadcast_to(cnt1_ref[:, here].astype(F32), (WIDE, ROWS)).T
        own = self_ref[...].astype(BF16)
        mean = (sum_ref[...] / count).astype(BF16)
        both = jnp.concatenate([own, mean], axis=1)
        product = jnp.dot(dpre_ref[of], both, preferred_element_type=F32)
        if step == 0:
            acc_ref[...] = product
        else:
            acc_ref[...] += product

    gathered = []
    for number, step in enumerate((0, -1, 1, -2, 2, -3, 3, -4)):
        fold(step)
        if number == 1:
            rows_ring.take(4)
            total = column_ref[piece(0)]
            for k in around:
                scattered[k].wait_recv()
                total = total + pieces_ref[k]
            piece_ref[0] = total
            along_x = [push(piece_ref.at[0], columns_ref.at[k], dp_sems, k, (at_shift(k, 0), feat)) for k in range(1, SIDE)]
        if number == 2:
            total = piece_ref[0]
            for i, copy in enumerate(along_x):
                copy.wait_recv()
                total = total + columns_ref[i + 1]
            piece_ref[1] = total
            along_y = [
                push(piece_ref.at[1], columns_ref.at[SIDE + i], dp_sems, SIDE + i, (at_shift(0, i), feat))
                for i in range(1, SIDE)
            ]
        if number == 3:
            total = piece_ref[1]
            for i, copy in enumerate(along_y):
                copy.wait_recv()
                total = total + columns_ref[SIDE + i + 1]
            mine_tall, mine_lanes = piece(0)
            block = final_ref.at[core, mine_tall, mine_lanes]
            final_ref[core, mine_tall, mine_lanes] = total
            for i in around:
                gathered.append(push(block, block, z2_sems, i, (dp, z_feat(i))))
        if number == 6:
            for copy in gathered:
                copy.wait_recv()
            second_back = push(final_ref.at[core], final_ref.at[core], over_sems, 1, partner)

    part_ref[...] = acc_ref[...].T
    first_over = [
        push(
            part_ref.at[pl.ds(pl.multiple_of(64 * (2 * i + 1 - core), 64), 64), :],
            theirs_ref.at[i],
            over_sems,
            2 + i,
            partner,
        )
        for i in range(2)
    ]
    second_back.wait_recv()
    self2_ref[...] = final_ref[0, :CLASSES, :]
    nbr2o_ref[...] = final_ref[1, :CLASSES, :]
    for i in range(2):
        first_over[i].wait_recv()
        mine_here = part_ref[pl.ds(pl.multiple_of(64 * (2 * i + core), 64), 64), :] + theirs_ref[i]
        part_ref[pl.ds(pl.multiple_of(64 * (2 * i + core), 64), 64), :] = mine_here

    def eight(to):
        return pl.ds(pl.multiple_of(lax.div(to, 8) * 128 + core * 64 + lax.rem(to, 8) * 8, 8), 8)

    spread = []
    for k in range(1, N_DP):
        to = at_shift(k // SIDE, k % SIDE)
        spread.append(push(part_ref.at[eight(to), :], got_ref.at[k], first_sems, k, (to, feat)))
    total = part_ref[eight(dp), :]
    for k, copy in enumerate(spread):
        copy.wait_recv()
        total = total + got_ref[k + 1]
    done_ref[dp] = jnp.concatenate([total[:, : HIDDEN // 2], total[:, HIDDEN // 2 :]], axis=0).astype(BF16)
    last = []
    for k in range(1, N_DP):
        to = at_shift(k // SIDE, k % SIDE)
        last.append(push(done_ref.at[dp], done_ref.at[dp], first2_sems, k, (to, feat)))
    for copy in last:
        copy.wait_recv()
    for k in range(N_DP):
        result = (self1_ref, nbr1_ref)[k // 8]
        eight_rows = done_ref[k].astype(F32)
        result[pl.ds(8 * (k % 8), 8), pl.ds(0, HIDDEN // 2)] = eight_rows[:8]
        result[pl.ds(8 * (k % 8), 8), pl.ds(HIDDEN // 2, HIDDEN // 2)] = eight_rows[8:]
    for copy in pending:
        copy.wait_send()


def main_step(*operands):
    vmem = pl.BlockSpec(memory_space=pltpu.VMEM)
    dma = pltpu.SemaphoreType.DMA
    return pl.pallas_call(
        main_kernel,
        out_shape=(
            jax.ShapeDtypeStruct((64, HIDDEN), F32),
            jax.ShapeDtypeStruct((64, HIDDEN), F32),
            jax.ShapeDtypeStruct((CLASSES, HIDDEN), F32),
            jax.ShapeDtypeStruct((CLASSES, HIDDEN), F32),
        ),
        in_specs=[vmem] * len(operands),
        out_specs=(vmem,) * 4,
        scratch_shapes=[
            pltpu.VMEM((WIDE, NODES + HUBS), BF16),
            pltpu.VMEM((NODES, WIDE), F32),
            pltpu.VMEM((2 * N_DP, QUARTER, WIDE), BF16),
            pltpu.VMEM((len(STAGED), QUARTER, WIDE), BF16),
            pltpu.VMEM((N_DP, 2, QUARTER, WIDE), BF16),
            pltpu.VMEM((N_DP, 2, QUARTER, WIDE), BF16),
            pltpu.VMEM((ZERO_ROW + 8, WIDE), F32),
            pltpu.VMEM((QUARTER, WIDE), F32),
            pltpu.SMEM((N_DP, HALF), jnp.int32),
            pltpu.VMEM((PICKS, N_FEAT * ROWS), jnp.int32),
            pltpu.SMEM((PICKS, N_FEAT * ROWS), jnp.int32),
            pltpu.VMEM((ROWS, 128), BF16),
            pltpu.VMEM((N_FEAT, NOTE, ROWS), BF16),
            pltpu.VMEM((TALL, ROWS), F32),
            pltpu.VMEM((TALL, ROWS), F32),
            pltpu.VMEM((N_Z, HIDDEN, ROWS), BF16),
            pltpu.VMEM((2, TALL, HIDDEN), F32),
            pltpu.VMEM((TALL, HIDDEN), F32),
            pltpu.VMEM((2, TALL // 2, 128), F32),
            pltpu.VMEM((N_Z, TALL // 2, 128), F32),
            pltpu.VMEM((TALL, HIDDEN), F32),
            pltpu.VMEM((2 * SIDE, TALL // 2, 128), F32),
            pltpu.VMEM((2, TALL, HIDDEN), F32),
            pltpu.VMEM((ROWS, WIDE), F32),
            pltpu.VMEM((ROWS, WIDE), F32),
            pltpu.VMEM((HIDDEN, 2 * WIDE), F32),
            pltpu.VMEM((2 * WIDE, HIDDEN), F32),
            pltpu.VMEM((2, 64, HIDDEN), F32),
            pltpu.VMEM((N_DP, 8, HIDDEN), F32),
            pltpu.VMEM((N_DP, 16, HIDDEN // 2), BF16),
            dma((2,)),
            dma((2, 2)),
            dma((2, len(STAGED))),
            dma((2, 2 * N_DP)),
            dma((2, 2 * N_DP)),
            dma((2, 4)),
            dma((2, 4)),
            dma((2, N_Z)),
            dma((2, 4)),
            dma((2, 4)),
            dma((2, 4)),
            dma((2, N_Z)),
            dma((2, N_DP)),
            dma((2, N_Z)),
            dma((2, N_DP)),
            dma((2, N_DP)),
        ],
        compiler_params=pltpu.CompilerParams(
            collective_id=1, has_side_effects=True, vmem_limit_bytes=60 * 1024 * 1024
        ),
        name="main_step",
    )(*operands)


def hand_kernel(*refs):
    for source, result in zip(refs[:4], refs[4:]):
        result[...] = source[...]


def hand_out(arrays):
    vmem = pl.BlockSpec(memory_space=pltpu.VMEM)
    return pl.pallas_call(
        hand_kernel,
        out_shape=tuple(jax.ShapeDtypeStruct(a.shape, a.dtype) for a in arrays),
        in_specs=[vmem] * 4,
        out_specs=(vmem,) * 4,
        compiler_params=pltpu.CompilerParams(vmem_limit_bytes=60 * 1024 * 1024),
        name="hand_out",
    )(*arrays)


def body(
    x_table,
    hub_feats,
    send_rows,
    self_slot,
    nbr1,
    cnt1,
    h_saved,
    seed_self,
    nbr2,
    cnt2,
    d_logits,
    w_self2,
    w_nbr2,
):
    sums = main_step(
        send_rows,
        self_slot[None],
        nbr1,
        x_table,
        hub_feats,
        cnt1[None],
        h_saved,
        seed_self[None],
        nbr2.T,
        cnt2[None],
        d_logits.T,
        w_self2.T,
        w_nbr2.T,
    )
    self1, nbr1_out, self2, nbr2_out = hand_out(sums)
    return (self1, nbr1_out, self2.T, nbr2_out.T)


def solution(mesh):
    placed = (
        P("feat", "dp"),
        P("feat", None),
        P("dp", None, None),
        P("dp"),
        P(None, "dp"),
        P("dp"),
        P(("dp", "feat"), None),
        P(("dp", "feat")),
        P(("dp", "feat"), None),
        P(("dp", "feat")),
        P(("dp", "feat"), None),
        P(),
        P(),
    )
    return jax.shard_map(
        body,
        mesh=mesh,
        in_specs=placed,
        out_specs=(P("feat", None), P("feat", None), P(), P()),
        check_vma=False,
    )
```

```python
import jax
import jax.numpy as jnp
from jax import lax
from jax.experimental import pallas as pl
from jax.experimental.pallas import tpu as pltpu
from jax.sharding import PartitionSpec as P

N_DP = 16
SIDE = 4
N_FEAT = 16
N_Z = 8
CAP = 2048
HALF = CAP // 2
QUARTER = HALF // 2
HUBS = 2048
NODES = 8192
ROWS = 256
GROUP = N_Z * ROWS
HIDDEN = 512
CLASSES = 172
TALL = 176
FAN1 = 10
FAN2 = 25
PICKS = 1 + FAN1
WIDE = 128
PART = N_DP * HALF
ZERO_ROW = 2 * PART + HUBS
NOTE = TALL + 32
NAMES = FAN2 + 1
MESH = pl.DeviceIdType.MESH
F32 = jnp.float32
BF16 = jnp.bfloat16
HIGHEST = lax.Precision.HIGHEST

TWO = [(2, 2), (2, 0), (0, 2), (2, 1), (2, 3), (1, 2), (3, 2)]
DIAGONAL = [(1, 1), (3, 3), (1, 3), (3, 1)]
NEXT = [(1, 0), (3, 0), (0, 1), (0, 3)]


def through(shift, half):
    one = 3 if half else 1
    dx, dy = shift
    if dx == 2:
        return (one, one if dy == 2 else 0)
    return (dx, one)


STAGED = [(shift, half) for shift in TWO for half in range(2)]


def main_kernel(
    send_rows_ref, self_slot_ref, slots_ref, x_ref, hub_ref, cnt1_ref, h_ref, seed_ref, nbr2_ref, cnt2_ref, dl_ref, ws_ref, wn_ref,
    self1_ref, nbr1_ref, self2_ref, nbr2o_ref,
    feats_ref, nodes_ref, stage_ref, mid_ref, own_ref, other_ref, table_ref, rows_ref,
    send_ref, slot_ref, self_at_ref, code_ref, note_ref, gnt_ref, gst_ref, dpre_ref, second_ref, extra_ref, piece_ref, pieces_ref, column_ref, columns_ref, final_ref,
    self_ref, sum_ref, acc_ref, part_ref, theirs_ref, got_ref, done_ref,
    index_sems, swap_sems, mid_sems, far_sems, near_sems, note_up, note_down, note_over,
    dpre_up, dpre_down, over_sems, z_sems, dp_sems, z2_sems, first_sems, first2_sems,
):
    dp = lax.axis_index("dp")
    feat = lax.axis_index("feat")
    core = lax.rem(feat, 2)
    z = lax.div(feat, 2)
    px = lax.div(dp, SIDE)
    py = lax.rem(dp, SIDE)
    partner = (dp, feat + 1 - 2 * core)
    pending = []

    def at_shift(dx, dy):
        return lax.rem(px + dx + SIDE, SIDE) * SIDE + lax.rem(py + dy + SIDE, SIDE)

    def z_feat(step):
        return lax.rem(z + step + N_Z, N_Z) * 2 + core

    def push(src, dst, sems, slot, device):
        copy = pltpu.make_async_remote_copy(
            src_ref=src,
            dst_ref=dst,
            send_sem=sems.at[0, slot],
            recv_sem=sems.at[1, slot],
            device_id=device,
            device_id_type=MESH,
        )
        copy.start()
        pending.append(copy)
        return copy

    wanted = [
        pltpu.make_async_copy(
            send_rows_ref.at[pl.ds(pl.multiple_of(k * CAP + core * HALF, HALF), HALF)],
            send_ref.at[pl.ds(k * HALF, HALF)],
            index_sems.at[k],
        )
        for k in range(N_DP)
    ]
    located = [
        pltpu.make_async_copy(slots_ref, slot_ref, index_sems.at[N_DP]),
        pltpu.make_async_copy(self_slot_ref, self_at_ref, index_sems.at[N_DP + 1]),
    ]
    for copy in wanted + located:
        copy.start()

    barrier = pltpu.get_barrier_semaphore()
    peers = [partner]
    peers += [(at_shift(k // SIDE, k % SIDE), feat) for k in range(1, N_DP)]
    peers += [(dp, z_feat(k)) for k in range(1, N_Z)]
    for peer in peers:
        pl.semaphore_signal(barrier, inc=1, device_id=peer, device_id_type=MESH)
    pl.semaphore_wait(barrier, len(peers))

    lane = pl.ds(pl.multiple_of(core * 64, 64), 64)
    swap_x = push(x_ref, feats_ref.at[lane, pl.ds(0, NODES)], swap_sems, 0, partner)
    swap_hub = push(hub_ref, feats_ref.at[lane, pl.ds(NODES, HUBS)], swap_sems, 1, partner)

    def code(row):
        power = jnp.where((row & 128) != 0, 2.0, 1.0)
        for bit in range(1, 5):
            power = power * jnp.where((row & (128 << bit)) != 0, 2.0 ** (2**bit), 1.0)
        return power * (128 + (row & 127)).astype(F32)

    cnt2 = cnt2_ref[...]
    kept = lax.broadcasted_iota(jnp.int32, (FAN2, ROWS), 0) < cnt2
    names = jnp.concatenate([jnp.where(kept, code(nbr2_ref[...]), 0.0), code(seed_ref[...]), cnt2.astype(F32)], axis=0)
    note_ref[feat, pl.ds(0, TALL), :] = jnp.concatenate(
        [dl_ref[...].astype(F32), jnp.zeros((TALL - CLASSES, ROWS), F32)], axis=0
    ).astype(BF16)
    note_ref[feat, pl.ds(TALL, 32), :] = jnp.concatenate(
        [names, jnp.zeros((32 - NAMES - 1, ROWS), F32)], axis=0
    ).astype(BF16)

    around = (1, 7, 2, 6, 3, 5, 4)

    class Ring:
        def __init__(self, view, up, down, over=None):
            self.view, self.up, self.down, self.over = view, up, down, over
            self.from_below, self.from_above, self.crossed = {}, {}, []

        def send_up(self, step):
            block = self.view(1 - step)
            self.from_below[step] = push(block, block, self.up, step - 1, (dp, z_feat(1)))

        def send_down(self, step):
            block = self.view(step - 1)
            self.from_above[step] = push(block, block, self.down, step - 1, (dp, z_feat(-1)))

        def cross(self, step):
            if self.over is not None:
                block = self.view(step)
                self.crossed.append(push(block, block, self.over, len(self.crossed), partner))

        def start(self):
            self.send_up(1)
            self.send_down(1)
            self.cross(0)

        def take(self, step):
            self.from_below[step].wait_recv()
            if step < 4:
                self.send_up(step + 1)
            self.cross(-step)
            if step < 4:
                self.from_above[step].wait_recv()
                if step < 3:
                    self.send_down(step + 1)
                self.cross(step)

    notes = Ring(lambda step: note_ref.at[z_feat(step)], note_up, note_down, note_over)
    notes.start()

    feats_ref[lane, pl.ds(0, NODES)] = x_ref[...]
    feats_ref[lane, pl.ds(NODES, HUBS)] = hub_ref[...]
    swap_x.wait_recv()

    eye_rows = lax.broadcasted_iota(jnp.int32, (256, 256), 0)
    eye_columns = lax.broadcasted_iota(jnp.int32, (256, 256), 1)
    eye = jnp.where(eye_rows == eye_columns, 1.0, 0.0).astype(BF16)
    across = (((1,), (1,)), ((), ()))

    def turned(at):
        return lax.dot_general(eye, feats_ref[:, pl.ds(at, 256)], across, preferred_element_type=F32)

    def turn(block, carry):
        for i in range(4):
            at = pl.multiple_of(block * 1024 + i * 256, 256)
            nodes_ref[pl.ds(at, 256), :] = turned(at)
        return carry

    lax.fori_loop(0, NODES // 1024, turn, 0)
    for copy in wanted:
        copy.wait()

    far = {}
    staged = {}

    def pick(shift, half):
        to = at_shift(*shift)
        first = to * HALF + half * QUARTER
        unroll = 32

        def some_rows(block, carry):
            at = pl.multiple_of(block * unroll, unroll)
            got = [nodes_ref[pl.ds(send_ref[first + at + r], 1), :] for r in range(unroll)]
            for r in range(unroll):
                rows_ref[pl.ds(at + r, 1), :] = got[r]
            return carry

        lax.fori_loop(0, QUARTER // unroll, some_rows, 0)
        if shift == (0, 0):
            own_ref[dp, half] = rows_ref[...].astype(BF16)
        else:
            stage_ref[2 * (shift[0] * SIDE + shift[1]) + half] = rows_ref[...].astype(BF16)

    def send(shift, half):
        slot = 2 * (shift[0] * SIDE + shift[1]) + half
        if (shift, half) in STAGED:
            s = STAGED.index((shift, half))
            staged[s] = push(stage_ref.at[slot], mid_ref.at[s], mid_sems, s, (at_shift(*through(shift, half)), feat))
        else:
            far[slot] = push(stage_ref.at[slot], own_ref.at[dp, half], far_sems, slot, (at_shift(*shift), feat))

    def pass_on(s):
        shift, half = STAGED[s]
        mx, my = through(shift, half)
        slot = 2 * (shift[0] * SIDE + shift[1]) + half
        staged[s].wait_recv()
        source = at_shift(-mx, -my)
        to = at_shift(shift[0] - mx, shift[1] - my)
        far[slot] = push(mid_ref.at[s], own_ref.at[source, half], far_sems, slot, (to, feat))

    near = {}

    def arrive(shift, half):
        slot = 2 * (shift[0] * SIDE + shift[1]) + half
        source = at_shift(-shift[0], -shift[1])
        if slot in far:
            far[slot].wait_recv()
        near[slot] = push(own_ref.at[source, half], other_ref.at[source, half], near_sems, slot, partner)
        at = pl.multiple_of(source * CAP + core * HALF + half * QUARTER, QUARTER)
        table_ref[pl.ds(at, QUARTER), :] = own_ref[source, half].astype(F32)

    def cross(shift, half):
        slot = 2 * (shift[0] * SIDE + shift[1]) + half
        source = at_shift(-shift[0], -shift[1])
        near[slot].wait_recv()
        at = pl.multiple_of(source * CAP + (1 - core) * HALF + half * QUARTER, QUARTER)
        table_ref[pl.ds(at, QUARTER), :] = other_ref[source, half].astype(F32)

    diagonal = [(shift, half) for shift in DIAGONAL for half in range(2)]
    nearest = [(shift, half) for half in range(2) for shift in NEXT]
    away = STAGED + diagonal + nearest
    notes.take(1)
    for number, block in enumerate(STAGED + diagonal):
        pick(*block)
        if number < len(STAGED):
            send(*block)
        if number in (5, 11, 17):
            notes.take(number // 6 + 2)
    for copy in notes.crossed:
        copy.wait_recv()

    code_ref[...] = code(feat * ROWS + lax.broadcasted_iota(jnp.int32, (ROWS, 128), 0)).astype(BF16)
    one = jnp.ones((ROWS, 128), BF16)
    none = jnp.zeros((ROWS, 128), BF16)
    both_last = (((1,), (1,)), ((), ()))
    for ref in (gnt_ref, gst_ref):
        ref[...] = jnp.zeros_like(ref)

    def one_device(f, carry):
        names_here = note_ref[f, pl.ds(TALL, 32), :].astype(F32)
        tallies, hots = [], []
        for side in range(ROWS // 128):
            total = none
            for j in range(NAMES):
                line = names_here[j : j + 1, side * 128 : side * 128 + 128].astype(BF16)
                match = jnp.where(jnp.broadcast_to(line, (ROWS, 128)) == code_ref[...], one, none)
                if j < FAN2:
                    total = total + match
                else:
                    hots.append(match)
            tallies.append(total)
        tally = jnp.concatenate(tallies, axis=1)
        hot = jnp.concatenate(hots, axis=1)
        dl = note_ref[f, pl.ds(0, TALL), :]
        dz = (dl.astype(F32) / names_here[NAMES : NAMES + 1, :]).astype(BF16)
        gnt_ref[...] += lax.dot_general(dz, tally, both_last, preferred_element_type=F32)
        gst_ref[...] += lax.dot_general(dl, hot, both_last, preferred_element_type=F32)
        return carry

    for part in range(8):
        lax.fori_loop(2 * part, 2 * part + 2, one_device, 0)
        for s in range(2 * part, min(2 * part + 2, len(STAGED))):
            pass_on(s)

    def twice(value, other, left):
        top = value.astype(BF16)
        rest = (value - top.astype(F32)).astype(BF16)
        if left:
            return jnp.dot(top, other, preferred_element_type=F32) + jnp.dot(rest, other, preferred_element_type=F32)
        return jnp.dot(other, top, preferred_element_type=F32) + jnp.dot(other, rest, preferred_element_type=F32)

    def upright(w_ref):
        return jnp.concatenate([w_ref[...].astype(F32), jnp.zeros((256 - CLASSES, HIDDEN), F32)], axis=0).T.astype(BF16)

    below = jnp.zeros((256 - TALL, ROWS), F32)
    gnt = gnt_ref[...]
    gst = gst_ref[...]
    hidden = twice(jnp.concatenate([gnt, below], axis=0), upright(wn_ref), False)
    hidden += twice(jnp.concatenate([gst, below], axis=0), upright(ws_ref), False)
    dpre_ref[z] = jnp.where(h_ref[...].astype(F32).T > 0, hidden, 0.0).astype(BF16)
    rows_ring = Ring(lambda step: dpre_ref.at[lax.rem(z + step + N_Z, N_Z)], dpre_up, dpre_down)
    rows_ring.start()
    for number, block in enumerate(nearest):
        send(*diagonal[number])
        pick(*block)
        send(*block)
    second_ref[0] = twice(gst, h_ref[...], True)
    second_ref[1] = twice(gnt, h_ref[...], True)
    second_over = push(second_ref.at[1 - core], extra_ref, over_sems, 0, partner)

    for half in range(2):
        pick((0, 0), half)
    rows_ring.take(1)
    swap_hub.wait_recv()

    def turn_hub(block, carry):
        for i in range(4):
            at = pl.multiple_of(block * 1024 + i * 256, 256)
            table_ref[pl.ds(2 * PART + at, 256), :] = turned(NODES + at)
        return carry

    lax.fori_loop(0, HUBS // 1024, turn_hub, 0)
    table_ref[pl.ds(ZERO_ROW, 8), :] = jnp.zeros((8, WIDE), F32)

    order = [((0, 0), half) for half in range(2)] + away
    for number, block in enumerate(order):
        arrive(*block)
        if number == 15:
            rows_ring.take(2)
    rows_ring.take(3)
    second_over.wait_recv()
    column_ref[...] = second_ref[core] + extra_ref[...]

    def piece(step):
        to = lax.rem(z + step + N_Z, N_Z)
        tall = pl.ds(pl.multiple_of(lax.div(to, 4) * (TALL // 2), 8), TALL // 2)
        return tall, pl.ds(pl.multiple_of(lax.rem(to, 4) * 128, 128), 128)

    scattered = {k: push(column_ref.at[piece(k)], pieces_ref.at[k], z_sems, k, (dp, z_feat(k))) for k in around}
    for block in order:
        cross(*block)
    for copy in located:
        copy.wait()

    unroll = 8

    def fold(step):
        of = lax.rem(z + step + N_Z, N_Z)
        base = (2 * of + core) * ROWS

        def some_sums(block, carry):
            at = pl.multiple_of(block * unroll, unroll)
            first = base + at
            for r in range(unroll):
                got = [table_ref[pl.ds(slot_ref[j * N_FEAT * ROWS + first + r], 1), :] for j in range(FAN1)]
                got.append(table_ref[pl.ds(self_at_ref[first + r], 1), :])
                rest = got[:FAN1]
                while len(rest) > 1:
                    rest = [rest[i] + rest[i + 1] if i + 1 < len(rest) else rest[i] for i in range(0, len(rest), 2)]
                self_ref[pl.ds(at + r, 1), :] = got[FAN1]
                sum_ref[pl.ds(at + r, 1), :] = rest[0]
            return carry

        lax.fori_loop(0, ROWS // unroll, some_sums, 0)
        here = pl.ds(pl.multiple_of(base, ROWS), ROWS)
        count = jnp.broadcast_to(cnt1_ref[:, here].astype(F32), (WIDE, ROWS)).T
        own = self_ref[...].astype(BF16)
        mean = (sum_ref[...] / count).astype(BF16)
        both = jnp.concatenate([own, mean], axis=1)
        product = jnp.dot(dpre_ref[of], both, preferred_element_type=F32)
        if step == 0:
            acc_ref[...] = product
        else:
            acc_ref[...] += product

    gathered = []
    for number, step in enumerate((0, -1, 1, -2, 2, -3, 3, -4)):
        fold(step)
        if number == 1:
            rows_ring.take(4)
            total = column_ref[piece(0)]
            for k in around:
                scattered[k].wait_recv()
                total = total + pieces_ref[k]
            piece_ref[0] = total
            along_x = [push(piece_ref.at[0], columns_ref.at[k], dp_sems, k, (at_shift(k, 0), feat)) for k in range(1, SIDE)]
        if number == 2:
            total = piece_ref[0]
            for i, copy in enumerate(along_x):
                copy.wait_recv()
                total = total + columns_ref[i + 1]
            piece_ref[1] = total
            along_y = [
                push(piece_ref.at[1], columns_ref.at[SIDE + i], dp_sems, SIDE + i, (at_shift(0, i), feat))
                for i in range(1, SIDE)
            ]
        if number == 3:
            total = piece_ref[1]
            for i, copy in enumerate(along_y):
                copy.wait_recv()
                total = total + columns_ref[SIDE + i + 1]
            mine_tall, mine_lanes = piece(0)
            block = final_ref.at[core, mine_tall, mine_lanes]
            final_ref[core, mine_tall, mine_lanes] = total
            for i in around:
                gathered.append(push(block, block, z2_sems, i, (dp, z_feat(i))))
        if number == 6:
            for copy in gathered:
                copy.wait_recv()
            second_back = push(final_ref.at[core], final_ref.at[core], over_sems, 1, partner)

    part_ref[...] = acc_ref[...].T
    first_over = [
        push(
            part_ref.at[pl.ds(pl.multiple_of(64 * (2 * i + 1 - core), 64), 64), :],
            theirs_ref.at[i],
            over_sems,
            2 + i,
            partner,
        )
        for i in range(2)
    ]
    second_back.wait_recv()
    self2_ref[...] = final_ref[0, :CLASSES, :]
    nbr2o_ref[...] = final_ref[1, :CLASSES, :]
    for i in range(2):
        first_over[i].wait_recv()
        mine_here = part_ref[pl.ds(pl.multiple_of(64 * (2 * i + core), 64), 64), :] + theirs_ref[i]
        part_ref[pl.ds(pl.multiple_of(64 * (2 * i + core), 64), 64), :] = mine_here

    def eight(to):
        return pl.ds(pl.multiple_of(lax.div(to, 8) * 128 + core * 64 + lax.rem(to, 8) * 8, 8), 8)

    spread = []
    for k in range(1, N_DP):
        to = at_shift(k // SIDE, k % SIDE)
        spread.append(push(part_ref.at[eight(to), :], got_ref.at[k], first_sems, k, (to, feat)))
    total = part_ref[eight(dp), :]
    for k, copy in enumerate(spread):
        copy.wait_recv()
        total = total + got_ref[k + 1]
    done_ref[dp] = jnp.concatenate([total[:, : HIDDEN // 2], total[:, HIDDEN // 2 :]], axis=0).astype(BF16)
    last = []
    for k in range(1, N_DP):
        to = at_shift(k // SIDE, k % SIDE)
        last.append(push(done_ref.at[dp], done_ref.at[dp], first2_sems, k, (to, feat)))
    for copy in last:
        copy.wait_recv()
    for k in range(N_DP):
        result = (self1_ref, nbr1_ref)[k // 8]
        eight_rows = done_ref[k].astype(F32)
        result[pl.ds(8 * (k % 8), 8), pl.ds(0, HIDDEN // 2)] = eight_rows[:8]
        result[pl.ds(8 * (k % 8), 8), pl.ds(HIDDEN // 2, HIDDEN // 2)] = eight_rows[8:]
    for copy in pending:
        copy.wait_send()


def main_step(*operands):
    vmem = pl.BlockSpec(memory_space=pltpu.VMEM)
    dma = pltpu.SemaphoreType.DMA
    return pl.pallas_call(
        main_kernel,
        out_shape=(
            jax.ShapeDtypeStruct((64, HIDDEN), F32),
            jax.ShapeDtypeStruct((64, HIDDEN), F32),
            jax.ShapeDtypeStruct((CLASSES, HIDDEN), F32),
            jax.ShapeDtypeStruct((CLASSES, HIDDEN), F32),
        ),
        in_specs=[pl.BlockSpec(memory_space=pl.ANY)] * 3 + [vmem] * (len(operands) - 3),
        out_specs=(vmem,) * 4,
        scratch_shapes=[
            pltpu.VMEM((WIDE, NODES + HUBS), BF16),
            pltpu.VMEM((NODES, WIDE), F32),
            pltpu.VMEM((2 * N_DP, QUARTER, WIDE), BF16),
            pltpu.VMEM((len(STAGED), QUARTER, WIDE), BF16),
            pltpu.VMEM((N_DP, 2, QUARTER, WIDE), BF16),
            pltpu.VMEM((N_DP, 2, QUARTER, WIDE), BF16),
            pltpu.VMEM((ZERO_ROW + 8, WIDE), F32),
            pltpu.VMEM((QUARTER, WIDE), F32),
            pltpu.SMEM((N_DP * HALF,), jnp.int32),
            pltpu.SMEM((FAN1 * N_FEAT * ROWS,), jnp.int32),
            pltpu.SMEM((N_FEAT * ROWS,), jnp.int32),
            pltpu.VMEM((ROWS, 128), BF16),
            pltpu.VMEM((N_FEAT, NOTE, ROWS), BF16),
            pltpu.VMEM((TALL, ROWS), F32),
            pltpu.VMEM((TALL, ROWS), F32),
            pltpu.VMEM((N_Z, HIDDEN, ROWS), BF16),
            pltpu.VMEM((2, TALL, HIDDEN), F32),
            pltpu.VMEM((TALL, HIDDEN), F32),
            pltpu.VMEM((2, TALL // 2, 128), F32),
            pltpu.VMEM((N_Z, TALL // 2, 128), F32),
            pltpu.VMEM((TALL, HIDDEN), F32),
            pltpu.VMEM((2 * SIDE, TALL // 2, 128), F32),
            pltpu.VMEM((2, TALL, HIDDEN), F32),
            pltpu.VMEM((ROWS, WIDE), F32),
            pltpu.VMEM((ROWS, WIDE), F32),
            pltpu.VMEM((HIDDEN, 2 * WIDE), F32),
            pltpu.VMEM((2 * WIDE, HIDDEN), F32),
            pltpu.VMEM((2, 64, HIDDEN), F32),
            pltpu.VMEM((N_DP, 8, HIDDEN), F32),
            pltpu.VMEM((N_DP, 16, HIDDEN // 2), BF16),
            dma((N_DP + 2,)),
            dma((2, 2)),
            dma((2, len(STAGED))),
            dma((2, 2 * N_DP)),
            dma((2, 2 * N_DP)),
            dma((2, 4)),
            dma((2, 4)),
            dma((2, N_Z)),
            dma((2, 4)),
            dma((2, 4)),
            dma((2, 4)),
            dma((2, N_Z)),
            dma((2, N_DP)),
            dma((2, N_Z)),
            dma((2, N_DP)),
            dma((2, N_DP)),
        ],
        compiler_params=pltpu.CompilerParams(
            collective_id=1, has_side_effects=True, vmem_limit_bytes=60 * 1024 * 1024
        ),
        name="main_step",
    )(*operands)


def hand_kernel(*refs):
    for source, result in zip(refs[:4], refs[4:]):
        result[...] = source[...]


def hand_out(arrays):
    vmem = pl.BlockSpec(memory_space=pltpu.VMEM)
    return pl.pallas_call(
        hand_kernel,
        out_shape=tuple(jax.ShapeDtypeStruct(a.shape, a.dtype) for a in arrays),
        in_specs=[vmem] * 4,
        out_specs=(vmem,) * 4,
        compiler_params=pltpu.CompilerParams(vmem_limit_bytes=60 * 1024 * 1024),
        name="hand_out",
    )(*arrays)


def body(
    x_table,
    hub_feats,
    send_rows,
    self_slot,
    nbr1,
    cnt1,
    h_saved,
    seed_self,
    nbr2,
    cnt2,
    d_logits,
    w_self2,
    w_nbr2,
):
    read = lax.iota(jnp.int32, FAN1)[:, None] < cnt1[None]
    sums = main_step(
        send_rows.reshape(-1),
        self_slot,
        jnp.where(read, nbr1, ZERO_ROW).reshape(-1),
        x_table,
        hub_feats,
        cnt1[None],
        h_saved,
        seed_self[None],
        nbr2.T,
        cnt2[None],
        d_logits.T,
        w_self2.T,
        w_nbr2.T,
    )
    self1, nbr1_out, self2, nbr2_out = hand_out(sums)
    return (self1, nbr1_out, self2.T, nbr2_out.T)


def solution(mesh):
    placed = (
        P("feat", "dp"),
        P("feat", None),
        P("dp", None, None),
        P("dp"),
        P(None, "dp"),
        P("dp"),
        P(("dp", "feat"), None),
        P(("dp", "feat")),
        P(("dp", "feat"), None),
        P(("dp", "feat")),
        P(("dp", "feat"), None),
        P(),
        P(),
    )
    return jax.shard_map(
        body,
        mesh=mesh,
        in_specs=placed,
        out_specs=(P("feat", None), P("feat", None), P(), P()),
        check_vma=False,
    )
```

```python
import jax
import jax.numpy as jnp
from jax import lax
from jax.experimental import pallas as pl
from jax.experimental.pallas import tpu as pltpu
from jax.sharding import PartitionSpec as P

N_DP = 16
SIDE = 4
N_FEAT = 16
N_Z = 8
CAP = 2048
HALF = CAP // 2
QUARTER = HALF // 2
HUBS = 2048
NODES = 8192
ROWS = 256
GROUP = N_Z * ROWS
HIDDEN = 512
CLASSES = 172
TALL = 176
FAN1 = 10
FAN2 = 25
PICKS = 1 + FAN1
WIDE = 128
PART = N_DP * HALF
ZERO_ROW = 2 * PART + HUBS
NOTE = TALL + 32
NAMES = FAN2 + 1
MESH = pl.DeviceIdType.MESH
F32 = jnp.float32
BF16 = jnp.bfloat16
HIGHEST = lax.Precision.HIGHEST

TWO = [(2, 2), (2, 0), (0, 2), (2, 1), (2, 3), (1, 2), (3, 2)]
DIAGONAL = [(1, 1), (3, 3), (1, 3), (3, 1)]
NEXT = [(1, 0), (3, 0), (0, 1), (0, 3)]


def through(shift, half):
    one = 3 if half else 1
    dx, dy = shift
    if dx == 2:
        return (one, one if dy == 2 else 0)
    return (dx, one)


STAGED = [(shift, half) for shift in TWO for half in range(2)]


def main_kernel(
    send_rows_ref, self_slot_ref, slots_ref, x_ref, hub_ref, cnt1_ref, h_ref, seed_ref, nbr2_ref, cnt2_ref, dl_ref, ws_ref, wn_ref,
    self1_ref, nbr1_ref, self2_ref, nbr2o_ref,
    feats_ref, nodes_ref, stage_ref, mid_ref, own_ref, other_ref, table_ref, rows_ref,
    send_ref, slot_ref, self_at_ref, code_ref, tally_ref, hot_ref, mean_ref, note_ref, gnt_ref, gst_ref, dpre_ref, second_ref, extra_ref, piece_ref, pieces_ref, column_ref, columns_ref, final_ref,
    self_ref, sum_ref, both_ref, acc_ref, part_ref, theirs_ref, got_ref, done_ref,
    index_sems, swap_sems, mid_sems, far_sems, near_sems, note_up, note_down, note_over,
    dpre_up, dpre_down, over_sems, z_sems, dp_sems, z2_sems, first_sems, first2_sems,
):
    dp = lax.axis_index("dp")
    feat = lax.axis_index("feat")
    core = lax.rem(feat, 2)
    z = lax.div(feat, 2)
    px = lax.div(dp, SIDE)
    py = lax.rem(dp, SIDE)
    partner = (dp, feat + 1 - 2 * core)
    pending = []

    def at_shift(dx, dy):
        return lax.rem(px + dx + SIDE, SIDE) * SIDE + lax.rem(py + dy + SIDE, SIDE)

    def z_feat(step):
        return lax.rem(z + step + N_Z, N_Z) * 2 + core

    def push(src, dst, sems, slot, device):
        copy = pltpu.make_async_remote_copy(
            src_ref=src,
            dst_ref=dst,
            send_sem=sems.at[0, slot],
            recv_sem=sems.at[1, slot],
            device_id=device,
            device_id_type=MESH,
        )
        copy.start()
        pending.append(copy)
        return copy

    wanted = [
        pltpu.make_async_copy(
            send_rows_ref.at[pl.ds(pl.multiple_of(k * CAP + core * HALF, HALF), HALF)],
            send_ref.at[pl.ds(k * HALF, HALF)],
            index_sems.at[k],
        )
        for k in range(N_DP)
    ]
    located = [
        pltpu.make_async_copy(slots_ref, slot_ref, index_sems.at[N_DP]),
        pltpu.make_async_copy(self_slot_ref, self_at_ref, index_sems.at[N_DP + 1]),
    ]
    for copy in wanted + located:
        copy.start()

    barrier = pltpu.get_barrier_semaphore()
    peers = [partner]
    peers += [(at_shift(k // SIDE, k % SIDE), feat) for k in range(1, N_DP)]
    peers += [(dp, z_feat(k)) for k in range(1, N_Z)]
    for peer in peers:
        pl.semaphore_signal(barrier, inc=1, device_id=peer, device_id_type=MESH)
    pl.semaphore_wait(barrier, len(peers))

    lane = pl.ds(pl.multiple_of(core * 64, 64), 64)
    swap_x = push(x_ref, feats_ref.at[lane, pl.ds(0, NODES)], swap_sems, 0, partner)
    swap_hub = push(hub_ref, feats_ref.at[lane, pl.ds(NODES, HUBS)], swap_sems, 1, partner)

    def code(row):
        power = jnp.where((row & 128) != 0, 2.0, 1.0)
        for bit in range(1, 5):
            power = power * jnp.where((row & (128 << bit)) != 0, 2.0 ** (2**bit), 1.0)
        return power * (128 + (row & 127)).astype(F32)

    cnt2 = cnt2_ref[...]
    kept = lax.broadcasted_iota(jnp.int32, (FAN2, ROWS), 0) < cnt2
    names = jnp.concatenate([jnp.where(kept, code(nbr2_ref[...]), 0.0), code(seed_ref[...]), cnt2.astype(F32)], axis=0)
    note_ref[feat, pl.ds(0, TALL), :] = jnp.concatenate(
        [dl_ref[...].astype(F32), jnp.zeros((TALL - CLASSES, ROWS), F32)], axis=0
    ).astype(BF16)
    note_ref[feat, pl.ds(TALL, 32), :] = jnp.concatenate(
        [names, jnp.zeros((32 - NAMES - 1, ROWS), F32)], axis=0
    ).astype(BF16)

    around = (1, 7, 2, 6, 3, 5, 4)

    class Ring:
        def __init__(self, view, up, down, over=None):
            self.view, self.up, self.down, self.over = view, up, down, over
            self.from_below, self.from_above, self.crossed = {}, {}, []

        def send_up(self, step):
            block = self.view(1 - step)
            self.from_below[step] = push(block, block, self.up, step - 1, (dp, z_feat(1)))

        def send_down(self, step):
            block = self.view(step - 1)
            self.from_above[step] = push(block, block, self.down, step - 1, (dp, z_feat(-1)))

        def cross(self, step):
            if self.over is not None:
                block = self.view(step)
                self.crossed.append(push(block, block, self.over, len(self.crossed), partner))

        def start(self):
            self.send_up(1)
            self.send_down(1)
            self.cross(0)

        def take(self, step):
            self.from_below[step].wait_recv()
            if step < 4:
                self.send_up(step + 1)
            self.cross(-step)
            if step < 4:
                self.from_above[step].wait_recv()
                if step < 3:
                    self.send_down(step + 1)
                self.cross(step)

    notes = Ring(lambda step: note_ref.at[z_feat(step)], note_up, note_down, note_over)
    notes.start()

    feats_ref[lane, pl.ds(0, NODES)] = x_ref[...]
    feats_ref[lane, pl.ds(NODES, HUBS)] = hub_ref[...]
    swap_x.wait_recv()

    eye_rows = lax.broadcasted_iota(jnp.int32, (256, 256), 0)
    eye_columns = lax.broadcasted_iota(jnp.int32, (256, 256), 1)
    eye = jnp.where(eye_rows == eye_columns, 1.0, 0.0).astype(BF16)
    across = (((1,), (1,)), ((), ()))

    def turned(at):
        return lax.dot_general(eye, feats_ref[:, pl.ds(at, 256)], across, preferred_element_type=F32)

    def turn(block, carry):
        for i in range(4):
            at = pl.multiple_of(block * 1024 + i * 256, 256)
            nodes_ref[pl.ds(at, 256), :] = turned(at)
        return carry

    lax.fori_loop(0, NODES // 1024, turn, 0)
    for copy in wanted:
        copy.wait()

    far = {}
    staged = {}

    def pick(shift, half):
        to = at_shift(*shift)
        first = to * HALF + half * QUARTER
        unroll = 64

        def some_rows(block, carry):
            at = pl.multiple_of(block * unroll, unroll)
            got = [nodes_ref[pl.ds(send_ref[first + at + r], 1), :] for r in range(unroll)]
            for r in range(unroll):
                rows_ref[pl.ds(at + r, 1), :] = got[r]
            return carry

        lax.fori_loop(0, QUARTER // unroll, some_rows, 0)
        if shift == (0, 0):
            own_ref[dp, half] = rows_ref[...].astype(BF16)
        else:
            stage_ref[2 * (shift[0] * SIDE + shift[1]) + half] = rows_ref[...].astype(BF16)

    def send(shift, half):
        slot = 2 * (shift[0] * SIDE + shift[1]) + half
        if (shift, half) in STAGED:
            s = STAGED.index((shift, half))
            staged[s] = push(stage_ref.at[slot], mid_ref.at[s], mid_sems, s, (at_shift(*through(shift, half)), feat))
        else:
            far[slot] = push(stage_ref.at[slot], own_ref.at[dp, half], far_sems, slot, (at_shift(*shift), feat))

    def pass_on(s):
        shift, half = STAGED[s]
        mx, my = through(shift, half)
        slot = 2 * (shift[0] * SIDE + shift[1]) + half
        staged[s].wait_recv()
        source = at_shift(-mx, -my)
        to = at_shift(shift[0] - mx, shift[1] - my)
        far[slot] = push(mid_ref.at[s], own_ref.at[source, half], far_sems, slot, (to, feat))

    near = {}

    def widen(ref, source, half, at):
        def some(block, carry):
            inner = pl.multiple_of(block * 128, 128)
            table_ref[pl.ds(pl.multiple_of(at + inner, 128), 128), :] = ref[source, half, pl.ds(inner, 128), :].astype(F32)
            return carry

        lax.fori_loop(0, QUARTER // 128, some, 0)

    def arrive(shift, half):
        slot = 2 * (shift[0] * SIDE + shift[1]) + half
        source = at_shift(-shift[0], -shift[1])
        if slot in far:
            far[slot].wait_recv()
        near[slot] = push(own_ref.at[source, half], other_ref.at[source, half], near_sems, slot, partner)
        at = pl.multiple_of(source * CAP + core * HALF + half * QUARTER, QUARTER)
        widen(own_ref, source, half, at)

    def cross(shift, half):
        slot = 2 * (shift[0] * SIDE + shift[1]) + half
        source = at_shift(-shift[0], -shift[1])
        near[slot].wait_recv()
        at = pl.multiple_of(source * CAP + (1 - core) * HALF + half * QUARTER, QUARTER)
        widen(other_ref, source, half, at)

    diagonal = [(shift, half) for shift in DIAGONAL for half in range(2)]
    nearest = [(shift, half) for half in range(2) for shift in NEXT]
    away = STAGED + diagonal + nearest
    notes.take(1)
    for number, block in enumerate(STAGED + diagonal):
        pick(*block)
        send(*block)
        if number in (5, 11, 17):
            notes.take(number // 6 + 2)
    for number, block in enumerate(nearest):
        for s in range(2 * number, min(2 * number + 2, len(STAGED))):
            pass_on(s)
        pick(*block)
        send(*block)
    for half in range(2):
        pick((0, 0), half)
    for copy in notes.crossed:
        copy.wait_recv()

    code_ref[...] = code(feat * ROWS + lax.broadcasted_iota(jnp.int32, (ROWS, 128), 0)).astype(BF16)
    one = jnp.ones((ROWS, 128), BF16)
    none = jnp.zeros((ROWS, 128), BF16)
    both_last = (((1,), (1,)), ((), ()))
    for ref in (gnt_ref, gst_ref):
        ref[...] = jnp.zeros_like(ref)

    def one_device(f, carry):
        names_here = note_ref[f, pl.ds(TALL, 32), :].astype(F32)
        tallies, hots = [], []
        for side in range(ROWS // 128):
            total = none
            for j in range(NAMES):
                line = names_here[j : j + 1, side * 128 : side * 128 + 128].astype(BF16)
                match = jnp.where(jnp.broadcast_to(line, (ROWS, 128)) == code_ref[...], one, none)
                if j < FAN2:
                    total = total + match
                else:
                    hots.append(match)
            tallies.append(total)
        tally_ref[f] = jnp.concatenate(tallies, axis=1)
        hot_ref[f] = jnp.concatenate(hots, axis=1)
        dl = note_ref[f, pl.ds(0, TALL), :]
        mean_ref[f] = (dl.astype(F32) / names_here[NAMES : NAMES + 1, :]).astype(BF16)
        return carry

    def four_devices(block, carry):
        nbr = gnt_ref[...]
        own = gst_ref[...]
        for i in range(4):
            f = 4 * block + i
            nbr += lax.dot_general(mean_ref[f], tally_ref[f], both_last, preferred_element_type=F32)
            own += lax.dot_general(
                note_ref[f, pl.ds(0, TALL), :], hot_ref[f], both_last, preferred_element_type=F32
            )
        gnt_ref[...] = nbr
        gst_ref[...] = own
        return carry

    lax.fori_loop(0, N_FEAT, one_device, 0)
    lax.fori_loop(0, N_FEAT // 4, four_devices, 0)

    def twice(value, other, left):
        top = value.astype(BF16)
        rest = (value - top.astype(F32)).astype(BF16)
        if left:
            return jnp.dot(top, other, preferred_element_type=F32) + jnp.dot(rest, other, preferred_element_type=F32)
        return jnp.dot(other, top, preferred_element_type=F32) + jnp.dot(other, rest, preferred_element_type=F32)

    def upright(w_ref):
        return jnp.concatenate([w_ref[...].astype(F32), jnp.zeros((256 - CLASSES, HIDDEN), F32)], axis=0).T.astype(BF16)

    below = jnp.zeros((256 - TALL, ROWS), F32)
    gnt = gnt_ref[...]
    gst = gst_ref[...]
    hidden = twice(jnp.concatenate([gnt, below], axis=0), upright(wn_ref), False)
    hidden += twice(jnp.concatenate([gst, below], axis=0), upright(ws_ref), False)
    dpre_ref[z] = jnp.where(h_ref[...].astype(F32).T > 0, hidden, 0.0).astype(BF16)
    rows_ring = Ring(lambda step: dpre_ref.at[lax.rem(z + step + N_Z, N_Z)], dpre_up, dpre_down)
    rows_ring.start()
    second_ref[0] = twice(gst, h_ref[...], True)
    second_ref[1] = twice(gnt, h_ref[...], True)
    second_over = push(second_ref.at[1 - core], extra_ref, over_sems, 0, partner)

    swap_hub.wait_recv()

    def turn_hub(block, carry):
        for i in range(4):
            at = pl.multiple_of(block * 1024 + i * 256, 256)
            table_ref[pl.ds(2 * PART + at, 256), :] = turned(NODES + at)
        return carry

    lax.fori_loop(0, HUBS // 1024, turn_hub, 0)
    table_ref[pl.ds(ZERO_ROW, 8), :] = jnp.zeros((8, WIDE), F32)

    order = [((0, 0), half) for half in range(2)] + away
    for number, block in enumerate(order):
        arrive(*block)
        if number == 15:
            rows_ring.take(1)
    rows_ring.take(2)
    second_over.wait_recv()
    column_ref[...] = second_ref[core] + extra_ref[...]

    def piece(step):
        to = lax.rem(z + step + N_Z, N_Z)
        tall = pl.ds(pl.multiple_of(lax.div(to, 4) * (TALL // 2), 8), TALL // 2)
        return tall, pl.ds(pl.multiple_of(lax.rem(to, 4) * 128, 128), 128)

    scattered = {k: push(column_ref.at[piece(k)], pieces_ref.at[k], z_sems, k, (dp, z_feat(k))) for k in around}
    for block in order:
        cross(*block)
    for copy in located:
        copy.wait()

    unroll = 16

    def fold(step):
        of = lax.rem(z + step + N_Z, N_Z)
        base = (2 * of + core) * ROWS

        def some_sums(block, carry):
            at = pl.multiple_of(block * unroll, unroll)
            first = base + at
            for r in range(unroll):
                got = [table_ref[pl.ds(slot_ref[j * N_FEAT * ROWS + first + r], 1), :] for j in range(FAN1)]
                got.append(table_ref[pl.ds(self_at_ref[first + r], 1), :])
                rest = got[:FAN1]
                while len(rest) > 1:
                    rest = [rest[i] + rest[i + 1] if i + 1 < len(rest) else rest[i] for i in range(0, len(rest), 2)]
                self_ref[pl.ds(at + r, 1), :] = got[FAN1]
                sum_ref[pl.ds(at + r, 1), :] = rest[0]
            return carry

        lax.fori_loop(0, ROWS // unroll, some_sums, 0)
        here = pl.ds(pl.multiple_of(base, ROWS), ROWS)
        count = jnp.broadcast_to(cnt1_ref[:, here].astype(F32), (WIDE, ROWS)).T
        both_ref[of, :, pl.ds(0, WIDE)] = self_ref[...].astype(BF16)
        both_ref[of, :, pl.ds(WIDE, WIDE)] = (sum_ref[...] / count).astype(BF16)

    gathered = []
    for number, step in enumerate((0, -1, 1, -2, 2, -3, 3, -4)):
        fold(step)
        if number == 0:
            rows_ring.take(3)
        if number == 1:
            total = column_ref[piece(0)]
            for k in around:
                scattered[k].wait_recv()
                total = total + pieces_ref[k]
            piece_ref[0] = total
            along_x = [push(piece_ref.at[0], columns_ref.at[k], dp_sems, k, (at_shift(k, 0), feat)) for k in range(1, SIDE)]
        if number == 2:
            total = piece_ref[0]
            for i, copy in enumerate(along_x):
                copy.wait_recv()
                total = total + columns_ref[i + 1]
            piece_ref[1] = total
            rows_ring.take(4)
            along_y = [
                push(piece_ref.at[1], columns_ref.at[SIDE + i], dp_sems, SIDE + i, (at_shift(0, i), feat))
                for i in range(1, SIDE)
            ]
        if number == 3:
            total = piece_ref[1]
            for i, copy in enumerate(along_y):
                copy.wait_recv()
                total = total + columns_ref[SIDE + i + 1]
            mine_tall, mine_lanes = piece(0)
            block = final_ref.at[core, mine_tall, mine_lanes]
            final_ref[core, mine_tall, mine_lanes] = total
            for i in around:
                gathered.append(push(block, block, z2_sems, i, (dp, z_feat(i))))
        if number == 6:
            for copy in gathered:
                copy.wait_recv()
            second_back = push(final_ref.at[core], final_ref.at[core], over_sems, 1, partner)

    def two_devices(block, carry):
        total = jnp.dot(dpre_ref[2 * block], both_ref[2 * block], preferred_element_type=F32)
        total += jnp.dot(dpre_ref[2 * block + 1], both_ref[2 * block + 1], preferred_element_type=F32)
        acc_ref[...] += total
        return carry

    acc_ref[...] = jnp.zeros_like(acc_ref)
    lax.fori_loop(0, N_Z // 2, two_devices, 0)
    part_ref[...] = acc_ref[...].T
    first_over = [
        push(
            part_ref.at[pl.ds(pl.multiple_of(64 * (2 * i + 1 - core), 64), 64), :],
            theirs_ref.at[i],
            over_sems,
            2 + i,
            partner,
        )
        for i in range(2)
    ]
    second_back.wait_recv()
    self2_ref[...] = final_ref[0, :CLASSES, :]
    nbr2o_ref[...] = final_ref[1, :CLASSES, :]
    for i in range(2):
        first_over[i].wait_recv()
        mine_here = part_ref[pl.ds(pl.multiple_of(64 * (2 * i + core), 64), 64), :] + theirs_ref[i]
        part_ref[pl.ds(pl.multiple_of(64 * (2 * i + core), 64), 64), :] = mine_here

    def eight(to):
        return pl.ds(pl.multiple_of(lax.div(to, 8) * 128 + core * 64 + lax.rem(to, 8) * 8, 8), 8)

    spread = []
    for k in range(1, N_DP):
        to = at_shift(k // SIDE, k % SIDE)
        spread.append(push(part_ref.at[eight(to), :], got_ref.at[k], first_sems, k, (to, feat)))
    total = part_ref[eight(dp), :]
    for k, copy in enumerate(spread):
        copy.wait_recv()
        total = total + got_ref[k + 1]
    done_ref[dp] = jnp.concatenate([total[:, : HIDDEN // 2], total[:, HIDDEN // 2 :]], axis=0).astype(BF16)
    last = []
    for k in range(1, N_DP):
        to = at_shift(k // SIDE, k % SIDE)
        last.append(push(done_ref.at[dp], done_ref.at[dp], first2_sems, k, (to, feat)))
    for copy in last:
        copy.wait_recv()
    for k in range(N_DP):
        result = (self1_ref, nbr1_ref)[k // 8]
        eight_rows = done_ref[k].astype(F32)
        result[pl.ds(8 * (k % 8), 8), pl.ds(0, HIDDEN // 2)] = eight_rows[:8]
        result[pl.ds(8 * (k % 8), 8), pl.ds(HIDDEN // 2, HIDDEN // 2)] = eight_rows[8:]
    for copy in pending:
        copy.wait_send()


def main_step(*operands):
    vmem = pl.BlockSpec(memory_space=pltpu.VMEM)
    dma = pltpu.SemaphoreType.DMA
    return pl.pallas_call(
        main_kernel,
        out_shape=(
            jax.ShapeDtypeStruct((64, HIDDEN), F32),
            jax.ShapeDtypeStruct((64, HIDDEN), F32),
            jax.ShapeDtypeStruct((CLASSES, HIDDEN), F32),
            jax.ShapeDtypeStruct((CLASSES, HIDDEN), F32),
        ),
        in_specs=[pl.BlockSpec(memory_space=pl.ANY)] * 3 + [vmem] * (len(operands) - 3),
        out_specs=(vmem,) * 4,
        scratch_shapes=[
            pltpu.VMEM((WIDE, NODES + HUBS), BF16),
            pltpu.VMEM((NODES, WIDE), F32),
            pltpu.VMEM((2 * N_DP, QUARTER, WIDE), BF16),
            pltpu.VMEM((len(STAGED), QUARTER, WIDE), BF16),
            pltpu.VMEM((N_DP, 2, QUARTER, WIDE), BF16),
            pltpu.VMEM((N_DP, 2, QUARTER, WIDE), BF16),
            pltpu.VMEM((ZERO_ROW + 8, WIDE), F32),
            pltpu.VMEM((QUARTER, WIDE), F32),
            pltpu.SMEM((N_DP * HALF,), jnp.int32),
            pltpu.SMEM((FAN1 * N_FEAT * ROWS,), jnp.int32),
            pltpu.SMEM((N_FEAT * ROWS,), jnp.int32),
            pltpu.VMEM((ROWS, 128), BF16),
            pltpu.VMEM((N_FEAT, ROWS, ROWS), BF16),
            pltpu.VMEM((N_FEAT, ROWS, ROWS), BF16),
            pltpu.VMEM((N_FEAT, TALL, ROWS), BF16),
            pltpu.VMEM((N_FEAT, NOTE, ROWS), BF16),
            pltpu.VMEM((TALL, ROWS), F32),
            pltpu.VMEM((TALL, ROWS), F32),
            pltpu.VMEM((N_Z, HIDDEN, ROWS), BF16),
            pltpu.VMEM((2, TALL, HIDDEN), F32),
            pltpu.VMEM((TALL, HIDDEN), F32),
            pltpu.VMEM((2, TALL // 2, 128), F32),
            pltpu.VMEM((N_Z, TALL // 2, 128), F32),
            pltpu.VMEM((TALL, HIDDEN), F32),
            pltpu.VMEM((2 * SIDE, TALL // 2, 128), F32),
            pltpu.VMEM((2, TALL, HIDDEN), F32),
            pltpu.VMEM((ROWS, WIDE), F32),
            pltpu.VMEM((ROWS, WIDE), F32),
            pltpu.VMEM((N_Z, ROWS, 2 * WIDE), BF16),
            pltpu.VMEM((HIDDEN, 2 * WIDE), F32),
            pltpu.VMEM((2 * WIDE, HIDDEN), F32),
            pltpu.VMEM((2, 64, HIDDEN), F32),
            pltpu.VMEM((N_DP, 8, HIDDEN), F32),
            pltpu.VMEM((N_DP, 16, HIDDEN // 2), BF16),
            dma((N_DP + 2,)),
            dma((2, 2)),
            dma((2, len(STAGED))),
            dma((2, 2 * N_DP)),
            dma((2, 2 * N_DP)),
            dma((2, 4)),
            dma((2, 4)),
            dma((2, N_Z)),
            dma((2, 4)),
            dma((2, 4)),
            dma((2, 4)),
            dma((2, N_Z)),
            dma((2, N_DP)),
            dma((2, N_Z)),
            dma((2, N_DP)),
            dma((2, N_DP)),
        ],
        compiler_params=pltpu.CompilerParams(
            collective_id=1, has_side_effects=True, vmem_limit_bytes=60 * 1024 * 1024
        ),
        name="main_step",
    )(*operands)


def hand_kernel(*refs):
    for source, result in zip(refs[:4], refs[4:]):
        result[...] = source[...]


def hand_out(arrays):
    vmem = pl.BlockSpec(memory_space=pltpu.VMEM)
    return pl.pallas_call(
        hand_kernel,
        out_shape=tuple(jax.ShapeDtypeStruct(a.shape, a.dtype) for a in arrays),
        in_specs=[vmem] * 4,
        out_specs=(vmem,) * 4,
        compiler_params=pltpu.CompilerParams(vmem_limit_bytes=60 * 1024 * 1024),
        name="hand_out",
    )(*arrays)


def body(
    x_table,
    hub_feats,
    send_rows,
    self_slot,
    nbr1,
    cnt1,
    h_saved,
    seed_self,
    nbr2,
    cnt2,
    d_logits,
    w_self2,
    w_nbr2,
):
    read = lax.iota(jnp.int32, FAN1)[:, None] < cnt1[None]
    sums = main_step(
        send_rows.reshape(-1),
        self_slot,
        jnp.where(read, nbr1, ZERO_ROW).reshape(-1),
        x_table,
        hub_feats,
        cnt1[None],
        h_saved,
        seed_self[None],
        nbr2.T,
        cnt2[None],
        d_logits.T,
        w_self2.T,
        w_nbr2.T,
    )
    self1, nbr1_out, self2, nbr2_out = hand_out(sums)
    return (self1, nbr1_out, self2.T, nbr2_out.T)


def solution(mesh):
    placed = (
        P("feat", "dp"),
        P("feat", None),
        P("dp", None, None),
        P("dp"),
        P(None, "dp"),
        P("dp"),
        P(("dp", "feat"), None),
        P(("dp", "feat")),
        P(("dp", "feat"), None),
        P(("dp", "feat")),
        P(("dp", "feat"), None),
        P(),
        P(),
    )
    return jax.shard_map(
        body,
        mesh=mesh,
        in_specs=placed,
        out_specs=(P("feat", None), P("feat", None), P(), P()),
        check_vma=False,
    )
```

```python
import jax
import jax.numpy as jnp
from jax import lax
from jax.experimental import pallas as pl
from jax.experimental.pallas import tpu as pltpu
from jax.sharding import PartitionSpec as P

N_DP = 16
SIDE = 4
N_FEAT = 16
N_Z = 8
CAP = 2048
HALF = CAP // 2
QUARTER = HALF // 2
HUBS = 2048
NODES = 8192
ROWS = 256
GROUP = N_Z * ROWS
HIDDEN = 512
CLASSES = 172
TALL = 176
FAN1 = 10
FAN2 = 25
PICKS = 1 + FAN1
WIDE = 128
PART = N_DP * HALF
ZERO_ROW = 2 * PART + HUBS
NOTE = TALL + 32
NAMES = FAN2 + 1
MESH = pl.DeviceIdType.MESH
F32 = jnp.float32
BF16 = jnp.bfloat16
HIGHEST = lax.Precision.HIGHEST

TWO = [(2, 2), (2, 0), (0, 2), (2, 1), (2, 3), (1, 2), (3, 2)]
DIAGONAL = [(1, 1), (3, 3), (1, 3), (3, 1)]
NEXT = [(1, 0), (3, 0), (0, 1), (0, 3)]


def through(shift, half):
    one = 3 if half else 1
    dx, dy = shift
    if dx == 2:
        return (one, one if dy == 2 else 0)
    return (dx, one)


STAGED = [(shift, half) for shift in TWO for half in range(2)]


def main_kernel(
    send_rows_ref, self_slot_ref, slots_ref, x_ref, hub_ref, cnt1_ref, h_ref, seed_ref, nbr2_ref, cnt2_ref, dl_ref, ws_ref, wn_ref,
    self1_ref, nbr1_ref, self2_ref, nbr2o_ref,
    feats_ref, nodes_ref, stage_ref, mid_ref, own_ref, other_ref, table_ref, rows_ref,
    send_ref, slot_ref, self_at_ref, code_ref, tally_ref, hot_ref, mean_ref, note_ref, gnt_ref, gst_ref, dpre_ref, second_ref, extra_ref, piece_ref, pieces_ref, column_ref, columns_ref, final_ref,
    self_ref, sum_ref, both_ref, acc_ref, part_ref, theirs_ref, got_ref, done_ref,
    index_sems, swap_sems, mid_sems, far_sems, near_sems, note_up, note_down, note_over,
    dpre_up, dpre_down, over_sems, z_sems, dp_sems, z2_sems, first_sems, first2_sems,
):
    dp = lax.axis_index("dp")
    feat = lax.axis_index("feat")
    core = lax.rem(feat, 2)
    z = lax.div(feat, 2)
    px = lax.div(dp, SIDE)
    py = lax.rem(dp, SIDE)
    partner = (dp, feat + 1 - 2 * core)
    pending = []

    def at_shift(dx, dy):
        return lax.rem(px + dx + SIDE, SIDE) * SIDE + lax.rem(py + dy + SIDE, SIDE)

    def z_feat(step):
        return lax.rem(z + step + N_Z, N_Z) * 2 + core

    def push(src, dst, sems, slot, device):
        copy = pltpu.make_async_remote_copy(
            src_ref=src,
            dst_ref=dst,
            send_sem=sems.at[0, slot],
            recv_sem=sems.at[1, slot],
            device_id=device,
            device_id_type=MESH,
        )
        copy.start()
        pending.append(copy)
        return copy

    wanted = [
        pltpu.make_async_copy(
            send_rows_ref.at[pl.ds(pl.multiple_of(k * CAP + core * HALF, HALF), HALF)],
            send_ref.at[pl.ds(k * HALF, HALF)],
            index_sems.at[k],
        )
        for k in range(N_DP)
    ]
    located = [
        pltpu.make_async_copy(slots_ref, slot_ref, index_sems.at[N_DP]),
        pltpu.make_async_copy(self_slot_ref, self_at_ref, index_sems.at[N_DP + 1]),
    ]
    for copy in wanted + located:
        copy.start()

    barrier = pltpu.get_barrier_semaphore()
    peers = [partner]
    peers += [(at_shift(k // SIDE, k % SIDE), feat) for k in range(1, N_DP)]
    peers += [(dp, z_feat(k)) for k in range(1, N_Z)]
    for peer in peers:
        pl.semaphore_signal(barrier, inc=1, device_id=peer, device_id_type=MESH)
    pl.semaphore_wait(barrier, len(peers))

    lane = pl.ds(pl.multiple_of(core * 64, 64), 64)
    swap_x = push(x_ref, feats_ref.at[lane, pl.ds(0, NODES)], swap_sems, 0, partner)
    swap_hub = push(hub_ref, feats_ref.at[lane, pl.ds(NODES, HUBS)], swap_sems, 1, partner)

    def code(row):
        power = jnp.where((row & 128) != 0, 2.0, 1.0)
        for bit in range(1, 5):
            power = power * jnp.where((row & (128 << bit)) != 0, 2.0 ** (2**bit), 1.0)
        return power * (128 + (row & 127)).astype(F32)

    cnt2 = cnt2_ref[...]
    kept = lax.broadcasted_iota(jnp.int32, (FAN2, ROWS), 0) < cnt2
    names = jnp.concatenate([jnp.where(kept, code(nbr2_ref[...]), 0.0), code(seed_ref[...]), cnt2.astype(F32)], axis=0)
    note_ref[feat, pl.ds(0, TALL), :] = jnp.concatenate(
        [dl_ref[...].astype(F32), jnp.zeros((TALL - CLASSES, ROWS), F32)], axis=0
    ).astype(BF16)
    note_ref[feat, pl.ds(TALL, 32), :] = jnp.concatenate(
        [names, jnp.zeros((32 - NAMES - 1, ROWS), F32)], axis=0
    ).astype(BF16)

    around = (1, 7, 2, 6, 3, 5, 4)

    class Ring:
        def __init__(self, view, up, down, over=None):
            self.view, self.up, self.down, self.over = view, up, down, over
            self.from_below, self.from_above, self.crossed = {}, {}, []

        def send_up(self, step):
            block = self.view(1 - step)
            self.from_below[step] = push(block, block, self.up, step - 1, (dp, z_feat(1)))

        def send_down(self, step):
            block = self.view(step - 1)
            self.from_above[step] = push(block, block, self.down, step - 1, (dp, z_feat(-1)))

        def cross(self, step):
            if self.over is not None:
                block = self.view(step)
                self.crossed.append(push(block, block, self.over, len(self.crossed), partner))

        def start(self):
            self.send_up(1)
            self.send_down(1)
            self.cross(0)

        def take(self, step):
            self.from_below[step].wait_recv()
            if step < 4:
                self.send_up(step + 1)
            self.cross(-step)
            if step < 4:
                self.from_above[step].wait_recv()
                if step < 3:
                    self.send_down(step + 1)
                self.cross(step)

    notes = Ring(lambda step: note_ref.at[z_feat(step)], note_up, note_down, note_over)
    notes.start()

    feats_ref[lane, pl.ds(0, NODES)] = x_ref[...]
    feats_ref[lane, pl.ds(NODES, HUBS)] = hub_ref[...]
    swap_x.wait_recv()

    eye_rows = lax.broadcasted_iota(jnp.int32, (256, 256), 0)
    eye_columns = lax.broadcasted_iota(jnp.int32, (256, 256), 1)
    eye = jnp.where(eye_rows == eye_columns, 1.0, 0.0).astype(BF16)
    across = (((1,), (1,)), ((), ()))

    def turned(at):
        return lax.dot_general(eye, feats_ref[:, pl.ds(at, 256)], across, preferred_element_type=F32)

    def turn(block, carry):
        for i in range(4):
            at = pl.multiple_of(block * 1024 + i * 256, 256)
            nodes_ref[pl.ds(at, 256), :] = turned(at)
        return carry

    lax.fori_loop(0, NODES // 1024, turn, 0)
    for copy in wanted:
        copy.wait()

    far = {}
    staged = {}

    def pick(shift, half):
        to = at_shift(*shift)
        first = to * HALF + half * QUARTER
        unroll = 64

        def some_rows(block, carry):
            at = pl.multiple_of(block * unroll, unroll)
            got = [nodes_ref[pl.ds(send_ref[first + at + r], 1), :] for r in range(unroll)]
            for r in range(unroll):
                rows_ref[pl.ds(at + r, 1), :] = got[r]
            return carry

        lax.fori_loop(0, QUARTER // unroll, some_rows, 0)
        if shift == (0, 0):
            own_ref[dp, half] = rows_ref[...].astype(BF16)
        else:
            stage_ref[2 * (shift[0] * SIDE + shift[1]) + half] = rows_ref[...].astype(BF16)

    def send(shift, half):
        slot = 2 * (shift[0] * SIDE + shift[1]) + half
        if (shift, half) in STAGED:
            s = STAGED.index((shift, half))
            staged[s] = push(stage_ref.at[slot], mid_ref.at[s], mid_sems, s, (at_shift(*through(shift, half)), feat))
        else:
            far[slot] = push(stage_ref.at[slot], own_ref.at[dp, half], far_sems, slot, (at_shift(*shift), feat))

    def pass_on(s):
        shift, half = STAGED[s]
        mx, my = through(shift, half)
        slot = 2 * (shift[0] * SIDE + shift[1]) + half
        staged[s].wait_recv()
        source = at_shift(-mx, -my)
        to = at_shift(shift[0] - mx, shift[1] - my)
        far[slot] = push(mid_ref.at[s], own_ref.at[source, half], far_sems, slot, (to, feat))

    near = {}

    def widen(ref, source, half, at):
        def some(block, carry):
            inner = pl.multiple_of(block * 128, 128)
            table_ref[pl.ds(pl.multiple_of(at + inner, 128), 128), :] = ref[source, half, pl.ds(inner, 128), :].astype(F32)
            return carry

        lax.fori_loop(0, QUARTER // 128, some, 0)

    def arrive(shift, half):
        slot = 2 * (shift[0] * SIDE + shift[1]) + half
        source = at_shift(-shift[0], -shift[1])
        if slot in far:
            far[slot].wait_recv()
        near[slot] = push(own_ref.at[source, half], other_ref.at[source, half], near_sems, slot, partner)
        at = pl.multiple_of(source * CAP + core * HALF + half * QUARTER, QUARTER)
        widen(own_ref, source, half, at)

    def cross(shift, half):
        slot = 2 * (shift[0] * SIDE + shift[1]) + half
        source = at_shift(-shift[0], -shift[1])
        near[slot].wait_recv()
        at = pl.multiple_of(source * CAP + (1 - core) * HALF + half * QUARTER, QUARTER)
        widen(other_ref, source, half, at)

    diagonal = [(shift, half) for shift in DIAGONAL for half in range(2)]
    nearest = [(shift, half) for half in range(2) for shift in NEXT]
    away = STAGED + diagonal + nearest
    notes.take(1)
    for number, block in enumerate(STAGED + diagonal):
        pick(*block)
        if number in (4, 9, 14):
            notes.take(number // 5 + 2)
        if number == 14:
            for earlier in STAGED:
                send(*earlier)
    for copy in notes.crossed:
        copy.wait_recv()

    code_ref[...] = code(feat * ROWS + lax.broadcasted_iota(jnp.int32, (ROWS, 128), 0)).astype(BF16)
    one = jnp.ones((ROWS, 128), BF16)
    none = jnp.zeros((ROWS, 128), BF16)
    both_last = (((1,), (1,)), ((), ()))
    for ref in (gnt_ref, gst_ref):
        ref[...] = jnp.zeros_like(ref)

    def one_device(f, carry):
        names_here = note_ref[f, pl.ds(TALL, 32), :].astype(F32)
        tallies, hots = [], []
        for side in range(ROWS // 128):
            total = none
            for j in range(NAMES):
                line = names_here[j : j + 1, side * 128 : side * 128 + 128].astype(BF16)
                match = jnp.where(jnp.broadcast_to(line, (ROWS, 128)) == code_ref[...], one, none)
                if j < FAN2:
                    total = total + match
                else:
                    hots.append(match)
            tallies.append(total)
        tally_ref[f] = jnp.concatenate(tallies, axis=1)
        hot_ref[f] = jnp.concatenate(hots, axis=1)
        dl = note_ref[f, pl.ds(0, TALL), :]
        mean_ref[f] = (dl.astype(F32) / names_here[NAMES : NAMES + 1, :]).astype(BF16)
        return carry

    def four_devices(block, carry):
        nbr = gnt_ref[...]
        own = gst_ref[...]
        for i in range(4):
            f = 4 * block + i
            nbr += lax.dot_general(mean_ref[f], tally_ref[f], both_last, preferred_element_type=F32)
            own += lax.dot_general(
                note_ref[f, pl.ds(0, TALL), :], hot_ref[f], both_last, preferred_element_type=F32
            )
        gnt_ref[...] = nbr
        gst_ref[...] = own
        return carry

    for quarter in range(4):
        lax.fori_loop(4 * quarter, 4 * quarter + 4, one_device, 0)
        for s in range(4 * quarter, min(4 * quarter + 4, len(STAGED))):
            pass_on(s)
    lax.fori_loop(0, N_FEAT // 4, four_devices, 0)

    def twice(value, other, left):
        top = value.astype(BF16)
        rest = (value - top.astype(F32)).astype(BF16)
        if left:
            return jnp.dot(top, other, preferred_element_type=F32) + jnp.dot(rest, other, preferred_element_type=F32)
        return jnp.dot(other, top, preferred_element_type=F32) + jnp.dot(other, rest, preferred_element_type=F32)

    def upright(w_ref):
        return jnp.concatenate([w_ref[...].astype(F32), jnp.zeros((256 - CLASSES, HIDDEN), F32)], axis=0).T.astype(BF16)

    below = jnp.zeros((256 - TALL, ROWS), F32)
    gnt = gnt_ref[...]
    gst = gst_ref[...]
    hidden = twice(jnp.concatenate([gnt, below], axis=0), upright(wn_ref), False)
    hidden += twice(jnp.concatenate([gst, below], axis=0), upright(ws_ref), False)
    dpre_ref[z] = jnp.where(h_ref[...].astype(F32).T > 0, hidden, 0.0).astype(BF16)
    rows_ring = Ring(lambda step: dpre_ref.at[lax.rem(z + step + N_Z, N_Z)], dpre_up, dpre_down)
    rows_ring.start()
    for number, block in enumerate(nearest):
        send(*diagonal[number])
        pick(*block)
        send(*block)
    second_ref[0] = twice(gst, h_ref[...], True)
    second_ref[1] = twice(gnt, h_ref[...], True)
    second_over = push(second_ref.at[1 - core], extra_ref, over_sems, 0, partner)

    for half in range(2):
        pick((0, 0), half)
    rows_ring.take(1)
    swap_hub.wait_recv()

    def turn_hub(block, carry):
        for i in range(4):
            at = pl.multiple_of(block * 1024 + i * 256, 256)
            table_ref[pl.ds(2 * PART + at, 256), :] = turned(NODES + at)
        return carry

    lax.fori_loop(0, HUBS // 1024, turn_hub, 0)
    table_ref[pl.ds(ZERO_ROW, 8), :] = jnp.zeros((8, WIDE), F32)

    order = [((0, 0), half) for half in range(2)] + away
    for number, block in enumerate(order):
        arrive(*block)
        if number == 15:
            rows_ring.take(2)
    rows_ring.take(3)
    second_over.wait_recv()
    column_ref[...] = second_ref[core] + extra_ref[...]

    def piece(step):
        to = lax.rem(z + step + N_Z, N_Z)
        tall = pl.ds(pl.multiple_of(lax.div(to, 4) * (TALL // 2), 8), TALL // 2)
        return tall, pl.ds(pl.multiple_of(lax.rem(to, 4) * 128, 128), 128)

    scattered = {k: push(column_ref.at[piece(k)], pieces_ref.at[k], z_sems, k, (dp, z_feat(k))) for k in around}
    for block in order:
        cross(*block)
    for copy in located:
        copy.wait()

    unroll = 16

    def fold(step):
        of = lax.rem(z + step + N_Z, N_Z)
        base = (2 * of + core) * ROWS

        def some_sums(block, carry):
            at = pl.multiple_of(block * unroll, unroll)
            first = base + at
            for r in range(unroll):
                got = [table_ref[pl.ds(slot_ref[j * N_FEAT * ROWS + first + r], 1), :] for j in range(FAN1)]
                got.append(table_ref[pl.ds(self_at_ref[first + r], 1), :])
                rest = got[:FAN1]
                while len(rest) > 1:
                    rest = [rest[i] + rest[i + 1] if i + 1 < len(rest) else rest[i] for i in range(0, len(rest), 2)]
                self_ref[pl.ds(at + r, 1), :] = got[FAN1]
                sum_ref[pl.ds(at + r, 1), :] = rest[0]
            return carry

        lax.fori_loop(0, ROWS // unroll, some_sums, 0)
        here = pl.ds(pl.multiple_of(base, ROWS), ROWS)
        count = jnp.broadcast_to(cnt1_ref[:, here].astype(F32), (WIDE, ROWS)).T
        both_ref[of, :, pl.ds(0, WIDE)] = self_ref[...].astype(BF16)
        both_ref[of, :, pl.ds(WIDE, WIDE)] = (sum_ref[...] / count).astype(BF16)

    gathered = []
    for number, step in enumerate((0, -1, 1, -2, 2, -3, 3, -4)):
        fold(step)
        if number == 1:
            rows_ring.take(4)
            total = column_ref[piece(0)]
            for k in around:
                scattered[k].wait_recv()
                total = total + pieces_ref[k]
            piece_ref[0] = total
            along_x = [push(piece_ref.at[0], columns_ref.at[k], dp_sems, k, (at_shift(k, 0), feat)) for k in range(1, SIDE)]
        if number == 2:
            total = piece_ref[0]
            for i, copy in enumerate(along_x):
                copy.wait_recv()
                total = total + columns_ref[i + 1]
            piece_ref[1] = total
            along_y = [
                push(piece_ref.at[1], columns_ref.at[SIDE + i], dp_sems, SIDE + i, (at_shift(0, i), feat))
                for i in range(1, SIDE)
            ]
        if number == 3:
            total = piece_ref[1]
            for i, copy in enumerate(along_y):
                copy.wait_recv()
                total = total + columns_ref[SIDE + i + 1]
            mine_tall, mine_lanes = piece(0)
            block = final_ref.at[core, mine_tall, mine_lanes]
            final_ref[core, mine_tall, mine_lanes] = total
            for i in around:
                gathered.append(push(block, block, z2_sems, i, (dp, z_feat(i))))
        if number == 6:
            for copy in gathered:
                copy.wait_recv()
            second_back = push(final_ref.at[core], final_ref.at[core], over_sems, 1, partner)

    def two_devices(block, carry):
        total = jnp.dot(dpre_ref[2 * block], both_ref[2 * block], preferred_element_type=F32)
        total += jnp.dot(dpre_ref[2 * block + 1], both_ref[2 * block + 1], preferred_element_type=F32)
        acc_ref[...] += total
        return carry

    acc_ref[...] = jnp.zeros_like(acc_ref)
    lax.fori_loop(0, N_Z // 2, two_devices, 0)
    part_ref[...] = acc_ref[...].T
    first_over = [
        push(
            part_ref.at[pl.ds(pl.multiple_of(64 * (2 * i + 1 - core), 64), 64), :],
            theirs_ref.at[i],
            over_sems,
            2 + i,
            partner,
        )
        for i in range(2)
    ]
    second_back.wait_recv()
    self2_ref[...] = final_ref[0, :CLASSES, :]
    nbr2o_ref[...] = final_ref[1, :CLASSES, :]
    for i in range(2):
        first_over[i].wait_recv()
        mine_here = part_ref[pl.ds(pl.multiple_of(64 * (2 * i + core), 64), 64), :] + theirs_ref[i]
        part_ref[pl.ds(pl.multiple_of(64 * (2 * i + core), 64), 64), :] = mine_here

    def eight(to):
        return pl.ds(pl.multiple_of(lax.div(to, 8) * 128 + core * 64 + lax.rem(to, 8) * 8, 8), 8)

    spread = []
    for k in range(1, N_DP):
        to = at_shift(k // SIDE, k % SIDE)
        spread.append(push(part_ref.at[eight(to), :], got_ref.at[k], first_sems, k, (to, feat)))
    total = part_ref[eight(dp), :]
    for k, copy in enumerate(spread):
        copy.wait_recv()
        total = total + got_ref[k + 1]
    done_ref[dp] = jnp.concatenate([total[:, : HIDDEN // 2], total[:, HIDDEN // 2 :]], axis=0).astype(BF16)
    last = []
    for k in range(1, N_DP):
        to = at_shift(k // SIDE, k % SIDE)
        last.append(push(done_ref.at[dp], done_ref.at[dp], first2_sems, k, (to, feat)))
    for copy in last:
        copy.wait_recv()
    for k in range(N_DP):
        result = (self1_ref, nbr1_ref)[k // 8]
        eight_rows = done_ref[k].astype(F32)
        result[pl.ds(8 * (k % 8), 8), pl.ds(0, HIDDEN // 2)] = eight_rows[:8]
        result[pl.ds(8 * (k % 8), 8), pl.ds(HIDDEN // 2, HIDDEN // 2)] = eight_rows[8:]
    for copy in pending:
        copy.wait_send()


def main_step(*operands):
    vmem = pl.BlockSpec(memory_space=pltpu.VMEM)
    dma = pltpu.SemaphoreType.DMA
    return pl.pallas_call(
        main_kernel,
        out_shape=(
            jax.ShapeDtypeStruct((64, HIDDEN), F32),
            jax.ShapeDtypeStruct((64, HIDDEN), F32),
            jax.ShapeDtypeStruct((CLASSES, HIDDEN), F32),
            jax.ShapeDtypeStruct((CLASSES, HIDDEN), F32),
        ),
        in_specs=[pl.BlockSpec(memory_space=pl.ANY)] * 3 + [vmem] * (len(operands) - 3),
        out_specs=(vmem,) * 4,
        scratch_shapes=[
            pltpu.VMEM((WIDE, NODES + HUBS), BF16),
            pltpu.VMEM((NODES, WIDE), F32),
            pltpu.VMEM((2 * N_DP, QUARTER, WIDE), BF16),
            pltpu.VMEM((len(STAGED), QUARTER, WIDE), BF16),
            pltpu.VMEM((N_DP, 2, QUARTER, WIDE), BF16),
            pltpu.VMEM((N_DP, 2, QUARTER, WIDE), BF16),
            pltpu.VMEM((ZERO_ROW + 8, WIDE), F32),
            pltpu.VMEM((QUARTER, WIDE), F32),
            pltpu.SMEM((N_DP * HALF,), jnp.int32),
            pltpu.SMEM((FAN1 * N_FEAT * ROWS,), jnp.int32),
            pltpu.SMEM((N_FEAT * ROWS,), jnp.int32),
            pltpu.VMEM((ROWS, 128), BF16),
            pltpu.VMEM((N_FEAT, ROWS, ROWS), BF16),
            pltpu.VMEM((N_FEAT, ROWS, ROWS), BF16),
            pltpu.VMEM((N_FEAT, TALL, ROWS), BF16),
            pltpu.VMEM((N_FEAT, NOTE, ROWS), BF16),
            pltpu.VMEM((TALL, ROWS), F32),
            pltpu.VMEM((TALL, ROWS), F32),
            pltpu.VMEM((N_Z, HIDDEN, ROWS), BF16),
            pltpu.VMEM((2, TALL, HIDDEN), F32),
            pltpu.VMEM((TALL, HIDDEN), F32),
            pltpu.VMEM((2, TALL // 2, 128), F32),
            pltpu.VMEM((N_Z, TALL // 2, 128), F32),
            pltpu.VMEM((TALL, HIDDEN), F32),
            pltpu.VMEM((2 * SIDE, TALL // 2, 128), F32),
            pltpu.VMEM((2, TALL, HIDDEN), F32),
            pltpu.VMEM((ROWS, WIDE), F32),
            pltpu.VMEM((ROWS, WIDE), F32),
            pltpu.VMEM((N_Z, ROWS, 2 * WIDE), BF16),
            pltpu.VMEM((HIDDEN, 2 * WIDE), F32),
            pltpu.VMEM((2 * WIDE, HIDDEN), F32),
            pltpu.VMEM((2, 64, HIDDEN), F32),
            pltpu.VMEM((N_DP, 8, HIDDEN), F32),
            pltpu.VMEM((N_DP, 16, HIDDEN // 2), BF16),
            dma((N_DP + 2,)),
            dma((2, 2)),
            dma((2, len(STAGED))),
            dma((2, 2 * N_DP)),
            dma((2, 2 * N_DP)),
            dma((2, 4)),
            dma((2, 4)),
            dma((2, N_Z)),
            dma((2, 4)),
            dma((2, 4)),
            dma((2, 4)),
            dma((2, N_Z)),
            dma((2, N_DP)),
            dma((2, N_Z)),
            dma((2, N_DP)),
            dma((2, N_DP)),
        ],
        compiler_params=pltpu.CompilerParams(
            collective_id=1, has_side_effects=True, vmem_limit_bytes=60 * 1024 * 1024
        ),
        name="main_step",
    )(*operands)


def hand_kernel(*refs):
    for source, result in zip(refs[:4], refs[4:]):
        result[...] = source[...]


def hand_out(arrays):
    vmem = pl.BlockSpec(memory_space=pltpu.VMEM)
    return pl.pallas_call(
        hand_kernel,
        out_shape=tuple(jax.ShapeDtypeStruct(a.shape, a.dtype) for a in arrays),
        in_specs=[vmem] * 4,
        out_specs=(vmem,) * 4,
        compiler_params=pltpu.CompilerParams(vmem_limit_bytes=60 * 1024 * 1024),
        name="hand_out",
    )(*arrays)


def body(
    x_table,
    hub_feats,
    send_rows,
    self_slot,
    nbr1,
    cnt1,
    h_saved,
    seed_self,
    nbr2,
    cnt2,
    d_logits,
    w_self2,
    w_nbr2,
):
    read = lax.iota(jnp.int32, FAN1)[:, None] < cnt1[None]
    sums = main_step(
        send_rows.reshape(-1),
        self_slot,
        jnp.where(read, nbr1, ZERO_ROW).reshape(-1),
        x_table,
        hub_feats,
        cnt1[None],
        h_saved,
        seed_self[None],
        nbr2.T,
        cnt2[None],
        d_logits.T,
        w_self2.T,
        w_nbr2.T,
    )
    self1, nbr1_out, self2, nbr2_out = hand_out(sums)
    return (self1, nbr1_out, self2.T, nbr2_out.T)


def solution(mesh):
    placed = (
        P("feat", "dp"),
        P("feat", None),
        P("dp", None, None),
        P("dp"),
        P(None, "dp"),
        P("dp"),
        P(("dp", "feat"), None),
        P(("dp", "feat")),
        P(("dp", "feat"), None),
        P(("dp", "feat")),
        P(("dp", "feat"), None),
        P(),
        P(),
    )
    return jax.shard_map(
        body,
        mesh=mesh,
        in_specs=placed,
        out_specs=(P("feat", None), P("feat", None), P(), P()),
        check_vma=False,
    )
```

```python
import jax
import jax.numpy as jnp
from jax import lax
from jax.experimental import pallas as pl
from jax.experimental.pallas import tpu as pltpu
from jax.sharding import PartitionSpec as P

N_DP = 16
SIDE = 4
N_FEAT = 16
N_Z = 8
CAP = 2048
HALF = CAP // 2
QUARTER = HALF // 2
HUBS = 2048
NODES = 8192
ROWS = 256
GROUP = N_Z * ROWS
HIDDEN = 512
CLASSES = 172
TALL = 176
FAN1 = 10
FAN2 = 25
PICKS = 1 + FAN1
WIDE = 128
PART = N_DP * HALF
ZERO_ROW = 2 * PART + HUBS
NOTE = TALL + 32
NAMES = FAN2 + 1
MESH = pl.DeviceIdType.MESH
F32 = jnp.float32
BF16 = jnp.bfloat16
HIGHEST = lax.Precision.HIGHEST

TWO = [(2, 2), (2, 0), (0, 2), (2, 1), (2, 3), (1, 2), (3, 2)]
DIAGONAL = [(1, 1), (3, 3), (1, 3), (3, 1)]
NEXT = [(1, 0), (3, 0), (0, 1), (0, 3)]


def through(shift, half):
    one = 3 if half else 1
    dx, dy = shift
    if dx == 2:
        return (one, one if dy == 2 else 0)
    return (dx, one)


STAGED = [(shift, half) for shift in TWO for half in range(2)]


def main_kernel(
    send_rows_ref, self_slot_ref, slots_ref, x_ref, hub_ref, cnt1_ref, h_ref, seed_ref, nbr2_ref, cnt2_ref, dl_ref, ws_ref, wn_ref,
    self1_ref, nbr1_ref, self2_ref, nbr2o_ref,
    feats_ref, nodes_ref, stage_ref, mid_ref, own_ref, other_ref, table_ref, rows_ref,
    send_ref, slot_ref, self_at_ref, code_ref, tally_ref, hot_ref, mean_ref, note_ref, gnt_ref, gst_ref, dpre_ref, second_ref, extra_ref, piece_ref, pieces_ref, column_ref, columns_ref, final_ref,
    self_ref, sum_ref, both_ref, acc_ref, part_ref, theirs_ref, got_ref, done_ref,
    index_sems, swap_sems, mid_sems, far_sems, near_sems, note_up, note_down, note_over,
    dpre_up, dpre_down, over_sems, z_sems, dp_sems, z2_sems, first_sems, first2_sems,
):
    dp = lax.axis_index("dp")
    feat = lax.axis_index("feat")
    core = lax.rem(feat, 2)
    z = lax.div(feat, 2)
    px = lax.div(dp, SIDE)
    py = lax.rem(dp, SIDE)
    partner = (dp, feat + 1 - 2 * core)
    pending = []

    def at_shift(dx, dy):
        return lax.rem(px + dx + SIDE, SIDE) * SIDE + lax.rem(py + dy + SIDE, SIDE)

    def z_feat(step):
        return lax.rem(z + step + N_Z, N_Z) * 2 + core

    def push(src, dst, sems, slot, device):
        copy = pltpu.make_async_remote_copy(
            src_ref=src,
            dst_ref=dst,
            send_sem=sems.at[0, slot],
            recv_sem=sems.at[1, slot],
            device_id=device,
            device_id_type=MESH,
        )
        copy.start()
        pending.append(copy)
        return copy

    wanted = [
        pltpu.make_async_copy(
            send_rows_ref.at[pl.ds(pl.multiple_of(k * CAP + core * HALF, HALF), HALF)],
            send_ref.at[pl.ds(k * HALF, HALF)],
            index_sems.at[k],
        )
        for k in range(N_DP)
    ]
    located = [
        pltpu.make_async_copy(slots_ref, slot_ref, index_sems.at[N_DP]),
        pltpu.make_async_copy(self_slot_ref, self_at_ref, index_sems.at[N_DP + 1]),
    ]
    for copy in wanted + located:
        copy.start()

    barrier = pltpu.get_barrier_semaphore()
    peers = [partner]
    peers += [(at_shift(k // SIDE, k % SIDE), feat) for k in range(1, N_DP)]
    peers += [(dp, z_feat(k)) for k in range(1, N_Z)]
    for peer in peers:
        pl.semaphore_signal(barrier, inc=1, device_id=peer, device_id_type=MESH)
    pl.semaphore_wait(barrier, len(peers))

    lane = pl.ds(pl.multiple_of(core * 64, 64), 64)
    swap_x = push(x_ref, feats_ref.at[lane, pl.ds(0, NODES)], swap_sems, 0, partner)
    swap_hub = push(hub_ref, feats_ref.at[lane, pl.ds(NODES, HUBS)], swap_sems, 1, partner)

    def code(row):
        power = jnp.where((row & 128) != 0, 2.0, 1.0)
        for bit in range(1, 5):
            power = power * jnp.where((row & (128 << bit)) != 0, 2.0 ** (2**bit), 1.0)
        return power * (128 + (row & 127)).astype(F32)

    cnt2 = cnt2_ref[...]
    kept = lax.broadcasted_iota(jnp.int32, (FAN2, ROWS), 0) < cnt2
    names = jnp.concatenate([jnp.where(kept, code(nbr2_ref[...]), 0.0), code(seed_ref[...]), cnt2.astype(F32)], axis=0)
    note_ref[feat, pl.ds(0, TALL), :] = jnp.concatenate(
        [dl_ref[...].astype(F32), jnp.zeros((TALL - CLASSES, ROWS), F32)], axis=0
    ).astype(BF16)
    note_ref[feat, pl.ds(TALL, 32), :] = jnp.concatenate(
        [names, jnp.zeros((32 - NAMES - 1, ROWS), F32)], axis=0
    ).astype(BF16)

    around = (1, 7, 2, 6, 3, 5, 4)

    class Ring:
        def __init__(self, view, up, down, over=None):
            self.view, self.up, self.down, self.over = view, up, down, over
            self.from_below, self.from_above, self.crossed = {}, {}, []

        def send_up(self, step):
            block = self.view(1 - step)
            self.from_below[step] = push(block, block, self.up, step - 1, (dp, z_feat(1)))

        def send_down(self, step):
            block = self.view(step - 1)
            self.from_above[step] = push(block, block, self.down, step - 1, (dp, z_feat(-1)))

        def cross(self, step):
            if self.over is not None:
                block = self.view(step)
                self.crossed.append(push(block, block, self.over, len(self.crossed), partner))

        def start(self):
            self.send_up(1)
            self.send_down(1)
            self.cross(0)

        def take(self, step):
            self.from_below[step].wait_recv()
            if step < 4:
                self.send_up(step + 1)
            self.cross(-step)
            if step < 4:
                self.from_above[step].wait_recv()
                if step < 3:
                    self.send_down(step + 1)
                self.cross(step)

    notes = Ring(lambda step: note_ref.at[z_feat(step)], note_up, note_down, note_over)
    notes.start()

    feats_ref[lane, pl.ds(0, NODES)] = x_ref[...]
    feats_ref[lane, pl.ds(NODES, HUBS)] = hub_ref[...]
    swap_x.wait_recv()

    eye_rows = lax.broadcasted_iota(jnp.int32, (256, 256), 0)
    eye_columns = lax.broadcasted_iota(jnp.int32, (256, 256), 1)
    eye = jnp.where(eye_rows == eye_columns, 1.0, 0.0).astype(BF16)
    across = (((1,), (1,)), ((), ()))

    def turned(at):
        return lax.dot_general(eye, feats_ref[:, pl.ds(at, 256)], across, preferred_element_type=F32)

    def turn(block, carry):
        for i in range(4):
            at = pl.multiple_of(block * 1024 + i * 256, 256)
            nodes_ref[pl.ds(at, 256), :] = turned(at)
        return carry

    lax.fori_loop(0, NODES // 1024, turn, 0)
    for copy in wanted:
        copy.wait()

    far = {}
    staged = {}

    def pick(shift, half):
        to = at_shift(*shift)
        first = to * HALF + half * QUARTER
        unroll = 32

        def some_rows(block, carry):
            at = pl.multiple_of(block * unroll, unroll)
            got = [nodes_ref[pl.ds(send_ref[first + at + r], 1), :] for r in range(unroll)]
            for r in range(unroll):
                rows_ref[pl.ds(at + r, 1), :] = got[r]
            return carry

        lax.fori_loop(0, QUARTER // unroll, some_rows, 0)
        if shift == (0, 0):
            own_ref[dp, half] = rows_ref[...].astype(BF16)
        else:
            stage_ref[2 * (shift[0] * SIDE + shift[1]) + half] = rows_ref[...].astype(BF16)

    def send(shift, half):
        slot = 2 * (shift[0] * SIDE + shift[1]) + half
        if (shift, half) in STAGED:
            s = STAGED.index((shift, half))
            staged[s] = push(stage_ref.at[slot], mid_ref.at[s], mid_sems, s, (at_shift(*through(shift, half)), feat))
        else:
            far[slot] = push(stage_ref.at[slot], own_ref.at[dp, half], far_sems, slot, (at_shift(*shift), feat))

    def pass_on(s):
        shift, half = STAGED[s]
        mx, my = through(shift, half)
        slot = 2 * (shift[0] * SIDE + shift[1]) + half
        staged[s].wait_recv()
        source = at_shift(-mx, -my)
        to = at_shift(shift[0] - mx, shift[1] - my)
        far[slot] = push(mid_ref.at[s], own_ref.at[source, half], far_sems, slot, (to, feat))

    near = {}

    def widen(ref, source, half, at):
        table_ref[pl.ds(at, QUARTER), :] = ref[source, half].astype(F32)

    def arrive(shift, half):
        slot = 2 * (shift[0] * SIDE + shift[1]) + half
        source = at_shift(-shift[0], -shift[1])
        if slot in far:
            far[slot].wait_recv()
        near[slot] = push(own_ref.at[source, half], other_ref.at[source, half], near_sems, slot, partner)
        at = pl.multiple_of(source * CAP + core * HALF + half * QUARTER, QUARTER)
        widen(own_ref, source, half, at)

    def cross(shift, half):
        slot = 2 * (shift[0] * SIDE + shift[1]) + half
        source = at_shift(-shift[0], -shift[1])
        near[slot].wait_recv()
        at = pl.multiple_of(source * CAP + (1 - core) * HALF + half * QUARTER, QUARTER)
        widen(other_ref, source, half, at)

    diagonal = [(shift, half) for shift in DIAGONAL for half in range(2)]
    nearest = [(shift, half) for half in range(2) for shift in NEXT]
    away = STAGED + diagonal + nearest
    notes.take(1)
    for number, block in enumerate(STAGED + diagonal):
        pick(*block)
        if number < len(STAGED):
            send(*block)
        if number in (5, 11, 17):
            notes.take(number // 6 + 2)
    for copy in notes.crossed:
        copy.wait_recv()

    code_ref[...] = code(feat * ROWS + lax.broadcasted_iota(jnp.int32, (ROWS, 128), 0)).astype(BF16)
    one = jnp.ones((ROWS, 128), BF16)
    none = jnp.zeros((ROWS, 128), BF16)
    both_last = (((1,), (1,)), ((), ()))
    for ref in (gnt_ref, gst_ref):
        ref[...] = jnp.zeros_like(ref)

    def one_device(f, carry):
        names_here = note_ref[f, pl.ds(TALL, 32), :].astype(F32)
        tallies, hots = [], []
        for side in range(ROWS // 128):
            total = none
            for j in range(NAMES):
                line = names_here[j : j + 1, side * 128 : side * 128 + 128].astype(BF16)
                match = jnp.where(jnp.broadcast_to(line, (ROWS, 128)) == code_ref[...], one, none)
                if j < FAN2:
                    total = total + match
                else:
                    hots.append(match)
            tallies.append(total)
        tally_ref[f] = jnp.concatenate(tallies, axis=1)
        hot_ref[f] = jnp.concatenate(hots, axis=1)
        dl = note_ref[f, pl.ds(0, TALL), :]
        mean_ref[f] = (dl.astype(F32) / names_here[NAMES : NAMES + 1, :]).astype(BF16)
        return carry

    def four_devices(block, carry):
        nbr = gnt_ref[...]
        own = gst_ref[...]
        for i in range(4):
            f = 4 * block + i
            nbr += lax.dot_general(mean_ref[f], tally_ref[f], both_last, preferred_element_type=F32)
            own += lax.dot_general(
                note_ref[f, pl.ds(0, TALL), :], hot_ref[f], both_last, preferred_element_type=F32
            )
        gnt_ref[...] = nbr
        gst_ref[...] = own
        return carry

    for quarter in range(4):
        lax.fori_loop(4 * quarter, 4 * quarter + 4, one_device, 0)
        for s in range(4 * quarter, min(4 * quarter + 4, len(STAGED))):
            pass_on(s)
    lax.fori_loop(0, N_FEAT // 4, four_devices, 0)

    def twice(value, other, left):
        top = value.astype(BF16)
        rest = (value - top.astype(F32)).astype(BF16)
        if left:
            return jnp.dot(top, other, preferred_element_type=F32) + jnp.dot(rest, other, preferred_element_type=F32)
        return jnp.dot(other, top, preferred_element_type=F32) + jnp.dot(other, rest, preferred_element_type=F32)

    def upright(w_ref):
        return jnp.concatenate([w_ref[...].astype(F32), jnp.zeros((256 - CLASSES, HIDDEN), F32)], axis=0).T.astype(BF16)

    below = jnp.zeros((256 - TALL, ROWS), F32)
    gnt = gnt_ref[...]
    gst = gst_ref[...]
    hidden = twice(jnp.concatenate([gnt, below], axis=0), upright(wn_ref), False)
    hidden += twice(jnp.concatenate([gst, below], axis=0), upright(ws_ref), False)
    dpre_ref[z] = jnp.where(h_ref[...].astype(F32).T > 0, hidden, 0.0).astype(BF16)
    rows_ring = Ring(lambda step: dpre_ref.at[lax.rem(z + step + N_Z, N_Z)], dpre_up, dpre_down)
    rows_ring.start()
    for number, block in enumerate(nearest):
        send(*diagonal[number])
        pick(*block)
        send(*block)
    second_ref[0] = twice(gst, h_ref[...], True)
    second_ref[1] = twice(gnt, h_ref[...], True)
    second_over = push(second_ref.at[1 - core], extra_ref, over_sems, 0, partner)

    for half in range(2):
        pick((0, 0), half)
    rows_ring.take(1)
    swap_hub.wait_recv()

    def turn_hub(block, carry):
        for i in range(4):
            at = pl.multiple_of(block * 1024 + i * 256, 256)
            table_ref[pl.ds(2 * PART + at, 256), :] = turned(NODES + at)
        return carry

    lax.fori_loop(0, HUBS // 1024, turn_hub, 0)
    table_ref[pl.ds(ZERO_ROW, 8), :] = jnp.zeros((8, WIDE), F32)

    order = [((0, 0), half) for half in range(2)] + away
    for number, block in enumerate(order):
        arrive(*block)
        if number == 15:
            rows_ring.take(2)
    rows_ring.take(3)
    second_over.wait_recv()
    column_ref[...] = second_ref[core] + extra_ref[...]

    def piece(step):
        to = lax.rem(z + step + N_Z, N_Z)
        tall = pl.ds(pl.multiple_of(lax.div(to, 4) * (TALL // 2), 8), TALL // 2)
        return tall, pl.ds(pl.multiple_of(lax.rem(to, 4) * 128, 128), 128)

    scattered = {k: push(column_ref.at[piece(k)], pieces_ref.at[k], z_sems, k, (dp, z_feat(k))) for k in around}
    for block in order:
        cross(*block)
    for copy in located:
        copy.wait()

    unroll = 16

    def fold(step):
        of = lax.rem(z + step + N_Z, N_Z)
        base = (2 * of + core) * ROWS

        def some_sums(block, carry):
            at = pl.multiple_of(block * unroll, unroll)
            first = base + at
            for r in range(unroll):
                got = [table_ref[pl.ds(slot_ref[j * N_FEAT * ROWS + first + r], 1), :] for j in range(FAN1)]
                got.append(table_ref[pl.ds(self_at_ref[first + r], 1), :])
                rest = got[:FAN1]
                while len(rest) > 1:
                    rest = [rest[i] + rest[i + 1] if i + 1 < len(rest) else rest[i] for i in range(0, len(rest), 2)]
                self_ref[pl.ds(at + r, 1), :] = got[FAN1]
                sum_ref[pl.ds(at + r, 1), :] = rest[0]
            return carry

        lax.fori_loop(0, ROWS // unroll, some_sums, 0)
        here = pl.ds(pl.multiple_of(base, ROWS), ROWS)
        count = jnp.broadcast_to(cnt1_ref[:, here].astype(F32), (WIDE, ROWS)).T
        both_ref[of, :, pl.ds(0, WIDE)] = self_ref[...].astype(BF16)
        both_ref[of, :, pl.ds(WIDE, WIDE)] = (sum_ref[...] / count).astype(BF16)

    gathered = []
    for number, step in enumerate((0, -1, 1, -2, 2, -3, 3, -4)):
        fold(step)
        if number == 1:
            rows_ring.take(4)
            total = column_ref[piece(0)]
            for k in around:
                scattered[k].wait_recv()
                total = total + pieces_ref[k]
            piece_ref[0] = total
            along_x = [push(piece_ref.at[0], columns_ref.at[k], dp_sems, k, (at_shift(k, 0), feat)) for k in range(1, SIDE)]
        if number == 2:
            total = piece_ref[0]
            for i, copy in enumerate(along_x):
                copy.wait_recv()
                total = total + columns_ref[i + 1]
            piece_ref[1] = total
            along_y = [
                push(piece_ref.at[1], columns_ref.at[SIDE + i], dp_sems, SIDE + i, (at_shift(0, i), feat))
                for i in range(1, SIDE)
            ]
        if number == 3:
            total = piece_ref[1]
            for i, copy in enumerate(along_y):
                copy.wait_recv()
                total = total + columns_ref[SIDE + i + 1]
            mine_tall, mine_lanes = piece(0)
            block = final_ref.at[core, mine_tall, mine_lanes]
            final_ref[core, mine_tall, mine_lanes] = total
            for i in around:
                gathered.append(push(block, block, z2_sems, i, (dp, z_feat(i))))
        if number == 6:
            for copy in gathered:
                copy.wait_recv()
            second_back = push(final_ref.at[core], final_ref.at[core], over_sems, 1, partner)

    def two_devices(block, carry):
        total = jnp.dot(dpre_ref[2 * block], both_ref[2 * block], preferred_element_type=F32)
        total += jnp.dot(dpre_ref[2 * block + 1], both_ref[2 * block + 1], preferred_element_type=F32)
        acc_ref[...] += total
        return carry

    acc_ref[...] = jnp.zeros_like(acc_ref)
    lax.fori_loop(0, N_Z // 2, two_devices, 0)
    part_ref[...] = acc_ref[...].T
    first_over = [
        push(
            part_ref.at[pl.ds(pl.multiple_of(64 * (2 * i + 1 - core), 64), 64), :],
            theirs_ref.at[i],
            over_sems,
            2 + i,
            partner,
        )
        for i in range(2)
    ]
    second_back.wait_recv()
    self2_ref[...] = final_ref[0, :CLASSES, :]
    nbr2o_ref[...] = final_ref[1, :CLASSES, :]
    for i in range(2):
        first_over[i].wait_recv()
        mine_here = part_ref[pl.ds(pl.multiple_of(64 * (2 * i + core), 64), 64), :] + theirs_ref[i]
        part_ref[pl.ds(pl.multiple_of(64 * (2 * i + core), 64), 64), :] = mine_here

    def eight(to):
        return pl.ds(pl.multiple_of(lax.div(to, 8) * 128 + core * 64 + lax.rem(to, 8) * 8, 8), 8)

    spread = []
    for k in range(1, N_DP):
        to = at_shift(k // SIDE, k % SIDE)
        spread.append(push(part_ref.at[eight(to), :], got_ref.at[k], first_sems, k, (to, feat)))
    total = part_ref[eight(dp), :]
    for k, copy in enumerate(spread):
        copy.wait_recv()
        total = total + got_ref[k + 1]
    done_ref[dp] = jnp.concatenate([total[:, : HIDDEN // 2], total[:, HIDDEN // 2 :]], axis=0).astype(BF16)
    last = []
    for k in range(1, N_DP):
        to = at_shift(k // SIDE, k % SIDE)
        last.append(push(done_ref.at[dp], done_ref.at[dp], first2_sems, k, (to, feat)))
    for copy in last:
        copy.wait_recv()
    for k in range(N_DP):
        result = (self1_ref, nbr1_ref)[k // 8]
        eight_rows = done_ref[k].astype(F32)
        result[pl.ds(8 * (k % 8), 8), pl.ds(0, HIDDEN // 2)] = eight_rows[:8]
        result[pl.ds(8 * (k % 8), 8), pl.ds(HIDDEN // 2, HIDDEN // 2)] = eight_rows[8:]
    for copy in pending:
        copy.wait_send()


def main_step(*operands):
    vmem = pl.BlockSpec(memory_space=pltpu.VMEM)
    dma = pltpu.SemaphoreType.DMA
    return pl.pallas_call(
        main_kernel,
        out_shape=(
            jax.ShapeDtypeStruct((64, HIDDEN), F32),
            jax.ShapeDtypeStruct((64, HIDDEN), F32),
            jax.ShapeDtypeStruct((CLASSES, HIDDEN), F32),
            jax.ShapeDtypeStruct((CLASSES, HIDDEN), F32),
        ),
        in_specs=[pl.BlockSpec(memory_space=pl.ANY)] * 3 + [vmem] * (len(operands) - 3),
        out_specs=(vmem,) * 4,
        scratch_shapes=[
            pltpu.VMEM((WIDE, NODES + HUBS), BF16),
            pltpu.VMEM((NODES, WIDE), F32),
            pltpu.VMEM((2 * N_DP, QUARTER, WIDE), BF16),
            pltpu.VMEM((len(STAGED), QUARTER, WIDE), BF16),
            pltpu.VMEM((N_DP, 2, QUARTER, WIDE), BF16),
            pltpu.VMEM((N_DP, 2, QUARTER, WIDE), BF16),
            pltpu.VMEM((ZERO_ROW + 8, WIDE), F32),
            pltpu.VMEM((QUARTER, WIDE), F32),
            pltpu.SMEM((N_DP * HALF,), jnp.int32),
            pltpu.SMEM((FAN1 * N_FEAT * ROWS,), jnp.int32),
            pltpu.SMEM((N_FEAT * ROWS,), jnp.int32),
            pltpu.VMEM((ROWS, 128), BF16),
            pltpu.VMEM((N_FEAT, ROWS, ROWS), BF16),
            pltpu.VMEM((N_FEAT, ROWS, ROWS), BF16),
            pltpu.VMEM((N_FEAT, TALL, ROWS), BF16),
            pltpu.VMEM((N_FEAT, NOTE, ROWS), BF16),
            pltpu.VMEM((TALL, ROWS), F32),
            pltpu.VMEM((TALL, ROWS), F32),
            pltpu.VMEM((N_Z, HIDDEN, ROWS), BF16),
            pltpu.VMEM((2, TALL, HIDDEN), F32),
            pltpu.VMEM((TALL, HIDDEN), F32),
            pltpu.VMEM((2, TALL // 2, 128), F32),
            pltpu.VMEM((N_Z, TALL // 2, 128), F32),
            pltpu.VMEM((TALL, HIDDEN), F32),
            pltpu.VMEM((2 * SIDE, TALL // 2, 128), F32),
            pltpu.VMEM((2, TALL, HIDDEN), F32),
            pltpu.VMEM((ROWS, WIDE), F32),
            pltpu.VMEM((ROWS, WIDE), F32),
            pltpu.VMEM((N_Z, ROWS, 2 * WIDE), BF16),
            pltpu.VMEM((HIDDEN, 2 * WIDE), F32),
            pltpu.VMEM((2 * WIDE, HIDDEN), F32),
            pltpu.VMEM((2, 64, HIDDEN), F32),
            pltpu.VMEM((N_DP, 8, HIDDEN), F32),
            pltpu.VMEM((N_DP, 16, HIDDEN // 2), BF16),
            dma((N_DP + 2,)),
            dma((2, 2)),
            dma((2, len(STAGED))),
            dma((2, 2 * N_DP)),
            dma((2, 2 * N_DP)),
            dma((2, 4)),
            dma((2, 4)),
            dma((2, N_Z)),
            dma((2, 4)),
            dma((2, 4)),
            dma((2, 4)),
            dma((2, N_Z)),
            dma((2, N_DP)),
            dma((2, N_Z)),
            dma((2, N_DP)),
            dma((2, N_DP)),
        ],
        compiler_params=pltpu.CompilerParams(
            collective_id=1, has_side_effects=True, vmem_limit_bytes=60 * 1024 * 1024
        ),
        name="main_step",
    )(*operands)


def hand_kernel(*refs):
    for source, result in zip(refs[:4], refs[4:]):
        result[...] = source[...]


def hand_out(arrays):
    vmem = pl.BlockSpec(memory_space=pltpu.VMEM)
    return pl.pallas_call(
        hand_kernel,
        out_shape=tuple(jax.ShapeDtypeStruct(a.shape, a.dtype) for a in arrays),
        in_specs=[vmem] * 4,
        out_specs=(vmem,) * 4,
        compiler_params=pltpu.CompilerParams(vmem_limit_bytes=60 * 1024 * 1024),
        name="hand_out",
    )(*arrays)


def body(
    x_table,
    hub_feats,
    send_rows,
    self_slot,
    nbr1,
    cnt1,
    h_saved,
    seed_self,
    nbr2,
    cnt2,
    d_logits,
    w_self2,
    w_nbr2,
):
    read = lax.iota(jnp.int32, FAN1)[:, None] < cnt1[None]
    sums = main_step(
        send_rows.reshape(-1),
        self_slot,
        jnp.where(read, nbr1, ZERO_ROW).reshape(-1),
        x_table,
        hub_feats,
        cnt1[None],
        h_saved,
        seed_self[None],
        nbr2.T,
        cnt2[None],
        d_logits.T,
        w_self2.T,
        w_nbr2.T,
    )
    self1, nbr1_out, self2, nbr2_out = hand_out(sums)
    return (self1, nbr1_out, self2.T, nbr2_out.T)


def solution(mesh):
    placed = (
        P("feat", "dp"),
        P("feat", None),
        P("dp", None, None),
        P("dp"),
        P(None, "dp"),
        P("dp"),
        P(("dp", "feat"), None),
        P(("dp", "feat")),
        P(("dp", "feat"), None),
        P(("dp", "feat")),
        P(("dp", "feat"), None),
        P(),
        P(),
    )
    return jax.shard_map(
        body,
        mesh=mesh,
        in_specs=placed,
        out_specs=(P("feat", None), P("feat", None), P(), P()),
        check_vma=False,
    )
```
